32 devices in a mesh: dp: 8 (over z, y), tensor: 4 (over x, core).
Axes of the slice: x: 2, y: 2, z: 4, core: 2. Of those that a mesh axis runs over, the one named last changes fastest.
Arguments:
- tokens: bfloat16 [16, 1024, 768], P('dp', 'tensor'), may hold values from -6 to 6
- segment_ids: int32 [16, 1024], P('dp'), may hold values from 0 to 15, as said below
- cotangent: bfloat16 [16, 1024, 768], P('dp', 'tensor'), may hold values from -8 to 8
- qkv_master: float32 [3, 768, 768], P(None, 'dp', 'tensor'), may hold values from -0.14433757 to 0.14433757
- out_master: float32 [768, 768], P('tensor', 'dp'), may hold values from -0.875 to 0.875
- up_master: float32 [768, 3072], P('dp', 'tensor'), may hold values from -0.28867513 to 0.28867513
- down_master: float32 [3072, 768], P('tensor', 'dp'), may hold values from -0.109375 to 0.109375
- norm_gains: float32 [2, 768], replicated, may hold values from 0.3 to 2.5
- position_bias: float32 [32, 12], replicated, may hold values from -6 to 6
- qkv_first: float32 [3, 768, 768], P(None, 'dp', 'tensor'), may hold values from -0.00024414062 to 0.00024414062
- qkv_second: float32 [3, 768, 768], P(None, 'dp', 'tensor'), may hold values from 1.4138801e-10 to 5.6555205e-10
- out_first: float32 [768, 768], P('tensor', 'dp'), may hold values from -0.00024414062 to 0.00024414062
- out_second: float32 [768, 768], P('tensor', 'dp'), may hold values from 2.8277604e-12 to 1.13110415e-11
- up_first: float32 [768, 3072], P('dp', 'tensor'), may hold values from -0.00024414062 to 0.00024414062
- up_second: float32 [768, 3072], P('dp', 'tensor'), may hold values from 2.8277604e-12 to 1.13110415e-11
- down_first: float32 [3072, 768], P('tensor', 'dp'), may hold values from -0.00024414062 to 0.00024414062
- down_second: float32 [3072, 768], P('tensor', 'dp'), may hold values from 1.4138801e-10 to 5.6555205e-10
- gain_first: float32 [2, 768], replicated, may hold values from -0.0007324219 to 0.0007324219
- gain_second: float32 [2, 768], replicated, may hold values from 4.2416404e-11 to 1.6966561e-10
- bias_first: float32 [32, 12], replicated, may hold values from -0.0007324219 to 0.0007324219
- bias_second: float32 [32, 12], replicated, may hold values from 3.1812303e-11 to 1.2724921e-10
Outputs:
- pooled: float32 [16, 16, 768], P('dp', None, 'tensor')
- tokens_grad: float32 [16, 1024, 768], P('dp', 'tensor')
- grad_qkv: float32 [3, 768, 768], P(None, 'dp', 'tensor')
- grad_out: float32 [768, 768], P('tensor', 'dp')
- grad_up: float32 [768, 3072], P('dp', 'tensor')
- grad_down: float32 [3072, 768], P('tensor', 'dp')
- grad_gains: float32 [2, 768], replicated
- grad_bias: float32 [32, 12], replicated
- gradient_norm: float32 [], replicated
- new_qkv: float32 [3, 768, 768], P(None, 'dp', 'tensor')
- new_out: float32 [768, 768], P('tensor', 'dp')
- new_up: float32 [768, 3072], P('dp', 'tensor')
- new_down: float32 [3072, 768], P('tensor', 'dp')
- new_gains: float32 [2, 768], replicated
- new_bias: float32 [32, 12], replicated
- second_qkv: float32 [3, 768, 768], P(None, 'dp', 'tensor')
- second_out: float32 [768, 768], P('tensor', 'dp')
- second_up: float32 [768, 3072], P('dp', 'tensor')
- second_down: float32 [3072, 768], P('tensor', 'dp')
- second_gains: float32 [2, 768], replicated
- second_bias: float32 [32, 12], replicated
The draws below stay inside these ranges and needn't reach their ends.
Inputs may be any that keep to these rules, and one draw needn't show every extreme that they name: `segment_ids`: within a row the ids start at 0 and never fall; in each aligned group of 2 rows one row is a single item and every other row holds exactly 16 items.
All inputs are finite; a program needn't handle non-finite values.
Results may differ from the reference program's by a relative error of at most 0.013.
The reference program's roundings to bfloat16 on the way count: a program that leaves them out, or rounds other values in their place, can miss the bound.
Values may be sent and summed in bfloat16 or wider, within the bound.
No kernel may reach another device: no remote copies, remote signals or barrier semaphores. Data moves between devices by JAX's collectives and lax.ppermute only.
A program may use at most 128 MiB of HBM per device.

```python
import math
import jax
import jax.numpy as jnp
from jax import lax

D = 768
H = 12
DH = 64
FF = 3072
NB = 32
SEQ = 1024
SEQS = 2
SEGS = 16
STEP = 10
ROWS = 16
NPARAM = 7079808


def draw_segment_ids(key, part):
    key = jax.random.fold_in(key, 11)
    order_key, pick_key = jax.random.split(key)
    row_keys = jax.random.split(order_key, ROWS)

    def row_order(row_key):
        return jax.random.permutation(row_key, SEQ - 1)
    position_rank = jax.vmap(row_order)(row_keys)
    starts = (position_rank < SEGS - 1).astype(jnp.int32)
    segment_index = jnp.concatenate([jnp.zeros((ROWS, 1), jnp.int32), jnp.cumsum(starts, axis=1).astype(jnp.int32)], axis=1)
    chosen = jax.random.randint(pick_key, (ROWS // SEQS,), 0, SEQS)
    row_in_group = jnp.arange(ROWS, dtype=jnp.int32) % SEQS
    single = row_in_group == jnp.repeat(chosen, SEQS, total_repeat_length=ROWS)
    return jnp.where(single[:, None], 0, segment_index).astype(jnp.int32)


def draw_cotangent(key, part):
    key = jax.random.fold_in(key, 7)
    column = jnp.arange(D, dtype=jnp.float32) / D
    entries = jnp.clip(jax.random.normal(key, (ROWS, SEQ, D), jnp.float32), -4.0, 4.0)
    column_scale = 0.6 + 1.2 * column
    return (entries * column_scale).astype(jnp.bfloat16)


def draw_qkv_master(key, part):
    key = jax.random.fold_in(key, 3)
    full_shape = (3, D, H * DH)
    entries = jnp.clip(jax.random.normal(key, full_shape, jnp.float32), -4.0, 4.0)
    slice_scale = jnp.array([(D * DH) ** (-0.5), D ** (-0.5), D ** (-0.5)], jnp.float32)
    return entries * slice_scale[:, None, None]


def draw_up_master(key, part):
    key = jax.random.fold_in(key, 5)
    column = jnp.arange(FF, dtype=jnp.float32) / FF
    entries = jnp.clip(jax.random.normal(key, (D, FF), jnp.float32), -4.0, 4.0)
    column_scale = 0.6 + 1.2 * column
    return entries * column_scale * D ** (-0.5)


def draw_norm_gains(key, part):
    key = jax.random.fold_in(key, 9)
    column = jnp.arange(D, dtype=jnp.float32) / D
    factor = jax.random.uniform(key, (2, D), jnp.float32, 0.85, 1.15)
    column_scale = 0.6 + 1.2 * column
    return factor * column_scale


def level_of(key, dims, pieces, least, high):
    level = 1.0
    for position, parts in pieces:
        heights = jax.random.uniform(jax.random.fold_in(jax.random.fold_in(key, 6), position), (parts,), jnp.float32, least / len(pieces), high / len(pieces))
        level = level * jnp.repeat(jnp.exp(heights), dims[position] // parts).reshape((-1,) + (1,) * (len(dims) - 1 - position))
    return level


def gaussian(stream_key, dims, spread, reach, cuts=(), kind=jnp.bfloat16):
    drawn = spread * jax.random.normal(stream_key, dims, jnp.float32)
    if cuts:
        drawn = drawn * level_of(stream_key, dims, cuts, -0.22, 0.18)
    return jnp.clip(drawn, -reach, reach).astype(kind)


def setup_inputs(seed: int = 0) -> dict:
    keys = jax.random.split(jax.random.key(seed), 22)
    return {
        "tokens": gaussian(keys[0], (ROWS, SEQ, D), 1.0, 6.0, ((0, 8), (1, 4))),
        "segment_ids": draw_segment_ids(jax.random.fold_in(keys[21], 71), 0),
        "cotangent": draw_cotangent(jax.random.fold_in(keys[21], 71), 0),
        "qkv_master": draw_qkv_master(jax.random.fold_in(keys[21], 71), 0),
        "out_master": gaussian(keys[4], (H * DH, D), (H * DH // 16) ** -0.5, 0.875, ((0, 4), (1, 8)), jnp.float32),
        "up_master": draw_up_master(jax.random.fold_in(keys[21], 71), 0),
        "down_master": gaussian(keys[6], (FF, D), FF ** -0.5, 0.109375, ((0, 4), (1, 8)), jnp.float32),
        "norm_gains": draw_norm_gains(jax.random.fold_in(keys[21], 71), 0),
        "position_bias": gaussian(keys[8], (NB, H), 1.0, 6.0, (), jnp.float32),
        "qkv_first": gaussian(keys[9], (3, D, H * DH), (NPARAM ** -0.5 / 9), 0.00024414062, ((1, 8), (2, 4)), jnp.float32),
        "qkv_second": jnp.clip(jnp.exp(math.log(5.655520496361532e-10) - 1.3862944 * jax.random.uniform(keys[10], (3, D, H * DH), jnp.float32) ** level_of(keys[10], (3, D, H * DH), ((1, 8), (2, 4)), -0.2, 0.2)), 1.413880124090383e-10, 5.655520496361532e-10),
        "out_first": gaussian(keys[11], (H * DH, D), (NPARAM ** -0.5 / 9), 0.00024414062, ((0, 4), (1, 8)), jnp.float32),
        "out_second": jnp.clip(jnp.exp(math.log(1.1311041513140108e-11) - 1.3862944 * jax.random.uniform(keys[12], (H * DH, D), jnp.float32) ** level_of(keys[12], (H * DH, D), ((0, 4), (1, 8)), -0.2, 0.2)), 2.827760378285027e-12, 1.1311041513140108e-11),
        "up_first": gaussian(keys[13], (D, FF), (NPARAM ** -0.5 / 9), 0.00024414062, ((0, 8), (1, 4)), jnp.float32),
        "up_second": jnp.clip(jnp.exp(math.log(1.1311041513140108e-11) - 1.3862944 * jax.random.uniform(keys[14], (D, FF), jnp.float32) ** level_of(keys[14], (D, FF), ((0, 8), (1, 4)), -0.2, 0.2)), 2.827760378285027e-12, 1.1311041513140108e-11),
        "down_first": gaussian(keys[15], (FF, D), (NPARAM ** -0.5 / 9), 0.00024414062, ((0, 4), (1, 8)), jnp.float32),
        "down_second": jnp.clip(jnp.exp(math.log(5.655520496361532e-10) - 1.3862944 * jax.random.uniform(keys[16], (FF, D), jnp.float32) ** level_of(keys[16], (FF, D), ((0, 4), (1, 8)), -0.2, 0.2)), 1.413880124090383e-10, 5.655520496361532e-10),
        "gain_first": gaussian(keys[17], (2, D), (NPARAM ** -0.5 / 3), 0.0007324219, (), jnp.float32),
        "gain_second": jnp.clip(jnp.exp(jax.random.uniform(keys[18], (2, D), jnp.float32, math.log(4.241640372271149e-11), math.log(1.6966561489084597e-10))), 4.241640372271149e-11, 1.6966561489084597e-10),
        "bias_first": gaussian(keys[19], (NB, H), (NPARAM ** -0.5 / 3), 0.0007324219, (), jnp.float32),
        "bias_second": jnp.clip(jnp.exp(jax.random.uniform(keys[20], (NB, H), jnp.float32, math.log(3.181230279203362e-11), math.log(1.2724921116813448e-10))), 3.181230279203362e-11, 1.2724921116813448e-10),
    }


norm_eps = 1e-06
mask_fill = -1000000000.0
clip_level = 1.0
beta_first = 0.9
beta_second = 0.999
adam_eps = 1e-08
decay_rate = 0.1
highest = lax.Precision.HIGHEST

@jax.custom_vjp
def low(v):
    return lax.optimization_barrier(v.astype(jnp.bfloat16)).astype(jnp.float32)

@jax.custom_vjp
def low_back(v):
    return v

def low_keep(v):
    return (low(v), None)

def low_pass(kept, grad):
    return (grad,)

def back_keep(v):
    return (v, None)

def back_low(kept, grad):
    return (low(grad),)
low.defvjp(low_keep, low_pass)
low_back.defvjp(back_keep, back_low)

def bucket_of(offset):
    distance = jnp.abs(offset)
    large = 8 + sum(((distance >= threshold).astype(jnp.int32) for threshold in (12, 16, 23, 32, 46, 64, 91)))
    inner_bucket = jnp.where(distance < 8, distance, large)
    return (inner_bucket + jnp.where(offset > 0, 16, 0)).astype(jnp.int32)

def rms_scale(values):
    return lax.rsqrt(lax.optimization_barrier(jnp.mean(values * values, axis=-1, keepdims=True)) + norm_eps)

def gelu_tanh(values):
    return jax.nn.gelu(values, approximate=True)

def learning_rates():
    qkv_rate = jnp.array([2.0 * (D * DH) ** (-0.5), 2.0 * D ** (-0.5), 2.0 * D ** (-0.5)], jnp.float32)[:, None, None]
    return (qkv_rate, 0.5 * (H * DH / 16) ** (-0.5), 0.5 * D ** (-0.5), 2.0 * FF ** (-0.5), 0.25, 0.5)

def adam_update(parameter, gradient, first_moment, second_moment, step_rate, clip_factor):
    clipped = gradient * clip_factor
    first_new = beta_first * first_moment + (1.0 - beta_first) * clipped
    second_new = beta_second * second_moment + (1.0 - beta_second) * clipped * clipped
    first_hat = first_new / (1.0 - beta_first ** STEP)
    second_hat = second_new / (1.0 - beta_second ** STEP)
    updated = parameter - step_rate * (first_hat / (jnp.sqrt(second_hat) + adam_eps) + decay_rate * parameter)
    return (updated, second_new)

def forward_row(row_tokens, row_seg, weight_set):
    qkv_weight, out_weight, up_weight, down_weight, gain_rows, bias_table = weight_set
    seq_len = row_tokens.shape[0]
    first_normed = low(row_tokens * rms_scale(row_tokens) * gain_rows[0])
    projected = jnp.einsum('sd,ide->ise', first_normed, qkv_weight, precision=highest)
    projected = low(low_back(projected)).reshape(3, seq_len, H, DH)
    positions = jnp.arange(seq_len, dtype=jnp.int32)
    buckets = bucket_of(positions[None, :] - positions[:, None])
    bias_vals = jnp.transpose(bias_table[buckets], (2, 0, 1))
    scores = jnp.einsum('qhd,khd->hqk', projected[0], projected[1], precision=highest) + bias_vals
    scores = low_back(scores)
    same_item = (row_seg[:, None] == row_seg[None, :])[None]
    masked = jnp.where(same_item, scores, mask_fill)
    row_top = lax.optimization_barrier(jnp.max(masked, axis=-1, keepdims=True))
    exp_scores = jnp.exp(masked - row_top)
    attn_probs = exp_scores / lax.optimization_barrier(jnp.sum(exp_scores, axis=-1, keepdims=True))
    mixed_heads = jnp.einsum('hqk,khd->qhd', low(attn_probs), projected[2], precision=highest)
    mixed_heads = low(low_back(mixed_heads.reshape(seq_len, H * DH)))
    middle = row_tokens + low_back(jnp.dot(mixed_heads, out_weight, precision=highest))
    second_normed = low(middle * rms_scale(middle) * gain_rows[1])
    pre_act = low_back(jnp.dot(second_normed, up_weight, precision=highest))
    activated = low(gelu_tanh(pre_act))
    return middle + low_back(jnp.dot(activated, down_weight, precision=highest))

def reference(tokens, segment_ids, cotangent, qkv_master, out_master, up_master, down_master, norm_gains, position_bias, qkv_first, qkv_second, out_first, out_second, up_first, up_second, down_first, down_second, gain_first, gain_second, bias_first, bias_second):
    masters = (qkv_master, out_master, up_master, down_master, norm_gains, position_bias)
    slot_ids = jnp.arange(SEGS, dtype=jnp.int32)

    def row_step(carried, row_inputs):
        row_tokens, row_seg, row_cot = row_inputs

        def row_block(param_set, row_input):
            qkv_weight, out_weight, up_weight, down_weight, gain_rows, bias_table = param_set
            return forward_row(row_input, row_seg, (low(qkv_weight), low(out_weight), low(up_weight), low(down_weight), gain_rows, bias_table))
        output_row, pullback = jax.vjp(row_block, masters, row_tokens.astype(jnp.float32))
        param_grads, token_grad = pullback(row_cot.astype(jnp.float32))
        carried = jax.tree.map(jnp.add, carried, param_grads)
        slot_hot = (row_seg[:, None] == slot_ids[None, :]).astype(jnp.float32)
        slot_sums = jnp.dot(slot_hot.T, output_row, precision=highest)
        counts = lax.optimization_barrier(jnp.sum(slot_hot, axis=0))
        pooled_row = slot_sums / jnp.maximum(counts, 1.0)[:, None]
        return (carried, (pooled_row, token_grad))
    zeros_init = jax.tree.map(jnp.zeros_like, masters)
    totals, (pooled, tokens_grad) = lax.scan(row_step, zeros_init, (tokens, segment_ids, cotangent))
    gradient_norm = jnp.sqrt(sum((jnp.sum(gradient_piece * gradient_piece) for gradient_piece in totals)))
    clip_factor = jnp.minimum(1.0, clip_level / gradient_norm)
    firsts = (qkv_first, out_first, up_first, down_first, gain_first, bias_first)
    seconds = (qkv_second, out_second, up_second, down_second, gain_second, bias_second)
    rates = learning_rates()
    results = [adam_update(masters[index], totals[index], firsts[index], seconds[index], rates[index], clip_factor) for index in range(6)]
    return (pooled, tokens_grad, totals[0], totals[1], totals[2], totals[3], totals[4], totals[5], gradient_norm, results[0][0], results[1][0], results[2][0], results[3][0], results[4][0], results[5][0], results[0][1], results[1][1], results[2][1], results[3][1], results[4][1], results[5][1])
```

```python
import jax
import jax.numpy as jnp
from jax import lax
from jax.experimental import pallas as pl
from jax.experimental.pallas import tpu as pltpu
from jax.sharding import PartitionSpec as P

D = 768
H = 12
DH = 64
FF = 3072
SEGS = 16
STEP = 10

norm_eps = 1e-06
mask_fill = -1000000000.0
clip_level = 1.0
beta_first = 0.9
beta_second = 0.999
adam_eps = 1e-08
decay_rate = 0.1
gelu_scale = 0.7978845608028654
gelu_cubic = 0.044715

bf16 = jnp.bfloat16
f32 = jnp.float32
i32 = jnp.int32

QB = 256
KC = 128
EDGE = 128
NEAR = QB + 2 * EDGE
VMEM_LIMIT = 56 << 20

SMEM_SPEC = pl.BlockSpec(memory_space=pltpu.SMEM)
VMEM_SPEC = pl.BlockSpec(memory_space=pltpu.VMEM)


def sds(shape, dtype):
    return jax.ShapeDtypeStruct(shape, dtype)


def nt(a, b):
    return lax.dot_general(a, b, (((1,), (1,)), ((), ())), preferred_element_type=f32)


def nn(a, b):
    return lax.dot_general(a, b, (((1,), (0,)), ((), ())), preferred_element_type=f32)


def call(body, name, smem, vmem, outs, scratch=(), flops=0, moved=0, exps=0):
    return pl.pallas_call(
        body,
        out_shape=tuple(outs),
        in_specs=[SMEM_SPEC] * len(smem) + [VMEM_SPEC] * len(vmem),
        out_specs=(VMEM_SPEC,) * len(outs),
        scratch_shapes=list(scratch),
        compiler_params=pltpu.CompilerParams(vmem_limit_bytes=VMEM_LIMIT),
        cost_estimate=pl.CostEstimate(flops=flops, bytes_accessed=moved, transcendentals=exps),
        name=name,
    )(*smem, *vmem)


def bucket_of(offset):
    distance = jnp.abs(offset)
    large = 8 + sum(
        ((distance >= threshold).astype(jnp.int32) for threshold in (12, 16, 23, 32, 46, 64, 91))
    )
    inner_bucket = jnp.where(distance < 8, distance, large)
    return inner_bucket + jnp.where(offset > 0, 16, 0)


def learning_rates():
    qkv_rate = jnp.array(
        [2.0 * (D * DH) ** (-0.5), 2.0 * D ** (-0.5), 2.0 * D ** (-0.5)], jnp.float32
    )[:, None, None]
    return (
        qkv_rate,
        0.5 * (H * DH / 16) ** (-0.5),
        0.5 * D ** (-0.5),
        2.0 * FF ** (-0.5),
        0.25,
        0.5,
    )


def adam_update(parameter, gradient, first_moment, second_moment, step_rate, clip_factor):
    clipped = gradient * clip_factor
    first_new = beta_first * first_moment + (1.0 - beta_first) * clipped
    second_new = beta_second * second_moment + (1.0 - beta_second) * clipped * clipped
    first_hat = first_new / (1.0 - beta_first**STEP)
    second_hat = second_new / (1.0 - beta_second**STEP)
    updated = parameter - step_rate * (
        first_hat / (jnp.sqrt(second_hat) + adam_eps) + decay_rate * parameter
    )
    return (updated, second_new)


def swap_core(value):
    return lax.ppermute(value, "tensor", [(i, i ^ 1) for i in range(lax.axis_size("tensor"))])


def swap_x(value):
    return lax.ppermute(value, "tensor", [(i, i ^ 2) for i in range(lax.axis_size("tensor"))])


def swap_dp(value, bits):
    return lax.ppermute(value, "dp", [(i, i ^ bits) for i in range(lax.axis_size("dp"))])


def high_groups(size):
    bits = []
    bit = 2
    while bit < size:
        bits.append(bit)
        bit *= 2
    groups = []
    while bits:
        take = bits[-2:]
        bits = bits[:-2]
        if len(take) == 2:
            groups.append((take[0], take[1], take[0] | take[1]))
        else:
            groups.append((take[0],))
    return groups


def gather_high(piece):
    stack = piece[None]
    offsets = [0]
    for group in high_groups(lax.axis_size("dp")):
        stack = jnp.concatenate([stack] + [swap_dp(stack, bits) for bits in group], axis=0)
        offsets = offsets + [known ^ bits for bits in group for known in offsets]
    return stack, offsets


def scatter_high(blocks, dp_rank):
    for group in high_groups(lax.axis_size("dp")):
        low = group[0]
        ways = len(group) + 1
        here = (dp_rank // low) % ways
        lead = blocks.shape[0] // ways
        split = blocks.reshape((ways, lead) + blocks.shape[1:])
        total = lax.dynamic_index_in_dim(split, here, 0, keepdims=False).astype(f32)
        got = []
        for way, bits in enumerate(group):
            send = lax.dynamic_index_in_dim(split, here ^ (way + 1), 0, keepdims=False)
            got.append(swap_dp(send.astype(bf16), bits))
        for piece in got:
            total = total + piece.astype(f32)
        blocks = total
    return blocks.reshape(blocks.shape[1:])


def near_kernel(table_ref, near_ref):
    heads = near_ref.shape[0]

    def rows(step, carried):
        start = pl.multiple_of(step * 16, 16)
        row = lax.broadcasted_iota(i32, (16, QB), 0) + start
        col = lax.broadcasted_iota(i32, (16, QB), 1)
        offset = row - EDGE - col
        buckets = bucket_of(offset)
        values = [jnp.where(offset > 0, table_ref[31, h], table_ref[15, h]) for h in range(heads)]
        for bucket in list(range(15)) + list(range(17, 31)):
            here = buckets == bucket
            values = [jnp.where(here, table_ref[bucket, h], values[h]) for h in range(heads)]
        for h in range(heads):
            near_ref[h, pl.ds(start, 16), :] = values[h]
        return carried

    lax.fori_loop(0, NEAR // 16, rows, 0)


def rms_of(values):
    return lax.rsqrt(jnp.mean(values * values, axis=-1, keepdims=True) + norm_eps)


def norm_kernel(place_ref, keep_ref, got_ref, other_ref, gain_ref, h_ref, hT_ref):
    length = keep_ref.shape[0]
    for index, block in enumerate((keep_ref, got_ref, other_ref.at[0], other_ref.at[1])):
        start = pl.multiple_of(place_ref[index] * length, length)
        values = block[...].astype(f32)
        normed = (values * rms_of(values) * gain_ref[0:1, :]).astype(bf16)
        h_ref[pl.ds(start, length), :] = normed
        hT_ref[:, pl.ds(start, length)] = normed.T


def place_weights(tab_ref, pieces, target):
    index = 0
    for piece in pieces:
        rows = piece.shape[1]
        for slot in range(piece.shape[0]):
            start = pl.multiple_of(tab_ref[index] * rows, 16)
            target[pl.ds(start, rows), :] = piece[slot]
            index += 1


def sub_sum(values):
    return jnp.sum(values.reshape(values.shape[0] // 8, 8, values.shape[1]), axis=0)


def sub_max(values):
    return jnp.max(values.reshape(values.shape[0] // 8, 8, values.shape[1]), axis=0)


def near_row(block, chunk):
    start = chunk * KC - block * QB + EDGE
    return start if 0 <= start and start + KC <= NEAR else None


def same_segment(segk_ref, keys, seg_query):
    seg_key = segk_ref[keys, :]
    return jnp.concatenate([seg_key] * (QB // seg_key.shape[1]), axis=1) == seg_query


def attend_kernel(
    flag_ref, far_ref, tab_ref, h_ref, piece_a_ref, piece_b_ref, near_ref, segk_ref, segq_ref,
    wT_ref, qkvT_ref, oT_ref, lse_ref, w_buf, s_buf, p_buf,
):
    seq = h_ref.shape[0]
    heads = near_ref.shape[0]
    width = oT_ref.shape[0]
    size = width // heads
    place_weights(tab_ref, (piece_a_ref, piece_b_ref), w_buf)
    wT_ref[...] = w_buf[...].T
    qkvT_ref[...] = nt(wT_ref[0 : 3 * width, :], h_ref[...]).astype(bf16)

    def head(h, masked):
        start = pl.multiple_of(h * size, size)
        keys = qkvT_ref[pl.ds(width + start, size), :].T
        valuesT = qkvT_ref[pl.ds(2 * width + start, size), :]
        far_left = far_ref[0, h]
        far_right = far_ref[1, h]
        for block in range(seq // QB):
            qs = slice(block * QB, (block + 1) * QB)
            queriesT = qkvT_ref[pl.ds(start, size), qs]
            top = jnp.full((8, QB), -3e38, f32)
            for chunk in range(seq // KC):
                ks = slice(chunk * KC, (chunk + 1) * KC)
                scores = nn(keys[ks, :], queriesT)
                row = near_row(block, chunk)
                if row is None:
                    scores = scores + (far_left if chunk * KC < block * QB else far_right)
                else:
                    scores = scores + near_ref[h, row : row + KC, :]
                if masked:
                    scores = jnp.where(
                        same_segment(segk_ref, ks, segq_ref[:, qs]), scores, mask_fill
                    )
                s_buf[ks, qs] = scores
                top = jnp.maximum(top, sub_max(scores))
            top = jnp.max(top, axis=0, keepdims=True)
            total = jnp.zeros((8, QB), f32)
            for chunk in range(seq // KC):
                ks = slice(chunk * KC, (chunk + 1) * KC)
                exps = jnp.exp(s_buf[ks, qs] - top)
                s_buf[ks, qs] = exps
                total = total + sub_sum(exps)
            total = jnp.sum(total, axis=0, keepdims=True)
            scale = 1.0 / total
            for chunk in range(seq // KC):
                ks = slice(chunk * KC, (chunk + 1) * KC)
                p_buf[ks, qs] = (s_buf[ks, qs] * scale).astype(bf16)
            oT_ref[pl.ds(start, size), qs] = nn(valuesT, p_buf[:, qs]).astype(bf16)
            lse_ref[pl.ds(h, 1), qs] = top + jnp.log(total)

    single = flag_ref[0]

    @pl.when(single == 1)
    def _():
        lax.fori_loop(0, heads, lambda h, carried: (head(h, False), carried)[1], 0)

    @pl.when(single != 1)
    def _():
        lax.fori_loop(0, heads, lambda h, carried: (head(h, True), carried)[1], 0)


def attend(flag, far, tab, h, pieces, near, segk, segq):
    seq = h.shape[0]
    cols = pieces[0].shape[2]
    width = cols // 4
    return call(
        attend_kernel,
        "attend",
        (flag, far, tab),
        (h, *pieces, near, segk, segq),
        (sds((cols, D), bf16), sds((3 * width, seq), bf16), sds((width, seq), bf16), sds((8, seq), f32)),
        (pltpu.VMEM((D, cols), bf16), pltpu.VMEM((seq, seq), f32), pltpu.VMEM((seq, seq), bf16)),
        flops=14_000_000_000,
        moved=8_000_000,
        exps=3 * seq * seq,
    )


def attend_back_kernel(
    flag_ref, far_ref, qkvT_ref, doT_ref, lse_ref, near_ref, segk_ref, segq_ref, hT_ref,
    dqkvT_ref, grad_ref, dnear_ref, dfar_ref, p_buf, dp_buf, pb_buf, ds_buf,
):
    width, seq = doT_ref.shape
    heads = near_ref.shape[0]
    size = width // heads
    blocks = seq // QB

    def head(h, masked):
        start = pl.multiple_of(h * size, size)
        keysT = qkvT_ref[pl.ds(width + start, size), :]
        key_value = jnp.concatenate([keysT, qkvT_ref[pl.ds(2 * width + start, size), :]], axis=0).T
        zeros = jnp.zeros((size, QB), bf16)
        far_left = far_ref[0, h]
        far_right = far_ref[1, h]
        for block in range(blocks):
            qs = slice(block * QB, (block + 1) * QB)
            queriesT = jnp.concatenate([qkvT_ref[pl.ds(start, size), qs], zeros], axis=0)
            d_outT = jnp.concatenate([zeros, doT_ref[pl.ds(start, size), qs]], axis=0)
            lse = lse_ref[pl.ds(h, 1), qs]
            lse_left = lse - far_left
            lse_right = lse - far_right
            dots = jnp.zeros((8, QB), f32)
            for chunk in range(seq // KC):
                ks = slice(chunk * KC, (chunk + 1) * KC)
                scores = nn(key_value[ks, :], queriesT)
                row = near_row(block, chunk)
                if row is None:
                    scores = scores - (lse_left if chunk * KC < block * QB else lse_right)
                else:
                    scores = scores + near_ref[h, row : row + KC, :] - lse
                probs = jnp.exp(scores)
                if masked:
                    probs = jnp.where(same_segment(segk_ref, ks, segq_ref[:, qs]), probs, 0.0)
                d_probs = nn(key_value[ks, :], d_outT)
                p_buf[ks, :] = probs
                dp_buf[ks, :] = d_probs
                pb_buf[ks, qs] = probs.astype(bf16)
                dots = dots + sub_sum(probs * d_probs)
            dots = jnp.sum(dots, axis=0, keepdims=True)
            for chunk in range(seq // KC):
                ks = slice(chunk * KC, (chunk + 1) * KC)
                d_scores = (p_buf[ks, :] * (dp_buf[ks, :] - dots)).astype(bf16)
                ds_buf[ks, qs] = d_scores
                row = near_row(block, chunk)
                if row is not None:
                    if block == 0 or (block == 1 and row == 0):
                        dnear_ref[h, row : row + KC, :] = d_scores.astype(f32)
                    else:
                        dnear_ref[h, row : row + KC, :] += d_scores.astype(f32)
        dqkvT_ref[pl.ds(start, size), :] = nn(keysT, ds_buf[...]).astype(bf16)
        row = lax.broadcasted_iota(i32, (size, seq), 0)
        col = lax.broadcasted_iota(i32, (size, seq), 1)
        in_block = (row == col // QB).astype(bf16)
        queries = jnp.concatenate([qkvT_ref[pl.ds(start, size), :], in_block], axis=0).T
        d_keys = nn(ds_buf[...], queries)
        key_row = lax.broadcasted_iota(i32, d_keys.shape, 0)
        of_block = lax.broadcasted_iota(i32, d_keys.shape, 1) - size
        counted = (of_block >= 0) & (of_block < blocks)
        left = jnp.sum(jnp.where(counted & (key_row < of_block * QB - EDGE), d_keys, 0.0))
        right = jnp.sum(jnp.where(counted & (key_row >= of_block * QB + QB + EDGE), d_keys, 0.0))
        lane = lax.broadcasted_iota(i32, (1, 128), 1)
        dfar_ref[pl.ds(h, 1), :] = jnp.where(lane == 0, left, jnp.where(lane == 1, right, 0.0))
        dqkvT_ref[pl.ds(width + start, size), :] = d_keys.astype(bf16).T[0:size, :]
        d_out = jnp.concatenate(
            [doT_ref[pl.ds(start, size), :], jnp.zeros((size, seq), bf16)], axis=0
        ).T
        d_values = nn(pb_buf[...], d_out)
        dqkvT_ref[pl.ds(2 * width + start, size), :] = d_values.astype(bf16).T[0:size, :]

    single = flag_ref[0]

    @pl.when(single == 1)
    def _():
        lax.fori_loop(0, heads, lambda h, carried: (head(h, False), carried)[1], 0)

    @pl.when(single != 1)
    def _():
        lax.fori_loop(0, heads, lambda h, carried: (head(h, True), carried)[1], 0)

    grad_ref[...] = nt(hT_ref[...], dqkvT_ref[...]).astype(bf16)


def attend_back(flag, far, qkvT, doT, lse, near, segk, segq, hT):
    width, seq = doT.shape
    return call(
        attend_back_kernel,
        "attend_back",
        (flag, far),
        (qkvT, doT, lse, near, segk, segq, hT),
        (sds(qkvT.shape, bf16), sds((D, 3 * width), bf16), sds(near.shape, f32), sds((8, 128), f32)),
        (
            pltpu.VMEM((seq, QB), f32),
            pltpu.VMEM((seq, QB), f32),
            pltpu.VMEM((seq, seq), bf16),
            pltpu.VMEM((seq, seq), bf16),
        ),
        flops=20_000_000_000,
        moved=8_000_000,
        exps=3 * seq * seq,
    )


def project_kernel(place_ref, oT0_ref, oT1_ref, wT0_ref, wT1_ref, keep_ref, send_ref, o_buf):
    width = oT0_ref.shape[0]
    length = keep_ref.shape[0] // 2
    o_buf[...] = jnp.concatenate([oT0_ref[...], oT1_ref[...]], axis=0).T
    w = jnp.concatenate([wT0_ref[3 * width :, :], wT1_ref[3 * width :, :]], axis=0)
    for index in range(4):
        start = pl.multiple_of(place_ref[index] * length, length)
        part = nn(o_buf[pl.ds(start, length), :], w)
        rows = slice((index % 2) * length, (index % 2 + 1) * length)
        if index < 2:
            keep_ref[rows, :] = part
        else:
            send_ref[rows, :] = part.astype(send_ref.dtype)


def middle_kernel(keep_tok_ref, got_tok_ref, part_ref, got_ref, gain_ref, x2_ref, h_ref):
    length = keep_tok_ref.shape[0]
    for index, block in enumerate((keep_tok_ref, got_tok_ref)):
        rows = slice(index * length, (index + 1) * length)
        values = block[...].astype(f32) + part_ref[rows, :] + got_ref[rows, :].astype(f32)
        x2_ref[rows, :] = values
        h_ref[rows, :] = (values * rms_of(values) * gain_ref[1:2, :]).astype(bf16)


def split3(values):
    high = values.astype(bf16)
    rest = values - high.astype(f32)
    mid = rest.astype(bf16)
    low = (rest - mid.astype(f32)).astype(bf16)
    return high, mid, low


def feed_kernel(
    tab_ref, h_own_ref, h_oth_ref, cot_keep_ref, cot_got_ref, cot_oth_ref,
    ua0_ref, ub0_ref, ua1_ref, ub1_ref, da0_ref, db0_ref, da1_ref, db1_ref, hot_ref, x2_ref,
    act_ref, dpre_ref, keep_ref, send_ref, pooled_ref, cot_ref, u0_buf, u1_buf, d0_buf, d1_buf,
):
    place_weights(tab_ref, (ua0_ref, ub0_ref), u0_buf)
    place_weights(tab_ref, (da0_ref, db0_ref), d0_buf)
    place_weights(tab_ref, (ua1_ref, ub1_ref), u1_buf)
    place_weights(tab_ref, (da1_ref, db1_ref), d1_buf)
    length = cot_keep_ref.shape[0]
    units = u0_buf.shape[1]
    cots = (cot_keep_ref, cot_got_ref, cot_oth_ref.at[0], cot_oth_ref.at[1])
    for index in range(4):
        rows = slice(index * length, (index + 1) * length)
        half = slice((index % 2) * length, (index % 2 + 1) * length)
        h = (h_own_ref if index < 2 else h_oth_ref)[half, :]
        cot = cots[index][...]
        cot_ref[rows, :] = cot
        total = None
        for side, (u_buf, d_buf) in enumerate(((u0_buf, d0_buf), (u1_buf, d1_buf))):
            cols = slice(side * units, (side + 1) * units)
            pre = nn(h, u_buf[...])
            d_act = nn(cot, d_buf[...])
            square = pre * pre
            bent = jnp.tanh(gelu_scale * pre * (1.0 + gelu_cubic * square))
            half_up = 0.5 * (1.0 + bent)
            act_ref[rows, cols] = (pre * half_up).astype(bf16)
            slope = half_up + (0.5 * gelu_scale) * pre * (1.0 - bent * bent) * (
                1.0 + (3.0 * gelu_cubic) * square
            )
            d_pre = (d_act * slope).astype(bf16)
            dpre_ref[rows, cols] = d_pre
            part = nt(d_pre, u_buf[...])
            total = part if total is None else total + part
        if index < 2:
            keep_ref[half, :] = total
        else:
            send_ref[half, :] = total.astype(send_ref.dtype)
    hot = hot_ref[...]
    pooled = None
    for side, d_buf in enumerate((d0_buf, d1_buf)):
        cols = slice(side * units, (side + 1) * units)
        sums = nn(hot, act_ref[:, cols])
        for term in split3(sums):
            part = nt(term, d_buf[...])
            pooled = part if pooled is None else pooled + part
    for term in split3(x2_ref[...]):
        pooled = pooled + nn(hot[:, 0 : 2 * length], term)
    pooled_ref[...] = pooled


def weight_grad_kernel(h_own_ref, h_oth_ref, cot_ref, act_ref, dpre_ref, gu0_ref, gu1_ref, gd0_ref, gd1_ref):
    units = gu0_ref.shape[1]
    hT = jnp.concatenate([h_own_ref[...], h_oth_ref[...]], axis=0).T
    gu0_ref[...] = nn(hT, dpre_ref[:, 0:units]).astype(bf16)
    gu1_ref[...] = nn(hT, dpre_ref[:, units:]).astype(bf16)
    cotT = cot_ref[...].T
    gd0_ref[...] = nn(cotT, act_ref[:, 0:units]).astype(bf16)
    gd1_ref[...] = nn(cotT, act_ref[:, units:]).astype(bf16)


def norm_back(values, gain, upstream):
    scale = rms_of(values)
    normed = values * scale
    gain_grad = jnp.sum(upstream * normed, axis=0, keepdims=True)
    scaled = upstream * gain
    inner = jnp.mean(scaled * normed, axis=-1, keepdims=True)
    return scale * (scaled - normed * inner), gain_grad


def middle_back_kernel(x2_ref, part_ref, got_ref, cot_ref, gain_ref, dx2_ref, da_ref, gain_grad_ref):
    length = x2_ref.shape[0] // 2
    for index in range(2):
        rows = slice(index * length, (index + 1) * length)
        d_values, gain_grad = norm_back(
            x2_ref[rows, :], gain_ref[1:2, :], part_ref[rows, :] + got_ref[rows, :].astype(f32)
        )
        dx2 = cot_ref[rows, :].astype(f32) + d_values
        dx2_ref[rows, :] = dx2
        da_ref[rows, :] = dx2.astype(bf16)
        if index == 0:
            gain_grad_ref[...] = gain_grad
        else:
            gain_grad_ref[...] += gain_grad


def branch_back_kernel(
    place_ref, da_own_ref, da_oth_ref, wT0_ref, wT1_ref, oT0_ref, oT1_ref,
    doT0_ref, doT1_ref, g0_ref, g1_ref, da_buf,
):
    width = oT0_ref.shape[0]
    length = da_own_ref.shape[0] // 2
    for index in range(4):
        start = pl.multiple_of(place_ref[index] * length, length)
        half = slice((index % 2) * length, (index % 2 + 1) * length)
        da_buf[pl.ds(start, length), :] = (da_own_ref if index < 2 else da_oth_ref)[half, :]
    da = da_buf[...]
    doT0_ref[...] = nt(wT0_ref[3 * width :, :], da).astype(bf16)
    doT1_ref[...] = nt(wT1_ref[3 * width :, :], da).astype(bf16)
    g0_ref[...] = nn(oT0_ref[...], da).T.astype(bf16)
    g1_ref[...] = nn(oT1_ref[...], da).T.astype(bf16)


def first_back_kernel(place_ref, d0_ref, d1_ref, wT0_ref, wT1_ref, keep_ref, send_ref, d_buf):
    rows3 = d0_ref.shape[0]
    length = keep_ref.shape[0] // 2
    d_buf[...] = jnp.concatenate([d0_ref[...], d1_ref[...]], axis=0).T
    w = jnp.concatenate([wT0_ref[0:rows3, :], wT1_ref[0:rows3, :]], axis=0)
    for index in range(4):
        start = pl.multiple_of(place_ref[index] * length, length)
        part = nn(d_buf[pl.ds(start, length), :], w)
        rows = slice((index % 2) * length, (index % 2 + 1) * length)
        if index < 2:
            keep_ref[rows, :] = part
        else:
            send_ref[rows, :] = part.astype(send_ref.dtype)


def token_grad_kernel(keep_tok_ref, got_tok_ref, part_ref, got_ref, dx2_ref, gain_ref, own_ref, away_ref, gain_grad_ref):
    length = keep_tok_ref.shape[0]
    for index, block in enumerate((keep_tok_ref, got_tok_ref)):
        rows = slice(index * length, (index + 1) * length)
        d_values, gain_grad = norm_back(
            block[...].astype(f32), gain_ref[0:1, :], part_ref[rows, :] + got_ref[rows, :].astype(f32)
        )
        if index == 0:
            own_ref[...] = dx2_ref[rows, :] + d_values
            gain_grad_ref[...] = gain_grad
        else:
            away_ref[...] = dx2_ref[rows, :] + d_values
            gain_grad_ref[...] += gain_grad


def bias_grad_kernel(dnear0_ref, dnear1_ref, dfar0_ref, dfar1_ref, grad_ref):
    heads = dnear0_ref.shape[0]
    row = lax.broadcasted_iota(i32, (NEAR, QB), 0)
    col = lax.broadcasted_iota(i32, (NEAR, QB), 1)
    offset = row - EDGE - col
    buckets = bucket_of(offset)
    lane = lax.broadcasted_iota(i32, (1, 128), 1)
    for side, (dnear_ref, dfar_ref) in enumerate(((dnear0_ref, dfar0_ref), (dnear1_ref, dfar1_ref))):
        for h in range(heads):
            values = dnear_ref[h]
            line = jnp.zeros((1, 128), f32)
            for bucket in range(32):
                if bucket == 16:
                    continue
                total = jnp.sum(jnp.where(buckets == bucket, values, 0.0))
                line = jnp.where(lane == bucket, total, line)
            far = dfar_ref[h : h + 1, :]
            left = jnp.sum(jnp.where(lane == 0, far, 0.0))
            right = jnp.sum(jnp.where(lane == 1, far, 0.0))
            line = line + jnp.where(lane == 15, left, jnp.where(lane == 31, right, 0.0))
            grad_ref[side * heads + h : side * heads + h + 1, :] = line


def per_device(
    tokens,
    segment_ids,
    cotangent,
    qkv_master,
    out_master,
    up_master,
    down_master,
    norm_gains,
    position_bias,
    qkv_first,
    qkv_second,
    out_first,
    out_second,
    up_first,
    up_second,
    down_first,
    down_second,
    gain_first,
    gain_second,
    bias_first,
    bias_second,
):
    rank = lax.axis_index("tensor")
    dp_rank = lax.axis_index("dp")
    dp_size = lax.axis_size("dp")
    side = rank // 2
    core = rank % 2
    row_bit = dp_rank % 2
    rows, length = tokens.shape[0], tokens.shape[1]
    seq = segment_ids.shape[1]
    shard_rows, width = qkv_master.shape[1], qkv_master.shape[2]
    heads = position_bias.shape[1] // lax.axis_size("tensor")
    assert rows == 2 and lax.axis_size("tensor") == 4 and seq == 4 * length
    pick = lambda value, index: lax.dynamic_index_in_dim(value, index, 0, keepdims=False)

    places = jnp.stack([rank, rank ^ 2, rank ^ 1, rank ^ 3]).astype(i32)

    pack_a = jnp.concatenate(
        [qkv_master[0], qkv_master[1], qkv_master[2], out_master.T], axis=1
    ).astype(bf16)
    pack_ud = jnp.stack([up_master, down_master.T]).astype(bf16)

    tok_keep = pick(tokens, side)
    tok_got = swap_x(pick(tokens, 1 - side))
    high_a, offsets = gather_high(pack_a)
    a_own = (high_a, swap_dp(high_a, 1))
    a_x = swap_x(high_a)
    a_other = (a_x, swap_dp(a_x, 1))
    tok_other = swap_core(jnp.stack([tok_keep, tok_got]))
    high_ud, _ = gather_high(pack_ud)
    high_u = high_ud[:, 0]
    high_d = high_ud[:, 1]
    u_own = (high_u, swap_dp(high_u, 1))
    u_x = swap_x(high_u)
    u_other = (u_x, swap_dp(u_x, 1))
    d_x = swap_x(high_d)
    d_y = swap_dp(high_d, 1)
    d_own = (high_d, d_y)
    d_other = (d_x, swap_x(d_y))
    cot_keep = pick(cotangent, side)
    cot_got = swap_x(pick(cotangent, 1 - side))
    cot_other = swap_core(jnp.stack([cot_keep, cot_got]))

    all_offsets = offsets + [known ^ 1 for known in offsets]
    if shard_rows % 16 == 0:
        tab = jnp.stack([dp_rank ^ known for known in all_offsets]).astype(i32)
        order = lambda pair: pair
    else:
        slot_of = [0] * dp_size
        for slot, known in enumerate(all_offsets):
            slot_of[known] = slot
        slots = jnp.asarray(slot_of, i32)[dp_rank ^ jnp.arange(dp_size)]
        tab = jnp.arange(2, dtype=i32)

        def order(pair):
            both = jnp.take(jnp.concatenate(pair, axis=0), slots, axis=0)
            both = both.reshape(2, 1, D // 2, both.shape[2])
            return both[0], both[1]

    seg_row = pick(segment_ids, side)
    flag = (seg_row[0] == seg_row[seq - 1]).astype(i32).reshape(1)
    segk = jnp.broadcast_to(seg_row[:, None], (seq, 128))
    segq = seg_row[None, :]
    tables = [
        lax.dynamic_slice_in_dim(position_bias, shard * heads, heads, 1)
        for shard in (rank, rank ^ 2)
    ]
    (near,) = call(
        near_kernel,
        "bias_tiles",
        (jnp.concatenate(tables, axis=1),),
        (),
        (sds((2 * heads, NEAR, QB), f32),),
        moved=4_000_000,
    )
    nears = (near[:heads], near[heads:])
    fars = [jnp.stack([table[15], table[31]]) for table in tables]

    h1, h1T = call(
        norm_kernel,
        "first_norm",
        (places,),
        (tok_keep, tok_got, tok_other, norm_gains),
        (sds((seq, D), bf16), sds((D, seq), bf16)),
        moved=6_000_000,
    )
    wT0, qkvT0, oT0, lse0 = attend(flag, fars[0], tab, h1, order(a_own), nears[0], segk, segq)
    wT1, qkvT1, oT1, lse1 = attend(flag, fars[1], tab, h1, order(a_other), nears[1], segk, segq)

    half = (seq // 2, D)
    keep, send = call(
        project_kernel,
        "project",
        (places,),
        (oT0, oT1, wT0, wT1),
        (sds(half, f32), sds(half, f32)),
        (pltpu.VMEM((seq, 2 * width), bf16),),
        flops=2 * seq * 2 * width * D,
        moved=8_000_000,
    )
    x2, h2 = call(
        middle_kernel,
        "second_norm",
        (),
        (tok_keep, tok_got, keep, swap_core(send), norm_gains),
        (sds(half, f32), sds(half, bf16)),
        moved=7_000_000,
    )
    h2_other = swap_core(h2)
    slot_ids = jnp.arange(SEGS, dtype=i32)
    seg_blocks = seg_row.reshape(4, length)
    seg_rel = jnp.concatenate([pick(seg_blocks, rank ^ bits) for bits in (0, 2, 1, 3)])
    hot = (seg_rel[None, :] == slot_ids[:, None]).astype(bf16)
    units = up_master.shape[1]
    act, d_pre, keep, send, pool_part, cot_rel = call(
        feed_kernel,
        "feed",
        (tab,),
        (
            h2, h2_other, cot_keep, cot_got, cot_other,
            *order(u_own), *order(u_other), *order(d_own), *order(d_other), hot, x2,
        ),
        (
            sds((seq, 2 * units), bf16),
            sds((seq, 2 * units), bf16),
            sds(half, f32),
            sds(half, f32),
            sds((SEGS, D), f32),
            sds((seq, D), bf16),
        ),
        [pltpu.VMEM((D, units), bf16)] * 4,
        flops=2 * 3 * seq * D * 2 * units,
        moved=20_000_000,
        exps=seq * 2 * units,
    )
    got = swap_core(send)
    gu0, gu1, gd0, gd1 = call(
        weight_grad_kernel,
        "feed_grads",
        (),
        (h2, h2_other, cot_rel, act, d_pre),
        (sds((D, units), bf16),) * 4,
        flops=2 * 2 * seq * D * 2 * units,
        moved=14_000_000,
    )
    dx2, da, gain_grad_second = call(
        middle_back_kernel,
        "second_norm_back",
        (),
        (x2, keep, got, cot_rel[: seq // 2], norm_gains),
        (sds(half, f32), sds(half, bf16), sds((1, D), f32)),
        moved=8_000_000,
    )
    da_other = swap_core(da)

    by_block = lambda grad: grad.reshape((dp_size // 2, 2, shard_rows) + grad.shape[1:])
    pick_y = lambda grad, bit: lax.dynamic_index_in_dim(by_block(grad), bit, 1, keepdims=False)

    def over_y(grad):
        got_rows = swap_dp(pick_y(grad, 1 - row_bit), 1)
        return pick_y(grad, row_bit).astype(f32) + got_rows.astype(f32)

    def over_x(own, other):
        return (own.astype(f32) + swap_x(other.astype(bf16)).astype(f32)).astype(bf16)

    grad_up = scatter_high(over_y(over_x(gu0, gu1)), dp_rank)
    down_y0, down_y1 = over_y(gd0), over_y(gd1)
    grad_down = scatter_high(over_x(down_y0, down_y1), dp_rank).T

    doT0, doT1, go0, go1 = call(
        branch_back_kernel,
        "branch_back",
        (places,),
        (da, da_other, wT0, wT1, oT0, oT1),
        (sds((width, seq), bf16),) * 2 + (sds((D, width), bf16),) * 2,
        (pltpu.VMEM((seq, D), bf16),),
        flops=2 * 2 * seq * D * 2 * width,
        moved=6_000_000,
    )
    dqkvT1, gq1, dnear1, dfar1 = attend_back(
        flag, fars[1], qkvT1, doT1, lse1, nears[1], segk, segq, h1T
    )
    dqkvT0, gq0, dnear0, dfar0 = attend_back(
        flag, fars[0], qkvT0, doT0, lse0, nears[0], segk, segq, h1T
    )
    keep, send = call(
        first_back_kernel,
        "first_back",
        (places,),
        (dqkvT0, dqkvT1, wT0, wT1),
        (sds(half, f32), sds(half, f32)),
        (pltpu.VMEM((seq, 6 * width), bf16),),
        flops=2 * seq * 6 * width * D,
        moved=8_000_000,
    )
    grad_a = scatter_high(
        over_y(over_x(jnp.concatenate([gq0, go0], axis=1), jnp.concatenate([gq1, go1], axis=1))),
        dp_rank,
    )
    tg_own, tg_away, gain_grad_first = call(
        token_grad_kernel,
        "first_norm_back",
        (),
        (tok_keep, tok_got, keep, swap_core(send), dx2, norm_gains),
        (sds((length, D), f32), sds((length, D), f32), sds((1, D), f32)),
        moved=8_000_000,
    )
    tg_got = swap_x(tg_away)
    first_row = side == 0
    tokens_grad = jnp.stack(
        [jnp.where(first_row, tg_own, tg_got), jnp.where(first_row, tg_got, tg_own)]
    )
    (table_grad,) = call(
        bias_grad_kernel,
        "bias_grad",
        (),
        (dnear0, dnear1, dfar0, dfar1),
        (sds((8, 128), f32),),
        moved=4_000_000,
    )
    table_grad = table_grad[: 2 * heads, :32].T
    bias_part = jnp.zeros(position_bias.shape, f32)
    for index, shard in enumerate((rank, rank ^ 2)):
        bias_part = lax.dynamic_update_slice(
            bias_part, table_grad[:, index * heads : (index + 1) * heads], (0, shard * heads)
        )

    pool_sums = pool_part + swap_core(pool_part)
    counts = jnp.sum((seg_row[None, :] == slot_ids[:, None]).astype(f32), axis=1)
    means = pool_sums / jnp.maximum(counts, 1.0)[:, None]
    mean_keep = lax.dynamic_slice_in_dim(means, rank * width, width, 1)
    mean_got = swap_x(lax.dynamic_slice_in_dim(means, (rank ^ 2) * width, width, 1))
    pooled = jnp.stack(
        [jnp.where(first_row, mean_keep, mean_got), jnp.where(first_row, mean_got, mean_keep)]
    )

    grad_qkv = jnp.stack([grad_a[:, i * width : (i + 1) * width] for i in range(3)])
    grad_out = grad_a[:, 3 * width :].T
    shard_squares = sum(
        (jnp.sum(piece * piece) for piece in (grad_a, grad_up, grad_down))
    )
    n_gain, n_bias = norm_gains.size, position_bias.size
    small = jnp.concatenate(
        [
            gain_grad_first[0],
            gain_grad_second[0],
            bias_part.reshape(-1),
            shard_squares[None],
        ]
    )
    lanes = -(-small.shape[0] // 1024) * 1024
    small = jnp.pad(small, (0, lanes - small.shape[0])).reshape(lanes // 128, 128)
    devices = dp_size * lax.axis_size("tensor")
    spread = jnp.broadcast_to(small[None], (devices,) + small.shape)
    summed = jnp.sum(
        lax.all_to_all(spread, ("dp", "tensor"), 0, 0, tiled=True), axis=0
    ).reshape(-1)
    grad_gains = summed[:n_gain].reshape(norm_gains.shape)
    grad_bias = summed[n_gain : n_gain + n_bias].reshape(position_bias.shape)
    total_squares = summed[n_gain + n_bias]
    gradient_norm = jnp.sqrt(
        total_squares + jnp.sum(grad_gains * grad_gains) + jnp.sum(grad_bias * grad_bias)
    )
    clip_factor = jnp.minimum(1.0, clip_level / gradient_norm)
    rates = learning_rates()
    new_qkv, second_qkv = adam_update(
        qkv_master, grad_qkv, qkv_first, qkv_second, rates[0], clip_factor
    )
    new_out, second_out = adam_update(
        out_master, grad_out, out_first, out_second, rates[1], clip_factor
    )
    new_up, second_up = adam_update(up_master, grad_up, up_first, up_second, rates[2], clip_factor)
    new_down, second_down = adam_update(
        down_master, grad_down, down_first, down_second, rates[3], clip_factor
    )
    new_gains, second_gains = adam_update(
        norm_gains, grad_gains, gain_first, gain_second, rates[4], clip_factor
    )
    new_bias, second_bias = adam_update(
        position_bias, grad_bias, bias_first, bias_second, rates[5], clip_factor
    )
    return (
        pooled,
        tokens_grad,
        grad_qkv,
        grad_out,
        grad_up,
        grad_down,
        grad_gains,
        grad_bias,
        gradient_norm,
        new_qkv,
        new_out,
        new_up,
        new_down,
        new_gains,
        new_bias,
        second_qkv,
        second_out,
        second_up,
        second_down,
        second_gains,
        second_bias,
    )


def solution(mesh):
    in_specs = (
        P("dp", "tensor", None),
        P("dp", None),
        P("dp", "tensor", None),
        P(None, "dp", "tensor"),
        P("tensor", "dp"),
        P("dp", "tensor"),
        P("tensor", "dp"),
        P(),
        P(),
        P(None, "dp", "tensor"),
        P(None, "dp", "tensor"),
        P("tensor", "dp"),
        P("tensor", "dp"),
        P("dp", "tensor"),
        P("dp", "tensor"),
        P("tensor", "dp"),
        P("tensor", "dp"),
        P(),
        P(),
        P(),
        P(),
    )
    out_specs = (
        P("dp", None, "tensor"),
        P("dp", "tensor", None),
        P(None, "dp", "tensor"),
        P("tensor", "dp"),
        P("dp", "tensor"),
        P("tensor", "dp"),
        P(),
        P(),
        P(),
        P(None, "dp", "tensor"),
        P("tensor", "dp"),
        P("dp", "tensor"),
        P("tensor", "dp"),
        P(),
        P(),
        P(None, "dp", "tensor"),
        P("tensor", "dp"),
        P("dp", "tensor"),
        P("tensor", "dp"),
        P(),
        P(),
    )
    return jax.shard_map(
        per_device, mesh=mesh, in_specs=in_specs, out_specs=out_specs, check_vma=False
    )
```

```python
import jax
import jax.numpy as jnp
from jax import lax
from jax.experimental import pallas as pl
from jax.experimental.pallas import tpu as pltpu
from jax.sharding import PartitionSpec as P

D = 768
H = 12
DH = 64
FF = 3072
SEGS = 16
STEP = 10

norm_eps = 1e-06
mask_fill = -1000000000.0
clip_level = 1.0
beta_first = 0.9
beta_second = 0.999
adam_eps = 1e-08
decay_rate = 0.1
gelu_scale = 0.7978845608028654
gelu_cubic = 0.044715

bf16 = jnp.bfloat16
f32 = jnp.float32
i32 = jnp.int32

QB = 256
KC = 128
EDGE = 128
NEAR = QB + 2 * EDGE
VMEM_LIMIT = 20 << 20

SMEM_SPEC = pl.BlockSpec(memory_space=pltpu.SMEM)
VMEM_SPEC = pl.BlockSpec(memory_space=pltpu.VMEM)


def sds(shape, dtype):
    return jax.ShapeDtypeStruct(shape, dtype)


def nt(a, b):
    return lax.dot_general(a, b, (((1,), (1,)), ((), ())), preferred_element_type=f32)


def nn(a, b):
    return lax.dot_general(a, b, (((1,), (0,)), ((), ())), preferred_element_type=f32)


def call(body, name, smem, vmem, outs, scratch=(), flops=0, moved=0, exps=0, limit=VMEM_LIMIT):
    return pl.pallas_call(
        body,
        out_shape=tuple(outs),
        in_specs=[SMEM_SPEC] * len(smem) + [VMEM_SPEC] * len(vmem),
        out_specs=(VMEM_SPEC,) * len(outs),
        scratch_shapes=list(scratch),
        compiler_params=pltpu.CompilerParams(vmem_limit_bytes=limit),
        cost_estimate=pl.CostEstimate(flops=flops, bytes_accessed=moved, transcendentals=exps),
        name=name,
    )(*smem, *vmem)


def bucket_of(offset):
    distance = jnp.abs(offset)
    large = 8 + sum(
        ((distance >= threshold).astype(jnp.int32) for threshold in (12, 16, 23, 32, 46, 64, 91))
    )
    inner_bucket = jnp.where(distance < 8, distance, large)
    return inner_bucket + jnp.where(offset > 0, 16, 0)


def learning_rates_plain():
    return (
        (2.0 * (D * DH) ** (-0.5), 2.0 * D ** (-0.5), 2.0 * D ** (-0.5)),
        0.5 * (H * DH / 16) ** (-0.5),
        0.5 * D ** (-0.5),
        2.0 * FF ** (-0.5),
        0.25,
        0.5,
    )


def adam_update(parameter, gradient, first_moment, second_moment, step_rate, clip_factor):
    clipped = gradient * clip_factor
    first_new = beta_first * first_moment + (1.0 - beta_first) * clipped
    second_new = beta_second * second_moment + (1.0 - beta_second) * clipped * clipped
    first_hat = first_new / (1.0 - beta_first**STEP)
    second_hat = second_new / (1.0 - beta_second**STEP)
    updated = parameter - step_rate * (
        first_hat / (jnp.sqrt(second_hat) + adam_eps) + decay_rate * parameter
    )
    return (updated, second_new)


def swap_core(value):
    return lax.ppermute(value, "tensor", [(i, i ^ 1) for i in range(lax.axis_size("tensor"))])


def swap_x(value):
    return lax.ppermute(value, "tensor", [(i, i ^ 2) for i in range(lax.axis_size("tensor"))])


def swap_dp(value, bits):
    return lax.ppermute(value, "dp", [(i, i ^ bits) for i in range(lax.axis_size("dp"))])


def swap_y(value):
    return swap_dp(value, 1)


def after(value, *others):
    return lax.optimization_barrier((value, *others))[0]


def high_groups(size):
    bits = []
    bit = 2
    while bit < size:
        bits.append(bit)
        bit *= 2
    groups = []
    while bits:
        take = bits[-2:]
        bits = bits[:-2]
        if len(take) == 2:
            groups.append((take[0], take[1], take[0] | take[1]))
        else:
            groups.append((take[0],))
    return groups


def gather_high(piece, *gates):
    stack = piece[None]
    offsets = [0]
    for group in high_groups(lax.axis_size("dp")):
        got = [swap_dp(stack, bits) for bits in group]
        stack = jnp.concatenate([after(stack, *gates)] + got, axis=0)
        offsets = offsets + [known ^ bits for bits in group for known in offsets]
    return stack, offsets


def scatter_high(blocks, dp_rank, finish, *gates):
    groups = high_groups(lax.axis_size("dp"))
    for index, group in enumerate(groups):
        low = group[0]
        ways = len(group) + 1
        here = (dp_rank // low) % ways
        lead = blocks.shape[0] // ways
        split = blocks.reshape((ways, lead) + blocks.shape[1:])
        total = lax.dynamic_index_in_dim(split, here, 0, keepdims=False).astype(f32)
        got = []
        for way, bits in enumerate(group):
            send = lax.dynamic_index_in_dim(split, here ^ (way + 1), 0, keepdims=False)
            got.append(swap_dp(send.astype(bf16), bits))
        if index + 1 == len(groups):
            return finish(after(total[0], *gates), *(piece[0] for piece in got))
        for piece in got:
            total = total + piece.astype(f32)
        blocks = total


def near_kernel(table_ref, own_ref, other_ref):
    heads = own_ref.shape[0]

    def rows(step, carried):
        start = pl.multiple_of(step * 16, 16)
        row = lax.broadcasted_iota(i32, (16, QB), 0) + start
        col = lax.broadcasted_iota(i32, (16, QB), 1)
        offset = row - EDGE - col
        buckets = bucket_of(offset)
        values = [
            jnp.where(offset > 0, table_ref[31, h], table_ref[15, h]) for h in range(2 * heads)
        ]
        for bucket in list(range(15)) + list(range(17, 31)):
            here = buckets == bucket
            values = [
                jnp.where(here, table_ref[bucket, h], values[h]) for h in range(2 * heads)
            ]
        for h in range(heads):
            own_ref[h, pl.ds(start, 16), :] = values[h]
            other_ref[h, pl.ds(start, 16), :] = values[heads + h]
        return carried

    lax.fori_loop(0, NEAR // 16, rows, 0)


def rms_of(values):
    return lax.rsqrt(jnp.mean(values * values, axis=-1, keepdims=True) + norm_eps)


def norm_kernel(place_ref, keep_ref, got_ref, other_ref, gain_ref, h_ref):
    length = keep_ref.shape[0]
    for index, block in enumerate((keep_ref, got_ref, other_ref.at[0], other_ref.at[1])):
        start = pl.multiple_of(place_ref[index] * length, length)
        values = block[...].astype(f32)
        h_ref[pl.ds(start, length), :] = (values * rms_of(values) * gain_ref[0:1, :]).astype(bf16)


def place_weights(tab_ref, pieces, target, kind=None):
    index = 0
    for piece in pieces:
        rows = piece.shape[-2]
        for slot in range(piece.shape[0]):
            start = pl.multiple_of(tab_ref[index] * rows, 16)
            target[pl.ds(start, rows), :] = piece[slot] if kind is None else piece[slot, kind]
            index += 1


def split_rows(bit_ref, source, own_ref, other_ref):
    rows = own_ref.shape[1]
    bit = bit_ref[0]
    for block in range(own_ref.shape[0]):
        start = pl.multiple_of((2 * block + bit) * rows, 16)
        own_ref[block] = source[pl.ds(start, rows), :]
        start = pl.multiple_of((2 * block + 1 - bit) * rows, 16)
        other_ref[block] = source[pl.ds(start, rows), :]


def sub_sum(values):
    return jnp.sum(values.reshape(values.shape[0] // 8, 8, values.shape[1]), axis=0)


def sub_max(values):
    return jnp.max(values.reshape(values.shape[0] // 8, 8, values.shape[1]), axis=0)


def blocks_even(seq):
    return (seq // QB) % 2 == 0


def near_row(block, chunk):
    start = chunk * KC - block * QB + EDGE
    return start if 0 <= start and start + KC <= NEAR else None


def same_segment(segk_ref, keys, seg_query):
    seg_key = segk_ref[keys, :]
    return jnp.concatenate([seg_key] * (QB // seg_key.shape[1]), axis=1) == seg_query


def attend_kernel(
    flag_ref, far_ref, tab_ref, h_ref, piece_a_ref, piece_b_ref, near_ref, segk_ref, segq_ref,
    wT_ref, qkvT_ref, oT_ref, lse_ref, w_buf, k_buf, s_buf, p_buf,
):
    seq = h_ref.shape[0]
    heads = near_ref.shape[0]
    width = oT_ref.shape[0]
    size = width // heads
    chunks = seq // KC
    assert blocks_even(seq)
    place_weights(tab_ref, (piece_a_ref, piece_b_ref), w_buf)
    wT_ref[...] = w_buf[...].T
    qkvT_ref[...] = nt(wT_ref[0 : 3 * width, :], h_ref[...]).astype(bf16)
    blocks = seq // QB

    def rows(part, h):
        return pl.ds(pl.multiple_of(part * width + h * size, size), size)

    def score(h, block):
        s_buf[block % 2] = nn(k_buf[h % 2], qkvT_ref[rows(0, h), block * QB : (block + 1) * QB])

    def soften(h, block, masked):
        slot = block % 2
        qs = slice(block * QB, (block + 1) * QB)
        top = jnp.full((8, QB), -3e38, f32)
        for chunk in range(chunks):
            ks = slice(chunk * KC, (chunk + 1) * KC)
            row = near_row(block, chunk)
            if row is None:
                scores = s_buf[slot, ks, :] + far_ref[0 if chunk * KC < block * QB else 1, h]
            else:
                scores = s_buf[slot, ks, :] + near_ref[h, row : row + KC, :]
            if masked:
                scores = jnp.where(same_segment(segk_ref, ks, segq_ref[:, qs]), scores, mask_fill)
            s_buf[slot, ks, :] = scores
            top = jnp.maximum(top, sub_max(scores))
        top = jnp.max(top, axis=0, keepdims=True)
        total = jnp.zeros((8, QB), f32)
        for chunk in range(chunks):
            ks = slice(chunk * KC, (chunk + 1) * KC)
            exps = jnp.exp(s_buf[slot, ks, :] - top)
            s_buf[slot, ks, :] = exps
            total = total + sub_sum(exps)
        total = jnp.sum(total, axis=0, keepdims=True)
        scale = 1.0 / total
        for chunk in range(chunks):
            ks = slice(chunk * KC, (chunk + 1) * KC)
            p_buf[slot, ks, :] = (s_buf[slot, ks, :] * scale).astype(bf16)
        lse_ref[pl.ds(h, 1), qs] = top + jnp.log(total)

    def mix(h, block):
        qs = slice(block * QB, (block + 1) * QB)
        oT_ref[rows(0, h), qs] = nn(qkvT_ref[rows(2, h), :], p_buf[block % 2]).astype(bf16)

    def run(masked):
        k_buf[0] = qkvT_ref[rows(1, 0), :].T
        score(0, 0)

        def head(h, carried):
            for block in range(blocks):
                if block + 1 < blocks:
                    score(h, block + 1)
                else:
                    later = jnp.minimum(h + 1, heads - 1)
                    k_buf[(h + 1) % 2] = qkvT_ref[rows(1, later), :].T
                    s_buf[0] = nn(k_buf[(h + 1) % 2], qkvT_ref[rows(0, later), 0:QB])
                soften(h, block, masked)
                if block:
                    mix(h, block - 1)
            mix(h, blocks - 1)
            return carried

        lax.fori_loop(0, heads, head, 0)

    @pl.when(flag_ref[0] == 1)
    def _():
        run(False)

    @pl.when(flag_ref[0] != 1)
    def _():
        run(True)


def attend(flag, far, tab, h, pieces, near, segk, segq):
    seq = h.shape[0]
    cols = pieces[0].shape[2]
    width = cols // 4
    return call(
        attend_kernel,
        "attend",
        (flag, far, tab),
        (h, *pieces, near, segk, segq),
        (sds((cols, D), bf16), sds((3 * width, seq), bf16), sds((width, seq), bf16), sds((8, seq), f32)),
        (
            pltpu.VMEM((D, cols), bf16),
            pltpu.VMEM((2, seq, width // near.shape[0]), bf16),
            pltpu.VMEM((2, seq, QB), f32),
            pltpu.VMEM((2, seq, QB), bf16),
        ),
        flops=14_000_000_000,
        moved=8_000_000,
        exps=3 * seq * seq,
    )


def attend_back_kernel(
    flag_ref, far_ref, bit_ref, qkvT_ref, doT_ref, lse_ref, near_ref, segk_ref, segq_ref, h_ref, goT_ref,
    dqkvT_ref, own_ref, other_ref, dnear_ref, dfar_ref,
    kv_buf, s_buf, dp_buf, ds_buf, pt_buf, dt_buf, dk_buf, dv_buf, g_buf,
):
    width, seq = doT_ref.shape
    heads = near_ref.shape[0]
    size = width // heads
    blocks = seq // QB
    chunks = seq // KC
    assert blocks_even(seq)

    def rows(part, h):
        return pl.ds(pl.multiple_of(part * width + h * size, size), size)

    def key_values(h, turn):
        kv_buf[turn] = jnp.concatenate([qkvT_ref[rows(1, h), :], qkvT_ref[rows(2, h), :]], axis=0).T

    def products(h, turn, block):
        slot = block % 2
        qs = slice(block * QB, (block + 1) * QB)
        zeros = jnp.zeros((size, QB), bf16)
        s_buf[slot] = nn(kv_buf[turn], jnp.concatenate([qkvT_ref[rows(0, h), qs], zeros], axis=0))
        dp_buf[slot] = nn(kv_buf[turn], jnp.concatenate([zeros, doT_ref[rows(0, h), qs]], axis=0))

    def soften(h, block, masked):
        slot = block % 2
        qs = slice(block * QB, (block + 1) * QB)
        lse = lse_ref[pl.ds(h, 1), qs]
        lse_left = lse - far_ref[0, h]
        lse_right = lse - far_ref[1, h]
        dots = jnp.zeros((8, QB), f32)
        for chunk in range(chunks):
            ks = slice(chunk * KC, (chunk + 1) * KC)
            row = near_row(block, chunk)
            if row is None:
                scores = s_buf[slot, ks, :] - (lse_left if chunk * KC < block * QB else lse_right)
            else:
                scores = s_buf[slot, ks, :] + near_ref[h, row : row + KC, :] - lse
            probs = jnp.exp(scores)
            if masked:
                probs = jnp.where(same_segment(segk_ref, ks, segq_ref[:, qs]), probs, 0.0)
            s_buf[slot, ks, :] = probs
            pt_buf[slot, :, ks] = probs.astype(bf16).T
            dots = dots + sub_sum(probs * dp_buf[slot, ks, :])
        dots = jnp.sum(dots, axis=0, keepdims=True)
        for chunk in range(chunks):
            ks = slice(chunk * KC, (chunk + 1) * KC)
            d_scores = (s_buf[slot, ks, :] * (dp_buf[slot, ks, :] - dots)).astype(bf16)
            ds_buf[slot, ks, :] = d_scores
            dt_buf[slot, :, ks] = d_scores.T
            row = near_row(block, chunk)
            if row is not None:
                if block == 0 or (block == 1 and row == 0):
                    dnear_ref[h, row : row + KC, :] = d_scores.astype(f32)
                else:
                    dnear_ref[h, row : row + KC, :] += d_scores.astype(f32)

    def outputs(h, block):
        slot = block % 2
        qs = slice(block * QB, (block + 1) * QB)
        dqkvT_ref[rows(0, h), qs] = nn(qkvT_ref[rows(1, h), :], ds_buf[slot]).astype(bf16)
        d_keys = nn(
            jnp.concatenate([qkvT_ref[rows(0, h), qs], jnp.ones((16, QB), bf16)], axis=0),
            dt_buf[slot],
        )
        d_values = nn(doT_ref[rows(0, h), qs], pt_buf[slot])
        if block == 0:
            dk_buf[...] = d_keys[0:size]
            dv_buf[...] = d_values
        elif block + 1 < blocks:
            dk_buf[...] += d_keys[0:size]
            dv_buf[...] += d_values
        else:
            dqkvT_ref[rows(1, h), :] = (dk_buf[...] + d_keys[0:size]).astype(bf16)
            dqkvT_ref[rows(2, h), :] = (dv_buf[...] + d_values).astype(bf16)
        sums = d_keys[size : size + 1]
        left_end = max(0, block * QB - EDGE)
        right_start = min(seq, block * QB + QB + EDGE)
        lane = lax.broadcasted_iota(i32, (1, 128), 1)
        line = jnp.zeros((1, 128), f32)
        if left_end:
            line = jnp.where(lane == 0, jnp.sum(sums[:, :left_end], axis=1, keepdims=True), line)
        if right_start < seq:
            line = jnp.where(lane == 1, jnp.sum(sums[:, right_start:], axis=1, keepdims=True), line)
        if block == 0:
            dfar_ref[pl.ds(h, 1), :] = line
        else:
            dfar_ref[pl.ds(h, 1), :] += line

    def run(masked):
        key_values(0, 0)
        products(0, 0, 0)

        def head(h, carried):
            for block in range(blocks):
                if block + 1 < blocks:
                    products(h, h % 2, block + 1)
                else:
                    later = jnp.minimum(h + 1, heads - 1)
                    key_values(later, (h + 1) % 2)
                    products(later, (h + 1) % 2, 0)
                soften(h, block, masked)
                if block:
                    outputs(h, block - 1)
            outputs(h, blocks - 1)
            return carried

        lax.fori_loop(0, heads, head, 0)

    @pl.when(flag_ref[0] == 1)
    def _():
        run(False)

    @pl.when(flag_ref[0] != 1)
    def _():
        run(True)

    grad = jnp.concatenate([nn(dqkvT_ref[...], h_ref[...]).astype(bf16), goT_ref[...]], axis=0)
    if other_ref is None:
        own_ref[...] = grad.T
    else:
        g_buf[...] = grad.T
        split_rows(bit_ref, g_buf, own_ref, other_ref)


def attend_back(flag, far, bit, qkvT, doT, lse, near, segk, segq, h, goT, grad_outs):
    width, seq = doT.shape
    size = width // near.shape[0]
    body = attend_back_kernel
    if len(grad_outs) == 1:

        def body(*refs):
            attend_back_kernel(*refs[:13], None, *refs[13:])

    return call(
        body,
        "attend_back",
        (flag, far, bit),
        (qkvT, doT, lse, near, segk, segq, h, goT),
        (sds(qkvT.shape, bf16), *grad_outs, sds(near.shape, f32), sds((8, 128), f32)),
        (
            pltpu.VMEM((2, seq, 2 * size), bf16),
            pltpu.VMEM((2, seq, QB), f32),
            pltpu.VMEM((2, seq, QB), f32),
            pltpu.VMEM((2, seq, QB), bf16),
            pltpu.VMEM((2, QB, seq), bf16),
            pltpu.VMEM((2, QB, seq), bf16),
            pltpu.VMEM((size, seq), f32),
            pltpu.VMEM((size, seq), f32),
            pltpu.VMEM((D, 4 * width), bf16),
        ),
        flops=20_000_000_000,
        moved=8_000_000,
        exps=3 * seq * seq,
    )


def project_kernel(place_ref, oT0_ref, oT1_ref, wT0_ref, wT1_ref, keep_ref, send_ref, o_buf):
    width = oT0_ref.shape[0]
    length = keep_ref.shape[0] // 2
    o_buf[...] = jnp.concatenate([oT0_ref[...], oT1_ref[...]], axis=0).T
    w = jnp.concatenate([wT0_ref[3 * width :, :], wT1_ref[3 * width :, :]], axis=0)
    for index in range(4):
        start = pl.multiple_of(place_ref[index] * length, length)
        part = nn(o_buf[pl.ds(start, length), :], w)
        rows = slice((index % 2) * length, (index % 2 + 1) * length)
        if index < 2:
            keep_ref[rows, :] = part
        else:
            send_ref[rows, :] = part.astype(send_ref.dtype)


def middle_kernel(keep_tok_ref, got_tok_ref, part_ref, got_ref, gain_ref, x2_ref, h_ref):
    length = keep_tok_ref.shape[0]
    for index, block in enumerate((keep_tok_ref, got_tok_ref)):
        rows = slice(index * length, (index + 1) * length)
        values = block[...].astype(f32) + part_ref[rows, :] + got_ref[rows, :].astype(f32)
        x2_ref[rows, :] = values
        h_ref[rows, :] = (values * rms_of(values) * gain_ref[1:2, :]).astype(bf16)


def split3(values):
    high = values.astype(bf16)
    rest = values - high.astype(f32)
    mid = rest.astype(bf16)
    low = (rest - mid.astype(f32)).astype(bf16)
    return high, mid, low


def feed_rows(h, cot, u_buf, d_buf, act_ref, dpre_ref, rows):
    pre = nn(h, u_buf[...])
    d_act = nn(cot, d_buf[...])
    square = pre * pre
    bent = jnp.tanh(gelu_scale * pre * (1.0 + gelu_cubic * square))
    half_up = 0.5 * (1.0 + bent)
    act_ref[rows, :] = (pre * half_up).astype(bf16)
    slope = half_up + (0.5 * gelu_scale) * pre * (1.0 - bent * bent) * (
        1.0 + (3.0 * gelu_cubic) * square
    )
    d_pre = (d_act * slope).astype(bf16)
    dpre_ref[rows, :] = d_pre
    return nt(d_pre, u_buf[...])


def pooled_units(hot, act_ref, d_buf):
    pooled = None
    for term in split3(nn(hot, act_ref[...])):
        part = nt(term, d_buf[...])
        pooled = part if pooled is None else pooled + part
    return pooled


def feed_own_kernel(
    tab_ref, h_own_ref, h_oth_ref, cot_keep_ref, cot_got_ref, cot_oth_ref,
    a_ref, b_ref, hot_ref, x2_ref,
    act_ref, dpre_ref, dh_ref, pooled_ref, u_buf, d_buf,
):
    place_weights(tab_ref, (a_ref, b_ref), u_buf, 0)
    place_weights(tab_ref, (a_ref, b_ref), d_buf, 1)
    length = cot_keep_ref.shape[0]
    cots = (cot_keep_ref, cot_got_ref, cot_oth_ref.at[0], cot_oth_ref.at[1])
    for index in range(4):
        rows = slice(index * length, (index + 1) * length)
        half = slice((index % 2) * length, (index % 2 + 1) * length)
        h = (h_own_ref if index < 2 else h_oth_ref)[half, :]
        dh_ref[rows, :] = feed_rows(h, cots[index][...], u_buf, d_buf, act_ref, dpre_ref, rows)
    hot = hot_ref[...]
    pooled = pooled_units(hot, act_ref, d_buf)
    for term in split3(x2_ref[...]):
        pooled = pooled + nn(hot[:, 0 : 2 * length], term)
    pooled_ref[...] = pooled


def feed_other_kernel(
    tab_ref, h_own_ref, h_oth_ref, cot_keep_ref, cot_got_ref, cot_oth_ref,
    ua_ref, ub_ref, db_ref, hot_ref, dh_ref, pool_ref,
    act_ref, dpre_ref, keep_ref, send_ref, pooled_ref, u_buf, d_buf,
):
    place_weights(tab_ref, (ua_ref,), u_buf, 0)
    place_weights(tab_ref, (ua_ref,), d_buf, 1)
    for source, target in ((ub_ref, u_buf), (db_ref, d_buf)):
        first = ua_ref.shape[0]
        rows = source.shape[1]
        for slot in range(source.shape[0]):
            start = pl.multiple_of(tab_ref[first + slot] * rows, 16)
            target[pl.ds(start, rows), :] = source[slot]
    length = cot_keep_ref.shape[0]
    cots = (cot_keep_ref, cot_got_ref, cot_oth_ref.at[0], cot_oth_ref.at[1])
    for index in (2, 3, 0, 1):
        rows = slice(index * length, (index + 1) * length)
        half = slice((index % 2) * length, (index % 2 + 1) * length)
        h = (h_own_ref if index < 2 else h_oth_ref)[half, :]
        total = dh_ref[rows, :] + feed_rows(
            h, cots[index][...], u_buf, d_buf, act_ref, dpre_ref, rows
        )
        if index < 2:
            keep_ref[half, :] = total
        else:
            send_ref[half, :] = total.astype(send_ref.dtype)
    pooled_ref[...] = pool_ref[...] + pooled_units(hot_ref[...], act_ref, d_buf)


def weight_grad_kernel(
    bit_ref, h_own_ref, h_oth_ref, cot_keep_ref, cot_got_ref, cot_oth_ref, act_ref, dpre_ref, *refs
):
    *outs, g_buf = refs
    hT = jnp.concatenate([h_own_ref[...], h_oth_ref[...]], axis=0).T
    cotT = jnp.concatenate(
        [cot_keep_ref[...], cot_got_ref[...], cot_oth_ref[0], cot_oth_ref[1]], axis=0
    ).T
    if len(outs) == 2:
        outs[0][...] = nn(hT, dpre_ref[...]).astype(bf16)
        outs[1][...] = nn(cotT, act_ref[...]).astype(bf16)
    else:
        g_buf[0] = nn(hT, dpre_ref[...]).astype(bf16)
        split_rows(bit_ref, g_buf.at[0], outs[0], outs[1])
        g_buf[1] = nn(cotT, act_ref[...]).astype(bf16)
        split_rows(bit_ref, g_buf.at[1], outs[2], outs[3])


def norm_back(values, gain, upstream):
    scale = rms_of(values)
    normed = values * scale
    gain_grad = jnp.sum(upstream * normed, axis=0, keepdims=True)
    scaled = upstream * gain
    inner = jnp.mean(scaled * normed, axis=-1, keepdims=True)
    return scale * (scaled - normed * inner), gain_grad


def middle_back_kernel(
    x2_ref, part_ref, got_ref, cot_keep_ref, cot_got_ref, gain_ref, dx2_ref, da_ref, gain_grad_ref
):
    length = x2_ref.shape[0] // 2
    for index, cot in enumerate((cot_keep_ref, cot_got_ref)):
        rows = slice(index * length, (index + 1) * length)
        d_values, gain_grad = norm_back(
            x2_ref[rows, :], gain_ref[1:2, :], part_ref[rows, :] + got_ref[rows, :].astype(f32)
        )
        dx2 = cot[...].astype(f32) + d_values
        dx2_ref[rows, :] = dx2
        da_ref[rows, :] = dx2.astype(bf16)
        if index == 0:
            gain_grad_ref[...] = gain_grad
        else:
            gain_grad_ref[...] += gain_grad


def branch_back_kernel(
    place_ref, da_own_ref, da_oth_ref, wT0_ref, wT1_ref, oT0_ref, oT1_ref,
    doT0_ref, doT1_ref, g0_ref, g1_ref, da_buf,
):
    width = oT0_ref.shape[0]
    length = da_own_ref.shape[0] // 2
    for index in range(4):
        start = pl.multiple_of(place_ref[index] * length, length)
        half = slice((index % 2) * length, (index % 2 + 1) * length)
        da_buf[pl.ds(start, length), :] = (da_own_ref if index < 2 else da_oth_ref)[half, :]
    da = da_buf[...]
    doT0_ref[...] = nt(wT0_ref[3 * width :, :], da).astype(bf16)
    doT1_ref[...] = nt(wT1_ref[3 * width :, :], da).astype(bf16)
    g0_ref[...] = nn(oT0_ref[...], da).astype(bf16)
    g1_ref[...] = nn(oT1_ref[...], da).astype(bf16)


def first_back_kernel(place_ref, d0_ref, d1_ref, wT0_ref, wT1_ref, keep_ref, send_ref, d_buf):
    rows3 = d0_ref.shape[0]
    length = keep_ref.shape[0] // 2
    d_buf[...] = jnp.concatenate([d0_ref[...], d1_ref[...]], axis=0).T
    w = jnp.concatenate([wT0_ref[0:rows3, :], wT1_ref[0:rows3, :]], axis=0)
    for index in (2, 3, 0, 1):
        start = pl.multiple_of(place_ref[index] * length, length)
        part = nn(d_buf[pl.ds(start, length), :], w)
        rows = slice((index % 2) * length, (index % 2 + 1) * length)
        if index < 2:
            keep_ref[rows, :] = part
        else:
            send_ref[rows, :] = part.astype(send_ref.dtype)


def token_grad_kernel(
    keep_tok_ref, got_tok_ref, part_ref, got_ref, dx2_ref, gain_ref, own_ref, away_ref, gain_grad_ref
):
    length = keep_tok_ref.shape[0]
    for index, block in enumerate((keep_tok_ref, got_tok_ref)):
        rows = slice(index * length, (index + 1) * length)
        d_values, gain_grad = norm_back(
            block[...].astype(f32), gain_ref[0:1, :], part_ref[rows, :] + got_ref[rows, :].astype(f32)
        )
        if index == 0:
            own_ref[...] = dx2_ref[rows, :] + d_values
            gain_grad_ref[...] = gain_grad
        else:
            away_ref[...] = dx2_ref[rows, :] + d_values
            gain_grad_ref[...] += gain_grad


def bias_grad_kernel(dnear0_ref, dnear1_ref, dfar0_ref, dfar1_ref, grad_ref, line_buf):
    heads = dnear0_ref.shape[0]
    span = 2 * NEAR
    line_buf[...] = jnp.zeros_like(line_buf)
    for side, dnear_ref in enumerate((dnear0_ref, dnear1_ref)):
        for h in range(heads):
            values = dnear_ref[h]
            left = NEAR
            rows = NEAR
            while rows > 8:
                rows //= 2
                low, high = values[:rows], values[rows:]
                if rows % 128 == 0:
                    pad = jnp.zeros((rows, rows), f32)
                    values = jnp.concatenate([pad, low], axis=1) + jnp.concatenate([high, pad], axis=1)
                    left -= rows
                else:
                    if values.shape[1] < span:
                        missing = span - values.shape[1]
                        pad = jnp.zeros((rows, missing), f32)
                        low = jnp.concatenate([pad, low], axis=1)
                        high = jnp.concatenate([pad, high], axis=1)
                        left -= missing
                    values = low + pltpu.roll(high, span - rows, 1)
            while rows > 1:
                rows //= 2
                values = values[:rows] + pltpu.roll(values[rows:], span - rows, 1)
            index = side * heads + h
            line_buf[index : index + 1, :] = values
    lines = line_buf[...]
    shift = span - QB
    col = lax.broadcasted_iota(i32, lines.shape, 1)
    buckets = bucket_of(shift - EDGE - col)
    lane = lax.broadcasted_iota(i32, (8, 128), 1)
    grad = jnp.zeros((8, 128), f32)
    for bucket in range(32):
        if bucket != 16:
            total = jnp.sum(jnp.where(buckets == bucket, lines, 0.0), axis=1, keepdims=True)
            grad = jnp.where(lane == bucket, total, grad)
    grad_ref[...] = grad
    for side, dfar_ref in enumerate((dfar0_ref, dfar1_ref)):
        far = dfar_ref[0:heads, :]
        lane = lax.broadcasted_iota(i32, far.shape, 1)
        left = jnp.sum(jnp.where(lane == 0, far, 0.0), axis=1, keepdims=True)
        right = jnp.sum(jnp.where(lane == 1, far, 0.0), axis=1, keepdims=True)
        grad_ref[side * heads : (side + 1) * heads, :] += jnp.where(
            lane == 15, left, jnp.where(lane == 31, right, 0.0)
        )


def finish_a_kernel(own_ref, *refs):
    *pieces, qkv_ref, out_ref, squares_ref = refs
    total = own_ref[...]
    for piece in pieces:
        total = total + piece[...].astype(f32)
    width = qkv_ref.shape[2]
    for part in range(3):
        qkv_ref[part] = total[:, part * width : (part + 1) * width]
    out_ref[...] = total[:, 3 * width :].T
    squares_ref[...] = jnp.broadcast_to(jnp.sum(total * total, axis=(0, 1), keepdims=True), (8, 128))


def finish_ud_kernel(own_ref, *refs):
    *pieces, up_ref, down_ref, squares_ref = refs
    total = own_ref[...]
    for piece in pieces:
        total = total + piece[...].astype(f32)
    units = up_ref.shape[1]
    up_ref[...] = total[:, :units]
    down_ref[...] = total[:, units:]
    squares_ref[...] = jnp.broadcast_to(jnp.sum(total * total, axis=(0, 1), keepdims=True), (8, 128))


def adam_kernel(small_ref, squares_ref, *refs):
    total = jnp.sum(jnp.sum(squares_ref[...], axis=0)[0:1, 0:1], axis=(0, 1), keepdims=True)
    norm = jnp.sqrt(total + small_ref[0:1, 0:1])
    clip = jnp.minimum(1.0, clip_level / norm)
    count = 6
    outs = refs[4 * count :]
    rates = learning_rates_plain()
    for index in range(count):
        param, grad, first, second = (refs[4 * index + k] for k in range(4))
        new, new_second = outs[2 * index], outs[2 * index + 1]
        if isinstance(rates[index], tuple):
            for part, rate in enumerate(rates[index]):
                value, moment = adam_update(
                    param[part], grad[part], first[part], second[part], rate, clip
                )
                new[part] = value
                new_second[part] = moment
        else:
            value, moment = adam_update(
                param[...], grad[...], first[...], second[...], rates[index], clip
            )
            new[...] = value
            new_second[...] = moment
    outs[2 * count][...] = jnp.broadcast_to(norm, (8, 128))


def per_device(
    tokens,
    segment_ids,
    cotangent,
    qkv_master,
    out_master,
    up_master,
    down_master,
    norm_gains,
    position_bias,
    qkv_first,
    qkv_second,
    out_first,
    out_second,
    up_first,
    up_second,
    down_first,
    down_second,
    gain_first,
    gain_second,
    bias_first,
    bias_second,
):
    rank = lax.axis_index("tensor")
    dp_rank = lax.axis_index("dp")
    dp_size = lax.axis_size("dp")
    side = rank // 2
    row_bit = dp_rank % 2
    rows, length = tokens.shape[0], tokens.shape[1]
    seq = segment_ids.shape[1]
    shard_rows, width = qkv_master.shape[1], qkv_master.shape[2]
    units = up_master.shape[1]
    heads = position_bias.shape[1] // lax.axis_size("tensor")
    half = (seq // 2, D)
    assert rows == 2 and lax.axis_size("tensor") == 4 and seq == 4 * length
    pick = lambda value, index: lax.dynamic_index_in_dim(value, index, 0, keepdims=False)

    places = jnp.stack([rank, rank ^ 2, rank ^ 1, rank ^ 3]).astype(i32)

    pack_a = jnp.concatenate(
        [qkv_master[0], qkv_master[1], qkv_master[2], out_master.T], axis=1
    ).astype(bf16)
    tables = [
        lax.dynamic_slice_in_dim(position_bias, shard * heads, heads, 1)
        for shard in (rank, rank ^ 2)
    ]
    fars = [jnp.stack([table[15], table[31]]) for table in tables]
    near0, near1 = call(
        near_kernel,
        "bias_tiles",
        (jnp.concatenate(tables, axis=1),),
        (),
        (sds((heads, NEAR, QB), f32),) * 2,
        flops=10_000_000_000,
        moved=4_000_000,
    )
    high_a, offsets = gather_high(pack_a, near0, near1)
    tok_keep = pick(tokens, side)
    tok_got = swap_x(pick(tokens, 1 - side))
    cot_keep = pick(cotangent, side)
    cot_got = swap_x(after(pick(cotangent, 1 - side), tok_got))
    tok_other = swap_core(jnp.stack([tok_keep, tok_got]))
    a_y = swap_y(high_a)
    a_x = swap_x(high_a)
    a_own = (high_a, a_y)

    all_offsets = offsets + [known ^ 1 for known in offsets]
    whole_rows = shard_rows % 16 == 0
    if whole_rows:
        tab = jnp.stack([dp_rank ^ known for known in all_offsets]).astype(i32)
        order = lambda pair: pair
        blocks_out = (sds((dp_size // 2, shard_rows, D), bf16),) * 2
    else:
        slot_of = [0] * dp_size
        for slot, known in enumerate(all_offsets):
            slot_of[known] = slot
        slots = jnp.asarray(slot_of, i32)[dp_rank ^ jnp.arange(dp_size)]
        tab = jnp.arange(2, dtype=i32)
        blocks_out = (sds((D, D), bf16),)

        def order(pair):
            both = jnp.take(jnp.concatenate(pair, axis=0), slots, axis=0)
            both = jnp.moveaxis(both, 0, -3)
            both = both.reshape(both.shape[:-3] + (D, both.shape[-1]))
            both = jnp.stack([both[..., : D // 2, :], both[..., D // 2 :, :]])[:, None]
            return both[0], both[1]

    bit = row_bit.astype(i32).reshape(1)

    seg_row = pick(segment_ids, side)
    flag = (seg_row[0] == seg_row[seq - 1]).astype(i32).reshape(1)
    segk = jnp.broadcast_to(seg_row[:, None], (seq, 128))
    segq = seg_row[None, :]
    slot_ids = jnp.arange(SEGS, dtype=i32)
    seg_blocks = seg_row.reshape(4, length)
    seg_rel = jnp.concatenate([pick(seg_blocks, rank ^ bits) for bits in (0, 2, 1, 3)])
    hot = (seg_rel[None, :] == slot_ids[:, None]).astype(bf16)
    (h1,) = call(
        norm_kernel,
        "first_norm",
        (after(places, high_a),),
        (tok_keep, tok_got, tok_other, norm_gains),
        (sds((seq, D), bf16),),
        moved=6_000_000,
    )
    flag0 = after(flag, a_y, a_x, near0, near1, h1)
    a_other = (a_x, swap_y(after(a_x, a_y)))
    wT0, qkvT0, oT0, lse0 = attend(flag0, fars[0], tab, h1, order(a_own), near0, segk, segq)
    pack_ud = jnp.stack([up_master, down_master.T]).astype(bf16)
    high_ud, _ = gather_high(after(pack_ud, high_a), oT0)
    flag1 = after(flag0, a_other[1], high_ud, oT0)
    ud_x = swap_x(after(high_ud, a_other[1]))
    ud_y = swap_y(after(high_ud, a_other[1]))
    wT1, qkvT1, oT1, lse1 = attend(flag1, fars[1], tab, h1, order(a_other), near1, segk, segq)

    keep, send = call(
        project_kernel,
        "project",
        (after(places, oT1),),
        (oT0, oT1, wT0, wT1),
        (sds(half, f32), sds(half, f32)),
        (pltpu.VMEM((seq, 2 * width), bf16),),
        flops=2 * seq * 2 * width * D,
        moved=8_000_000,
    )
    cot_other = swap_core(jnp.stack([after(cot_keep, keep), cot_got]))
    x2, h2 = call(
        middle_kernel,
        "second_norm",
        (),
        (tok_keep, tok_got, keep, swap_core(send), norm_gains),
        (sds(half, f32), sds(half, bf16)),
        moved=7_000_000,
    )
    h2_other = swap_core(h2)
    u_xy = swap_y(after(ud_x, ud_y, h2)[:, 0])
    d_xy = swap_x(after(ud_y, ud_x, h2)[:, 1])
    cots = (cot_keep, cot_got, cot_other)
    feed_flops = 2 * 3 * seq * D * units
    act0, d_pre0, dh_part, pool_part = call(
        feed_own_kernel,
        "feed_own",
        (after(tab, ud_y, ud_x),),
        (h2, h2_other, *cots, *order((high_ud, ud_y)), hot, x2),
        (
            sds((seq, units), bf16),
            sds((seq, units), bf16),
            sds((seq, D), f32),
            sds((SEGS, D), f32),
        ),
        [pltpu.VMEM((D, units), bf16)] * 2,
        flops=feed_flops,
        moved=14_000_000,
        exps=seq * units,
    )

    def weight_grads(act, d_pre, name):
        return call(
            weight_grad_kernel,
            name,
            (bit,),
            (h2, h2_other, *cots, act, d_pre),
            blocks_out * 2,
            (pltpu.VMEM((2, D, units), bf16),),
            flops=2 * 2 * seq * D * units,
            moved=9_000_000,
        )

    def of_y(grad, wanted):
        blocks = grad.reshape((dp_size // 2, 2, shard_rows) + grad.shape[1:])
        return lax.dynamic_index_in_dim(blocks, wanted, 1, keepdims=False)

    def by_y(grads):
        if whole_rows:
            return tuple(grads)
        return tuple(of_y(grad, wanted) for grad in grads for wanted in (row_bit, 1 - row_bit))

    gu0_own, gu0_oth, gd0_own, gd0_oth = by_y(weight_grads(act0, d_pre0, "feed_grads_own"))
    if whole_rows:
        ud_other = (ud_x, u_xy, d_xy)
    else:
        first, second = order((ud_x, jnp.stack([u_xy, d_xy], axis=1)))
        ud_other = (first, second[:, 0], second[:, 1])
    act1, d_pre1, keep, send, pool_part = call(
        feed_other_kernel,
        "feed_other",
        (after(tab, gu0_oth, gd0_oth),),
        (h2, h2_other, *cots, *ud_other, hot, dh_part, pool_part),
        (
            sds((seq, units), bf16),
            sds((seq, units), bf16),
            sds(half, f32),
            sds(half, f32),
            sds((SEGS, D), f32),
        ),
        [pltpu.VMEM((D, units), bf16)] * 2,
        flops=feed_flops,
        moved=18_000_000,
        exps=seq * units,
    )
    got = swap_core(send)
    gu1_own, gu1_oth, gd1_own, gd1_oth = by_y(weight_grads(act1, d_pre1, "feed_grads_other"))
    dx2, da, gain_grad_second = call(
        middle_back_kernel,
        "second_norm_back",
        (),
        (x2, keep, got, cot_keep, cot_got, after(norm_gains, gu1_oth, gd1_oth)),
        (sds(half, f32), sds(half, bf16), sds((1, D), f32)),
        moved=8_000_000,
    )
    da_other = swap_core(da)
    add = lambda one, two: (one.astype(f32) + two.astype(f32)).astype(bf16)

    up_y1 = swap_y(gu1_oth)
    down_x1 = swap_x(gd1_oth)
    up_y0 = swap_y(after(gu0_oth, up_y1))
    down_x0 = swap_x(after(gd1_own, down_x1))
    doT0, doT1, goT0, goT1 = call(
        branch_back_kernel,
        "branch_back",
        (places,),
        (da, da_other, wT0, wT1, oT0, oT1),
        (sds((width, seq), bf16),) * 2 + (sds((width, D), bf16),) * 2,
        (pltpu.VMEM((seq, D), bf16),),
        flops=2 * 2 * seq * D * 2 * width,
        moved=6_000_000,
    )
    up_x = swap_x(add(after(gu1_own, doT0), up_y1))
    down_y = swap_y(add(after(gd0_oth, doT0), down_x1))
    flag2 = after(flag1, up_y1, down_x1, doT0, doT1)
    dqkvT1, *ga1, dnear1, dfar1 = attend_back(
        flag2, fars[1], bit, qkvT1, doT1, lse1, near1, segk, segq, h1, goT1, blocks_out
    )
    ga1_own, ga1_oth = by_y(ga1)
    gu0_own, gd0_own = after(gu0_own, ga1_oth), after(gd0_own, ga1_oth)
    total = lambda one, two, three: one.astype(f32) + two.astype(f32) + three.astype(f32)
    ud_sum = jnp.concatenate(
        [total(gu0_own, up_y0, up_x), total(gd0_own, down_x0, down_y)], axis=2
    )
    a_y1 = swap_y(ga1_oth)
    flag3 = after(flag2, ud_sum, ga1_oth)
    dqkvT0, *ga0, dnear0, dfar0 = attend_back(
        flag3, fars[0], bit, qkvT0, doT0, lse0, near0, segk, segq, h1, goT0, blocks_out
    )
    ga0_own, ga0_oth = by_y(ga0)


    def finish_ud(own, *pieces):
        if whole_rows:
            return call(
                finish_ud_kernel,
                "finish_ud",
                (),
                (own, *pieces),
                (sds((shard_rows, units), f32),) * 2 + (sds((8, 128), f32),),
                moved=2_000_000,
            )
        for piece in pieces:
            own = own + piece.astype(f32)
        return own[:, :units], own[:, units:], jnp.broadcast_to(jnp.sum(own * own), (8, 128))

    def finish_a(own, *pieces):
        if whole_rows:
            return call(
                finish_a_kernel,
                "finish_a",
                (),
                (own, *pieces),
                (
                    sds(qkv_master.shape, f32),
                    sds(out_master.shape, f32),
                    sds((8, 128), f32),
                ),
                moved=2_000_000,
            )
        for piece in pieces:
            own = own + piece.astype(f32)
        parts = jnp.stack([own[:, i * width : (i + 1) * width] for i in range(3)])
        return parts, own[:, 3 * width :].T, jnp.broadcast_to(jnp.sum(own * own), (8, 128))

    a_x1 = swap_x(add(after(ga1_own, dqkvT0), a_y1))
    a_y0 = swap_y(ga0_oth)
    keep, send = call(
        first_back_kernel,
        "first_back",
        (after(places, dqkvT0, a_y1),),
        (dqkvT0, dqkvT1, wT0, wT1),
        (sds(half, f32), sds(half, f32)),
        (pltpu.VMEM((seq, 6 * width), bf16),),
        flops=2 * seq * 6 * width * D,
        moved=8_000_000,
    )
    tg_own, tg_away, gain_grad_first = call(
        token_grad_kernel,
        "first_norm_back",
        (),
        (tok_keep, tok_got, keep, swap_core(send), dx2, norm_gains),
        (sds((length, D), f32), sds((length, D), f32), sds((1, D), f32)),
        moved=8_000_000,
    )
    tg_got = swap_x(tg_away)
    (table_grad,) = call(
        bias_grad_kernel,
        "bias_grad",
        (),
        (dnear0, dnear1, dfar0, dfar1),
        (sds((8, 128), f32),),
        (pltpu.VMEM((8, 2 * NEAR), f32),),
        moved=4_000_000,
    )
    grad_up, grad_downT, ud_squares = scatter_high(ud_sum, dp_rank, finish_ud, dqkvT0, keep)
    grad_qkv, grad_out, a_squares = scatter_high(
        total(after(ga0_own, tg_own), a_y0, a_x1), dp_rank, finish_a, table_grad, grad_up
    )

    first_row = side == 0
    tokens_grad = jnp.stack(
        [jnp.where(first_row, tg_own, tg_got), jnp.where(first_row, tg_got, tg_own)]
    )
    bias_part = jnp.zeros(position_bias.shape[::-1], f32)
    for index, shard in enumerate((rank, rank ^ 2)):
        bias_part = lax.dynamic_update_slice(
            bias_part, table_grad[index * heads : (index + 1) * heads, :32], (shard * heads, 0)
        )

    pool_part = after(pool_part, dqkvT0)
    pool_sums = pool_part + swap_core(pool_part)
    counts = jnp.sum((seg_row[None, :] == slot_ids[:, None]).astype(f32), axis=1)
    means = pool_sums / jnp.maximum(counts, 1.0)[:, None]
    mean_keep = lax.dynamic_slice_in_dim(means, rank * width, width, 1)
    mean_got = swap_x(lax.dynamic_slice_in_dim(means, (rank ^ 2) * width, width, 1))
    pooled = jnp.stack(
        [jnp.where(first_row, mean_keep, mean_got), jnp.where(first_row, mean_got, mean_keep)]
    )

    devices = dp_size * lax.axis_size("tensor")

    def from_all(value):
        spread = jnp.broadcast_to(value[None], (devices,) + value.shape)
        return lax.all_to_all(spread, ("dp", "tensor"), 0, 0, tiled=True)

    n_gain, n_bias = norm_gains.size, position_bias.size
    small = jnp.concatenate(
        [gain_grad_first[0], gain_grad_second[0], bias_part.reshape(-1)]
    )
    lanes = -(-small.shape[0] // 1024) * 1024
    small = jnp.pad(small, (0, lanes - small.shape[0])).reshape(lanes // 128, 128)
    small = jnp.sum(from_all(small), axis=0)
    small_squares = jnp.broadcast_to(jnp.sum(small * small), (8, 128))
    small = small.reshape(-1)
    grad_gains = small[:n_gain].reshape(norm_gains.shape)
    grad_biasT = small[n_gain : n_gain + n_bias].reshape(position_bias.shape[::-1])

    squares = from_all(a_squares + ud_squares)

    groups = (
        (qkv_master, grad_qkv, qkv_first, qkv_second),
        (out_master, grad_out, out_first, out_second),
        (up_master, grad_up, up_first, up_second),
        (down_master.T, grad_downT, down_first.T, down_second.T),
        (norm_gains, grad_gains, gain_first, gain_second),
        (position_bias.T, grad_biasT, bias_first.T, bias_second.T),
    )
    updates = call(
        adam_kernel,
        "adam",
        (),
        (after(small_squares, tokens_grad, pooled), squares, *(array for group in groups for array in group)),
        [sds(group[0].shape, f32) for group in groups for _ in range(2)] + [sds((8, 128), f32)],
        moved=6_000_000,
    )
    new_qkv, second_qkv, new_out, second_out, new_up, second_up = updates[0:6]
    new_gains, second_gains = updates[8:10]
    new_down, second_down, new_bias, second_bias = (updates[i].T for i in (6, 7, 10, 11))
    grad_down, grad_bias = grad_downT.T, grad_biasT.T
    gradient_norm = updates[12][0, 0]
    return (
        pooled,
        tokens_grad,
        grad_qkv,
        grad_out,
        grad_up,
        grad_down,
        grad_gains,
        grad_bias,
        gradient_norm,
        new_qkv,
        new_out,
        new_up,
        new_down,
        new_gains,
        new_bias,
        second_qkv,
        second_out,
        second_up,
        second_down,
        second_gains,
        second_bias,
    )


def solution(mesh):
    in_specs = (
        P("dp", "tensor", None),
        P("dp", None),
        P("dp", "tensor", None),
        P(None, "dp", "tensor"),
        P("tensor", "dp"),
        P("dp", "tensor"),
        P("tensor", "dp"),
        P(),
        P(),
        P(None, "dp", "tensor"),
        P(None, "dp", "tensor"),
        P("tensor", "dp"),
        P("tensor", "dp"),
        P("dp", "tensor"),
        P("dp", "tensor"),
        P("tensor", "dp"),
        P("tensor", "dp"),
        P(),
        P(),
        P(),
        P(),
    )
    out_specs = (
        P("dp", None, "tensor"),
        P("dp", "tensor", None),
        P(None, "dp", "tensor"),
        P("tensor", "dp"),
        P("dp", "tensor"),
        P("tensor", "dp"),
        P(),
        P(),
        P(),
        P(None, "dp", "tensor"),
        P("tensor", "dp"),
        P("dp", "tensor"),
        P("tensor", "dp"),
        P(),
        P(),
        P(None, "dp", "tensor"),
        P("tensor", "dp"),
        P("dp", "tensor"),
        P("tensor", "dp"),
        P(),
        P(),
    )
    return jax.shard_map(
        per_device, mesh=mesh, in_specs=in_specs, out_specs=out_specs, check_vma=False
    )
```

```python
import jax
import jax.numpy as jnp
from jax import lax
from jax.experimental import pallas as pl
from jax.experimental.pallas import tpu as pltpu
from jax.sharding import PartitionSpec as P

D = 768
H = 12
DH = 64
FF = 3072
SEGS = 16
STEP = 10

norm_eps = 1e-06
mask_fill = -1000000000.0
clip_level = 1.0
beta_first = 0.9
beta_second = 0.999
adam_eps = 1e-08
decay_rate = 0.1
gelu_scale = 0.7978845608028654
gelu_cubic = 0.044715

bf16 = jnp.bfloat16
f32 = jnp.float32
i32 = jnp.int32

QB = 256
KC = 128
EDGE = 128
NEAR = QB + 2 * EDGE
VMEM_LIMIT = 20 << 20
FULL_LIMIT = 60 << 20
FLOPS = 1000

SMEM_SPEC = pl.BlockSpec(memory_space=pltpu.SMEM)
VMEM_SPEC = pl.BlockSpec(memory_space=pltpu.VMEM)


def sds(shape, dtype):
    return jax.ShapeDtypeStruct(shape, dtype)


def nt(a, b):
    return lax.dot_general(a, b, (((1,), (1,)), ((), ())), preferred_element_type=f32)


def nn(a, b):
    return lax.dot_general(a, b, (((1,), (0,)), ((), ())), preferred_element_type=f32)


def call(body, name, smem, vmem, outs, scratch=(), gates=(), work=0, limit=VMEM_LIMIT):
    first, taken = len(smem) + len(vmem), len(gates)

    def gated(*refs):
        body(*refs[:first], *refs[first + taken :])

    return pl.pallas_call(
        gated if gates else body,
        out_shape=tuple(outs),
        in_specs=[SMEM_SPEC] * len(smem)
        + [VMEM_SPEC] * len(vmem)
        + [pl.BlockSpec(memory_space=pl.ANY)] * taken,
        out_specs=(VMEM_SPEC,) * len(outs),
        scratch_shapes=list(scratch),
        compiler_params=pltpu.CompilerParams(vmem_limit_bytes=limit),
        cost_estimate=pl.CostEstimate(
            flops=max(1, work) * FLOPS, bytes_accessed=FLOPS, transcendentals=0
        ),
        name=name,
    )(*smem, *vmem, *gates)


def bucket_of(offset):
    distance = jnp.abs(offset)
    large = 8 + sum(
        ((distance >= threshold).astype(jnp.int32) for threshold in (12, 16, 23, 32, 46, 64, 91))
    )
    inner_bucket = jnp.where(distance < 8, distance, large)
    return inner_bucket + jnp.where(offset > 0, 16, 0)


def learning_rates_plain():
    return (
        (2.0 * (D * DH) ** (-0.5), 2.0 * D ** (-0.5), 2.0 * D ** (-0.5)),
        0.5 * (H * DH / 16) ** (-0.5),
        0.5 * D ** (-0.5),
        2.0 * FF ** (-0.5),
        0.25,
        0.5,
    )


def adam_update(parameter, gradient, first_moment, second_moment, step_rate, clip_factor):
    clipped = gradient * clip_factor
    first_new = beta_first * first_moment + (1.0 - beta_first) * clipped
    second_new = beta_second * second_moment + (1.0 - beta_second) * clipped * clipped
    first_hat = first_new / (1.0 - beta_first**STEP)
    second_hat = second_new / (1.0 - beta_second**STEP)
    updated = parameter - step_rate * (
        first_hat / (jnp.sqrt(second_hat) + adam_eps) + decay_rate * parameter
    )
    return (updated, second_new)


def swap_core(value):
    return lax.ppermute(value, "tensor", [(i, i ^ 1) for i in range(lax.axis_size("tensor"))])


def swap_x(value):
    return lax.ppermute(value, "tensor", [(i, i ^ 2) for i in range(lax.axis_size("tensor"))])


def swap_dp(value, bits):
    return lax.ppermute(value, "dp", [(i, i ^ bits) for i in range(lax.axis_size("dp"))])


def swap_y(value):
    return swap_dp(value, 1)


def over_high(blocks):
    size = lax.axis_size("dp")
    groups = [[index for index in range(size) if index % 2 == bit] for bit in range(2)]
    return lax.all_to_all(blocks, "dp", 0, 0, tiled=True, axis_index_groups=groups)


def near_kernel(table_ref, own_ref, other_ref):
    heads = own_ref.shape[0]
    span = 2 * NEAR
    lane = lax.broadcasted_iota(i32, (8, span), 1)
    offset = -EDGE - jnp.where(lane < span // 2, lane, lane - span)
    buckets = bucket_of(offset)
    values = [jnp.where(offset > 0, table_ref[31, h], table_ref[15, h]) for h in range(2 * heads)]
    for bucket in list(range(15)) + list(range(17, 31)):
        here = buckets == bucket
        values = [jnp.where(here, table_ref[bucket, h], values[h]) for h in range(2 * heads)]
    for h in range(2 * heads):
        line = jnp.broadcast_to(values[h][0:1, :], (NEAR, span))
        tile = pltpu.roll(line, 0, 1, stride=1, stride_axis=0)[:, :QB]
        if h < heads:
            own_ref[h] = tile
        else:
            other_ref[h - heads] = tile


def rms_of(values):
    return lax.rsqrt(jnp.mean(values * values, axis=-1, keepdims=True) + norm_eps)


def blocks_of(own_ref, other_ref, kind):
    return (own_ref.at[kind, 0], own_ref.at[kind, 1], other_ref.at[kind, 0], other_ref.at[kind, 1])


def norm_kernel(place_ref, own_ref, other_ref, gain_ref, h_ref):
    length = own_ref.shape[2]
    for index, block in enumerate(blocks_of(own_ref, other_ref, 0)):
        start = pl.multiple_of(place_ref[index] * length, length)
        values = block[...].astype(f32)
        h_ref[pl.ds(start, length), :] = (values * rms_of(values) * gain_ref[0:1, :]).astype(bf16)


def place_weights(tab_ref, pieces, target, kind=None):
    index = 0
    for piece in pieces:
        rows = piece.shape[-2]
        for slot in range(piece.shape[0]):
            start = pl.multiple_of(tab_ref[index] * rows, 16)
            target[pl.ds(start, rows), :] = piece[slot] if kind is None else piece[slot, kind]
            index += 1


def split_rows(bit_ref, source, own_ref, other_ref):
    rows = own_ref.shape[1]
    bit = bit_ref[0]
    for block in range(own_ref.shape[0]):
        start = pl.multiple_of((2 * block + bit) * rows, 16)
        own_ref[block] = source[pl.ds(start, rows), :]
        start = pl.multiple_of((2 * block + 1 - bit) * rows, 16)
        other_ref[block] = source[pl.ds(start, rows), :]


def sub_sum(values):
    return jnp.sum(values.reshape(values.shape[0] // 8, 8, values.shape[1]), axis=0)


def sub_max(values):
    return jnp.max(values.reshape(values.shape[0] // 8, 8, values.shape[1]), axis=0)


def blocks_even(seq):
    return (seq // QB) % 2 == 0


def near_row(block, chunk):
    start = chunk * KC - block * QB + EDGE
    return start if 0 <= start and start + KC <= NEAR else None


def same_segment(segk_ref, keys, seg_query):
    seg_key = segk_ref[keys, :]
    return jnp.concatenate([seg_key] * (QB // seg_key.shape[1]), axis=1) == seg_query


def attend_kernel(
    flag_ref, far_ref, tab_ref, h_ref, piece_a_ref, piece_b_ref, near_ref, segk_ref, segq_ref,
    wT_ref, qkvT_ref, oT_ref, lse_ref, w_buf, k_buf, s_buf, p_buf,
):
    seq = h_ref.shape[0]
    heads = near_ref.shape[0]
    width = oT_ref.shape[0]
    size = width // heads
    chunks = seq // KC
    assert blocks_even(seq)
    place_weights(tab_ref, (piece_a_ref, piece_b_ref), w_buf)
    wT_ref[...] = w_buf[...].T
    qkvT_ref[...] = nt(wT_ref[0 : 3 * width, :], h_ref[...]).astype(bf16)
    blocks = seq // QB

    def rows(part, h):
        return pl.ds(pl.multiple_of(part * width + h * size, size), size)

    def score(h, block):
        s_buf[block % 2] = nn(k_buf[h % 2], qkvT_ref[rows(0, h), block * QB : (block + 1) * QB])

    def soften(h, block, masked):
        slot = block % 2
        qs = slice(block * QB, (block + 1) * QB)
        top = jnp.full((8, QB), -3e38, f32)
        for chunk in range(chunks):
            ks = slice(chunk * KC, (chunk + 1) * KC)
            row = near_row(block, chunk)
            if row is None:
                scores = s_buf[slot, ks, :] + far_ref[0 if chunk * KC < block * QB else 1, h]
            else:
                scores = s_buf[slot, ks, :] + near_ref[h, row : row + KC, :]
            if masked:
                scores = jnp.where(same_segment(segk_ref, ks, segq_ref[:, qs]), scores, mask_fill)
            s_buf[slot, ks, :] = scores
            top = jnp.maximum(top, sub_max(scores))
        top = jnp.max(top, axis=0, keepdims=True)
        total = jnp.zeros((8, QB), f32)
        for chunk in range(chunks):
            ks = slice(chunk * KC, (chunk + 1) * KC)
            exps = jnp.exp(s_buf[slot, ks, :] - top)
            s_buf[slot, ks, :] = exps
            total = total + sub_sum(exps)
        total = jnp.sum(total, axis=0, keepdims=True)
        scale = 1.0 / total
        for chunk in range(chunks):
            ks = slice(chunk * KC, (chunk + 1) * KC)
            p_buf[slot, ks, :] = (s_buf[slot, ks, :] * scale).astype(bf16)
        lse_ref[pl.ds(h, 1), qs] = top + jnp.log(total)

    def mix(h, block):
        qs = slice(block * QB, (block + 1) * QB)
        oT_ref[rows(0, h), qs] = nn(qkvT_ref[rows(2, h), :], p_buf[block % 2]).astype(bf16)

    def run(masked):
        k_buf[0] = qkvT_ref[rows(1, 0), :].T
        score(0, 0)

        def head(h, carried):
            for block in range(blocks):
                if block + 1 < blocks:
                    score(h, block + 1)
                else:
                    later = jnp.minimum(h + 1, heads - 1)
                    k_buf[(h + 1) % 2] = qkvT_ref[rows(1, later), :].T
                    s_buf[0] = nn(k_buf[(h + 1) % 2], qkvT_ref[rows(0, later), 0:QB])
                soften(h, block, masked)
                if block:
                    mix(h, block - 1)
            mix(h, blocks - 1)
            return carried

        lax.fori_loop(0, heads, head, 0)

    @pl.when(flag_ref[0] == 1)
    def _():
        run(False)

    @pl.when(flag_ref[0] != 1)
    def _():
        run(True)


def attend(flag, far, tab, h, pieces, near, segk, segq, gates):
    seq = h.shape[0]
    cols = pieces[0].shape[2]
    width = cols // 4
    return call(
        attend_kernel,
        "attend",
        (flag, far, tab),
        (h, *pieces, near, segk, segq),
        (sds((cols, D), bf16), sds((3 * width, seq), bf16), sds((width, seq), bf16), sds((8, seq), f32)),
        (
            pltpu.VMEM((D, cols), bf16),
            pltpu.VMEM((2, seq, width // near.shape[0]), bf16),
            pltpu.VMEM((2, seq, QB), f32),
            pltpu.VMEM((2, seq, QB), bf16),
        ),
        gates,
        work=10,
    )


def attend_back_kernel(
    flag_ref, far_ref, bit_ref, qkvT_ref, doT_ref, lse_ref, near_ref, segk_ref, segq_ref, h_ref, goT_ref,
    dqkvT_ref, own_ref, other_ref, dnear_ref, dfar_ref,
    kv_buf, s_buf, dp_buf, ds_buf, pt_buf, dt_buf, dk_buf, dv_buf, g_buf,
):
    width, seq = doT_ref.shape
    heads = near_ref.shape[0]
    size = width // heads
    blocks = seq // QB
    chunks = seq // KC
    assert blocks_even(seq)

    def rows(part, h):
        return pl.ds(pl.multiple_of(part * width + h * size, size), size)

    def key_values(h, turn):
        kv_buf[turn] = jnp.concatenate([qkvT_ref[rows(1, h), :], qkvT_ref[rows(2, h), :]], axis=0).T

    def products(h, turn, block):
        slot = block % 2
        qs = slice(block * QB, (block + 1) * QB)
        zeros = jnp.zeros((size, QB), bf16)
        s_buf[slot] = nn(kv_buf[turn], jnp.concatenate([qkvT_ref[rows(0, h), qs], zeros], axis=0))
        dp_buf[slot] = nn(kv_buf[turn], jnp.concatenate([zeros, doT_ref[rows(0, h), qs]], axis=0))

    def soften(h, block, masked):
        slot = block % 2
        qs = slice(block * QB, (block + 1) * QB)
        lse = lse_ref[pl.ds(h, 1), qs]
        lse_left = lse - far_ref[0, h]
        lse_right = lse - far_ref[1, h]
        dots = jnp.zeros((8, QB), f32)
        for chunk in range(chunks):
            ks = slice(chunk * KC, (chunk + 1) * KC)
            row = near_row(block, chunk)
            if row is None:
                scores = s_buf[slot, ks, :] - (lse_left if chunk * KC < block * QB else lse_right)
            else:
                scores = s_buf[slot, ks, :] + near_ref[h, row : row + KC, :] - lse
            probs = jnp.exp(scores)
            if masked:
                probs = jnp.where(same_segment(segk_ref, ks, segq_ref[:, qs]), probs, 0.0)
            s_buf[slot, ks, :] = probs
            pt_buf[slot, :, ks] = probs.astype(bf16).T
            dots = dots + sub_sum(probs * dp_buf[slot, ks, :])
        dots = jnp.sum(dots, axis=0, keepdims=True)
        for chunk in range(chunks):
            ks = slice(chunk * KC, (chunk + 1) * KC)
            d_scores = (s_buf[slot, ks, :] * (dp_buf[slot, ks, :] - dots)).astype(bf16)
            ds_buf[slot, ks, :] = d_scores
            dt_buf[slot, :, ks] = d_scores.T
            row = near_row(block, chunk)
            if row is not None:
                if block == 0 or (block == 1 and row == 0):
                    dnear_ref[h, row : row + KC, :] = d_scores.astype(f32)
                else:
                    dnear_ref[h, row : row + KC, :] += d_scores.astype(f32)

    def outputs(h, block):
        slot = block % 2
        qs = slice(block * QB, (block + 1) * QB)
        dqkvT_ref[rows(0, h), qs] = nn(qkvT_ref[rows(1, h), :], ds_buf[slot]).astype(bf16)
        d_keys = nn(
            jnp.concatenate([qkvT_ref[rows(0, h), qs], jnp.ones((16, QB), bf16)], axis=0),
            dt_buf[slot],
        )
        d_values = nn(doT_ref[rows(0, h), qs], pt_buf[slot])
        if block == 0:
            dk_buf[...] = d_keys[0:size]
            dv_buf[...] = d_values
        elif block + 1 < blocks:
            dk_buf[...] += d_keys[0:size]
            dv_buf[...] += d_values
        else:
            dqkvT_ref[rows(1, h), :] = (dk_buf[...] + d_keys[0:size]).astype(bf16)
            dqkvT_ref[rows(2, h), :] = (dv_buf[...] + d_values).astype(bf16)
        sums = d_keys[size : size + 1]
        left_end = max(0, block * QB - EDGE)
        right_start = min(seq, block * QB + QB + EDGE)
        lane = lax.broadcasted_iota(i32, (1, 128), 1)
        line = jnp.zeros((1, 128), f32)
        if left_end:
            line = jnp.where(lane == 0, jnp.sum(sums[:, :left_end], axis=1, keepdims=True), line)
        if right_start < seq:
            line = jnp.where(lane == 1, jnp.sum(sums[:, right_start:], axis=1, keepdims=True), line)
        if block == 0:
            dfar_ref[pl.ds(h, 1), :] = line
        else:
            dfar_ref[pl.ds(h, 1), :] += line

    def run(masked):
        key_values(0, 0)
        products(0, 0, 0)

        def head(h, carried):
            for block in range(blocks):
                if block + 1 < blocks:
                    products(h, h % 2, block + 1)
                else:
                    later = jnp.minimum(h + 1, heads - 1)
                    key_values(later, (h + 1) % 2)
                    products(later, (h + 1) % 2, 0)
                soften(h, block, masked)
                if block:
                    outputs(h, block - 1)
            outputs(h, blocks - 1)
            return carried

        lax.fori_loop(0, heads, head, 0)

    @pl.when(flag_ref[0] == 1)
    def _():
        run(False)

    @pl.when(flag_ref[0] != 1)
    def _():
        run(True)

    grad = jnp.concatenate([nn(dqkvT_ref[...], h_ref[...]).astype(bf16), goT_ref[...]], axis=0)
    if other_ref is None:
        own_ref[...] = grad.T
    else:
        g_buf[...] = grad.T
        split_rows(bit_ref, g_buf, own_ref, other_ref)


def attend_back(flag, far, bit, qkvT, doT, lse, near, segk, segq, h, goT, grad_outs, gates):
    width, seq = doT.shape
    size = width // near.shape[0]
    body = attend_back_kernel
    if len(grad_outs) == 1:

        def body(*refs):
            attend_back_kernel(*refs[:13], None, *refs[13:])

    return call(
        body,
        "attend_back",
        (flag, far, bit),
        (qkvT, doT, lse, near, segk, segq, h, goT),
        (sds(qkvT.shape, bf16), *grad_outs, sds(near.shape, f32), sds((8, 128), f32)),
        (
            pltpu.VMEM((2, seq, 2 * size), bf16),
            pltpu.VMEM((2, seq, QB), f32),
            pltpu.VMEM((2, seq, QB), f32),
            pltpu.VMEM((2, seq, QB), bf16),
            pltpu.VMEM((2, QB, seq), bf16),
            pltpu.VMEM((2, QB, seq), bf16),
            pltpu.VMEM((size, seq), f32),
            pltpu.VMEM((size, seq), f32),
            pltpu.VMEM((D, 4 * width), bf16),
        ),
        gates,
        work=13,
    )


def project_kernel(place_ref, oT0_ref, oT1_ref, wT0_ref, wT1_ref, keep_ref, send_ref, o_buf):
    width = oT0_ref.shape[0]
    length = keep_ref.shape[0] // 2
    o_buf[...] = jnp.concatenate([oT0_ref[...], oT1_ref[...]], axis=0).T
    w = jnp.concatenate([wT0_ref[3 * width :, :], wT1_ref[3 * width :, :]], axis=0)
    for index in range(4):
        start = pl.multiple_of(place_ref[index] * length, length)
        part = nn(o_buf[pl.ds(start, length), :], w)
        rows = slice((index % 2) * length, (index % 2 + 1) * length)
        if index < 2:
            keep_ref[rows, :] = part
        else:
            send_ref[rows, :] = part.astype(send_ref.dtype)


def middle_kernel(own_ref, part_ref, got_ref, gain_ref, x2_ref, h_ref):
    length = own_ref.shape[2]
    for index, block in enumerate((own_ref.at[0, 0], own_ref.at[0, 1])):
        rows = slice(index * length, (index + 1) * length)
        values = block[...].astype(f32) + part_ref[rows, :] + got_ref[rows, :].astype(f32)
        x2_ref[rows, :] = values
        h_ref[rows, :] = (values * rms_of(values) * gain_ref[1:2, :]).astype(bf16)


def split3(values):
    high = values.astype(bf16)
    rest = values - high.astype(f32)
    mid = rest.astype(bf16)
    low = (rest - mid.astype(f32)).astype(bf16)
    return high, mid, low


def feed_rows(h, cot, u_buf, d_buf, act_ref, dpre_ref, rows):
    pre = nn(h, u_buf[...])
    d_act = nn(cot, d_buf[...])
    square = pre * pre
    bent = jnp.tanh(gelu_scale * pre * (1.0 + gelu_cubic * square))
    half_up = 0.5 * (1.0 + bent)
    act_ref[rows, :] = (pre * half_up).astype(bf16)
    slope = half_up + (0.5 * gelu_scale) * pre * (1.0 - bent * bent) * (
        1.0 + (3.0 * gelu_cubic) * square
    )
    d_pre = (d_act * slope).astype(bf16)
    dpre_ref[rows, :] = d_pre
    return nt(d_pre, u_buf[...])


def pooled_units(hot, act_ref, d_buf):
    pooled = None
    for term in split3(nn(hot, act_ref[...])):
        part = nt(term, d_buf[...])
        pooled = part if pooled is None else pooled + part
    return pooled


def feed_own_kernel(
    tab_ref, h_own_ref, h_oth_ref, own_ref, oth_ref,
    a_ref, b_ref, hot_ref, x2_ref,
    act_ref, dpre_ref, dh_ref, pooled_ref, u_buf, d_buf,
):
    place_weights(tab_ref, (a_ref, b_ref), u_buf, 0)
    place_weights(tab_ref, (a_ref, b_ref), d_buf, 1)
    length = own_ref.shape[2]
    cots = blocks_of(own_ref, oth_ref, 1)
    for index in range(4):
        rows = slice(index * length, (index + 1) * length)
        half = slice((index % 2) * length, (index % 2 + 1) * length)
        h = (h_own_ref if index < 2 else h_oth_ref)[half, :]
        dh_ref[rows, :] = feed_rows(h, cots[index][...], u_buf, d_buf, act_ref, dpre_ref, rows)
    hot = hot_ref[...]
    pooled = pooled_units(hot, act_ref, d_buf)
    for term in split3(x2_ref[...]):
        pooled = pooled + nn(hot[:, 0 : 2 * length], term)
    pooled_ref[...] = pooled


def feed_other_kernel(
    tab_ref, h_own_ref, h_oth_ref, own_ref, oth_ref,
    ua_ref, ub_ref, db_ref, hot_ref, dh_ref, pool_ref,
    act_ref, dpre_ref, keep_ref, send_ref, pooled_ref, u_buf, d_buf,
):
    place_weights(tab_ref, (ua_ref,), u_buf, 0)
    place_weights(tab_ref, (ua_ref,), d_buf, 1)
    for source, target in ((ub_ref, u_buf), (db_ref, d_buf)):
        first = ua_ref.shape[0]
        rows = source.shape[1]
        for slot in range(source.shape[0]):
            start = pl.multiple_of(tab_ref[first + slot] * rows, 16)
            target[pl.ds(start, rows), :] = source[slot]
    length = own_ref.shape[2]
    cots = blocks_of(own_ref, oth_ref, 1)
    for index in (2, 3, 0, 1):
        rows = slice(index * length, (index + 1) * length)
        half = slice((index % 2) * length, (index % 2 + 1) * length)
        h = (h_own_ref if index < 2 else h_oth_ref)[half, :]
        total = dh_ref[rows, :] + feed_rows(
            h, cots[index][...], u_buf, d_buf, act_ref, dpre_ref, rows
        )
        if index < 2:
            keep_ref[half, :] = total
        else:
            send_ref[half, :] = total.astype(send_ref.dtype)
    pooled_ref[...] = pool_ref[...] + pooled_units(hot_ref[...], act_ref, d_buf)


def weight_grad_kernel(
    bit_ref, h_own_ref, h_oth_ref, own_ref, oth_ref, act_ref, dpre_ref, *refs
):
    *outs, g_buf = refs
    hT = jnp.concatenate([h_own_ref[...], h_oth_ref[...]], axis=0).T
    cotT = jnp.concatenate([block[...] for block in blocks_of(own_ref, oth_ref, 1)], axis=0).T
    if len(outs) == 2:
        outs[0][...] = nn(hT, dpre_ref[...]).astype(bf16)
        outs[1][...] = nn(cotT, act_ref[...]).astype(bf16)
    else:
        g_buf[0] = nn(hT, dpre_ref[...]).astype(bf16)
        split_rows(bit_ref, g_buf.at[0], outs[0], outs[1])
        g_buf[1] = nn(cotT, act_ref[...]).astype(bf16)
        split_rows(bit_ref, g_buf.at[1], outs[2], outs[3])


def norm_back(values, gain, upstream):
    scale = rms_of(values)
    normed = values * scale
    gain_grad = jnp.sum(upstream * normed, axis=0, keepdims=True)
    scaled = upstream * gain
    inner = jnp.mean(scaled * normed, axis=-1, keepdims=True)
    return scale * (scaled - normed * inner), gain_grad


def middle_back_kernel(
    x2_ref, part_ref, got_ref, own_ref, gain_ref, dx2_ref, da_ref, gain_grad_ref
):
    length = x2_ref.shape[0] // 2
    for index, cot in enumerate((own_ref.at[1, 0], own_ref.at[1, 1])):
        rows = slice(index * length, (index + 1) * length)
        d_values, gain_grad = norm_back(
            x2_ref[rows, :], gain_ref[1:2, :], part_ref[rows, :] + got_ref[rows, :].astype(f32)
        )
        dx2 = cot[...].astype(f32) + d_values
        dx2_ref[rows, :] = dx2
        da_ref[rows, :] = dx2.astype(bf16)
        if index == 0:
            gain_grad_ref[...] = gain_grad
        else:
            gain_grad_ref[...] += gain_grad


def branch_back_kernel(
    place_ref, da_own_ref, da_oth_ref, wT0_ref, wT1_ref, oT0_ref, oT1_ref,
    doT0_ref, doT1_ref, g0_ref, g1_ref, da_buf,
):
    width = oT0_ref.shape[0]
    length = da_own_ref.shape[0] // 2
    for index in range(4):
        start = pl.multiple_of(place_ref[index] * length, length)
        half = slice((index % 2) * length, (index % 2 + 1) * length)
        da_buf[pl.ds(start, length), :] = (da_own_ref if index < 2 else da_oth_ref)[half, :]
    da = da_buf[...]
    doT0_ref[...] = nt(wT0_ref[3 * width :, :], da).astype(bf16)
    doT1_ref[...] = nt(wT1_ref[3 * width :, :], da).astype(bf16)
    g0_ref[...] = nn(oT0_ref[...], da).astype(bf16)
    g1_ref[...] = nn(oT1_ref[...], da).astype(bf16)


def first_back_kernel(place_ref, d0_ref, d1_ref, wT0_ref, wT1_ref, keep_ref, send_ref, d_buf):
    rows3 = d0_ref.shape[0]
    length = keep_ref.shape[0] // 2
    d_buf[...] = jnp.concatenate([d0_ref[...], d1_ref[...]], axis=0).T
    w = jnp.concatenate([wT0_ref[0:rows3, :], wT1_ref[0:rows3, :]], axis=0)
    for index in (2, 3, 0, 1):
        start = pl.multiple_of(place_ref[index] * length, length)
        part = nn(d_buf[pl.ds(start, length), :], w)
        rows = slice((index % 2) * length, (index % 2 + 1) * length)
        if index < 2:
            keep_ref[rows, :] = part
        else:
            send_ref[rows, :] = part.astype(send_ref.dtype)


def token_grad_kernel(
    rows_ref, part_ref, got_ref, dx2_ref, gain_ref, mean_ref, own_ref, away_ref, gain_grad_ref
):
    length = rows_ref.shape[2]
    away_ref[length:, :] = jnp.zeros((away_ref.shape[0] - length, away_ref.shape[1]), f32)
    away_ref[length:, 0 : mean_ref.shape[1]] = mean_ref[...]
    for index, block in enumerate((rows_ref.at[0, 0], rows_ref.at[0, 1])):
        rows = slice(index * length, (index + 1) * length)
        d_values, gain_grad = norm_back(
            block[...].astype(f32), gain_ref[0:1, :], part_ref[rows, :] + got_ref[rows, :].astype(f32)
        )
        if index == 0:
            own_ref[...] = dx2_ref[rows, :] + d_values
            gain_grad_ref[...] = gain_grad
        else:
            away_ref[0:length, :] = dx2_ref[rows, :] + d_values
            gain_grad_ref[...] += gain_grad


def bias_grad_kernel(dnear0_ref, dnear1_ref, dfar0_ref, dfar1_ref, grad_ref, line_buf):
    heads = dnear0_ref.shape[0]
    span = 2 * NEAR
    line_buf[...] = jnp.zeros_like(line_buf)
    for side, dnear_ref in enumerate((dnear0_ref, dnear1_ref)):
        for h in range(heads):
            values = dnear_ref[h]
            left = NEAR
            rows = NEAR
            while rows > 8:
                rows //= 2
                low, high = values[:rows], values[rows:]
                if rows % 128 == 0:
                    pad = jnp.zeros((rows, rows), f32)
                    values = jnp.concatenate([pad, low], axis=1) + jnp.concatenate([high, pad], axis=1)
                    left -= rows
                else:
                    if values.shape[1] < span:
                        missing = span - values.shape[1]
                        pad = jnp.zeros((rows, missing), f32)
                        low = jnp.concatenate([pad, low], axis=1)
                        high = jnp.concatenate([pad, high], axis=1)
                        left -= missing
                    values = low + pltpu.roll(high, span - rows, 1)
            while rows > 1:
                rows //= 2
                values = values[:rows] + pltpu.roll(values[rows:], span - rows, 1)
            index = side * heads + h
            line_buf[index : index + 1, :] = values
    lines = line_buf[...]
    shift = span - QB
    col = lax.broadcasted_iota(i32, lines.shape, 1)
    buckets = bucket_of(shift - EDGE - col)
    lane = lax.broadcasted_iota(i32, (8, 128), 1)
    grad = jnp.zeros((8, 128), f32)
    for bucket in range(32):
        if bucket != 16:
            total = jnp.sum(jnp.where(buckets == bucket, lines, 0.0), axis=1, keepdims=True)
            grad = jnp.where(lane == bucket, total, grad)
    grad_ref[...] = grad
    for side, dfar_ref in enumerate((dfar0_ref, dfar1_ref)):
        far = dfar_ref[0:heads, :]
        lane = lax.broadcasted_iota(i32, far.shape, 1)
        left = jnp.sum(jnp.where(lane == 0, far, 0.0), axis=1, keepdims=True)
        right = jnp.sum(jnp.where(lane == 1, far, 0.0), axis=1, keepdims=True)
        grad_ref[side * heads : (side + 1) * heads, :] += jnp.where(
            lane == 15, left, jnp.where(lane == 31, right, 0.0)
        )


def pack_kernel(side_ref, qkv_ref, out_ref, tokens_ref, cot_ref, pack_ref, keep_ref, send_ref):
    packed = jnp.concatenate([qkv_ref[0], qkv_ref[1], qkv_ref[2], out_ref[...].T], axis=1).astype(bf16)
    for slot in range(pack_ref.shape[0]):
        pack_ref[slot] = packed
    rows_kernel(side_ref, tokens_ref, cot_ref, keep_ref, send_ref)


def pack_ud_kernel(up_ref, down_ref, pack_ref):
    up, down = up_ref[...].astype(bf16), down_ref[...].astype(bf16)
    for slot in range(pack_ref.shape[0]):
        pack_ref[slot, 0] = up
        pack_ref[slot, 1] = down


def rows_kernel(side_ref, tokens_ref, cot_ref, keep_ref, send_ref):
    side = side_ref[0]
    keep_ref[0] = tokens_ref[side]
    keep_ref[1] = cot_ref[side]
    send_ref[0] = tokens_ref[1 - side]
    send_ref[1] = cot_ref[1 - side]


def join_kernel(keep_ref, got_ref, both_ref):
    both_ref[:, 0] = keep_ref[...]
    both_ref[:, 1] = got_ref[...]


def place_kernel(side_ref, own_ref, got_ref, mean_ref, out_ref, pooled_ref):
    side = side_ref[0]
    length, width = own_ref.shape[0], mean_ref.shape[1]
    out_ref[side] = own_ref[...]
    out_ref[1 - side] = got_ref[0:length, :]
    pooled_ref[side] = mean_ref[...]
    pooled_ref[1 - side] = got_ref[length:, 0:width]


def pick_kernel(from_x_ref, from_y_ref, up_ref, down_ref):
    up_ref[...] = from_x_ref[:, 0]
    down_ref[...] = from_y_ref[:, 1]


def total_of(refs):
    total = refs[0][...].astype(f32)
    for ref in refs[1:]:
        total = total + ref[...].astype(f32)
    return total


def add_kernel(*refs):
    refs[-1][...] = total_of(refs[:-1]).astype(bf16)


def add_pairs_kernel(up_ref, up_got_ref, down_ref, down_got_ref, pass_ref, up_sum_ref, down_sum_ref, passed_ref):
    up_sum_ref[...] = total_of((up_ref, up_got_ref)).astype(bf16)
    down_sum_ref[...] = total_of((down_ref, down_got_ref)).astype(bf16)
    passed_ref[...] = pass_ref[...]


def sum_blocks(ref):
    total = ref[0].astype(f32)
    for slot in range(1, ref.shape[0]):
        total = total + ref[slot].astype(f32)
    return total


def finish_kernel(blocks_ref, grad_ref, squares_ref):
    total = sum_blocks(blocks_ref)
    grad_ref[...] = total
    squares_ref[...] = jnp.broadcast_to(jnp.sum(total * total, axis=(0, 1), keepdims=True), (8, 128))


def finish_a_kernel(blocks_ref, up_ref, down_ref, qkv_ref, out_ref, squares_ref):
    total = sum_blocks(blocks_ref)
    width = qkv_ref.shape[2]
    for part in range(3):
        qkv_ref[part] = total[:, part * width : (part + 1) * width]
    out_ref[...] = total[:, 3 * width :].T
    squares = up_ref[...] + down_ref[...] + jnp.sum(total * total, axis=(0, 1), keepdims=True)
    for slot in range(squares_ref.shape[0]):
        squares_ref[slot] = squares


def adam_kernel(small_ref, squares_ref, *refs):
    *refs, sems = refs
    sources, refs = refs[:24], refs[24:]
    outs, refs = refs[:13], refs[13:]
    copies = [
        pltpu.make_async_copy(source, target, sems.at[index])
        for index, (source, target) in enumerate(zip(sources, refs))
    ]
    for copy in copies:
        copy.start()
    for copy in copies:
        copy.wait()
    total = jnp.sum(squares_ref[...], axis=0)[0:1, 0:1]
    small = small_ref[...]
    norm = jnp.sqrt(total + jnp.sum(small * small, axis=(0, 1), keepdims=True))
    clip = jnp.minimum(1.0, clip_level / norm)
    count = 6
    rates = learning_rates_plain()
    for index in range(count):
        param, grad, first, second = (refs[4 * index + k] for k in range(4))
        new, new_second = outs[2 * index], outs[2 * index + 1]
        if isinstance(rates[index], tuple):
            for part, rate in enumerate(rates[index]):
                value, moment = adam_update(
                    param[part], grad[part], first[part], second[part], rate, clip
                )
                new[part] = value
                new_second[part] = moment
        else:
            value, moment = adam_update(
                param[...], grad[...], first[...], second[...], rates[index], clip
            )
            new[...] = value
            new_second[...] = moment
    outs[2 * count][0, 0] = jnp.max(norm)


def per_device(
    tokens,
    segment_ids,
    cotangent,
    qkv_master,
    out_master,
    up_master,
    down_master,
    norm_gains,
    position_bias,
    qkv_first,
    qkv_second,
    out_first,
    out_second,
    up_first,
    up_second,
    down_first,
    down_second,
    gain_first,
    gain_second,
    bias_first,
    bias_second,
):
    rank = lax.axis_index("tensor")
    dp_rank = lax.axis_index("dp")
    dp_size = lax.axis_size("dp")
    side = rank // 2
    row_bit = dp_rank % 2
    rows, length = tokens.shape[0], tokens.shape[1]
    seq = segment_ids.shape[1]
    shard_rows, width = qkv_master.shape[1], qkv_master.shape[2]
    units = up_master.shape[1]
    heads = position_bias.shape[1] // lax.axis_size("tensor")
    half = (seq // 2, D)
    assert rows == 2 and lax.axis_size("tensor") == 4 and seq == 4 * length
    pick = lambda value, index: lax.dynamic_index_in_dim(value, index, 0, keepdims=False)

    places = jnp.stack([rank, rank ^ 2, rank ^ 1, rank ^ 3]).astype(i32)
    side_at = side.astype(i32).reshape(1)
    bit = row_bit.astype(i32).reshape(1)
    high = dp_size // 2
    aligned = shard_rows % 16 == 0

    if aligned:
        pack_a, own_rows, sent_rows = call(
            pack_kernel,
            "pack_a",
            (side_at,),
            (qkv_master, out_master, tokens, cotangent),
            (sds((high, shard_rows, D), bf16),) + (sds((2, length, D), bf16),) * 2,
            limit=FULL_LIMIT,
        )
        tab = jnp.concatenate(
            [2 * jnp.arange(high, dtype=i32) + row_bit, 2 * jnp.arange(high, dtype=i32) + 1 - row_bit]
        ).astype(i32)
        order = lambda pair: pair
        blocks_out = (sds((high, shard_rows, D), bf16),) * 2
    else:
        packed = jnp.concatenate([*qkv_master, out_master.T], axis=1).astype(bf16)
        pack_a = jnp.broadcast_to(packed, (high,) + packed.shape)
        tab = jnp.arange(2, dtype=i32)
        blocks_out = (sds((D, D), bf16),)
        own_rows, sent_rows = call(
            rows_kernel, "rows", (side_at,), (tokens, cotangent), (sds((2, length, D), bf16),) * 2
        )

        def order(pair):
            own, other = pair
            first = jnp.where(row_bit == 0, own, other)
            second = jnp.where(row_bit == 0, other, own)
            both = jnp.moveaxis(jnp.stack([first, second], axis=1), (0, 1), (-4, -3))
            both = both.reshape(both.shape[:-4] + (D, both.shape[-1]))
            both = jnp.stack([both[..., : D // 2, :], both[..., D // 2 :, :]])[:, None]
            return both[0], both[1]

    high_a = over_high(pack_a)
    got_rows = swap_x(sent_rows)
    tables = [
        lax.dynamic_slice_in_dim(position_bias, shard * heads, heads, 1)
        for shard in (rank, rank ^ 2)
    ]
    fars = [jnp.stack([table[15], table[31]]) for table in tables]
    near0, near1 = call(
        near_kernel,
        "bias_tiles",
        (jnp.concatenate(tables, axis=1),),
        (),
        (sds((heads, NEAR, QB), f32),) * 2,
    )
    a_y = swap_y(high_a)
    a_x = swap_x(high_a)
    (pack_ud,) = call(
        pack_ud_kernel,
        "pack_ud",
        (),
        (up_master, down_master.T),
        (sds((high, 2, shard_rows, units), bf16),),
        gates=(high_a,),
    )
    high_ud = over_high(pack_ud)
    (own_both,) = call(
        join_kernel, "join_rows", (), (own_rows, got_rows), (sds((2, 2, length, D), bf16),)
    )
    other_both = swap_core(own_both)

    seg_row = pick(segment_ids, side)
    flag = (seg_row[0] == seg_row[seq - 1]).astype(i32).reshape(1)
    segk = jnp.broadcast_to(seg_row[:, None], (seq, 128))
    segq = seg_row[None, :]
    slot_ids = jnp.arange(SEGS, dtype=i32)
    seg_blocks = seg_row.reshape(4, length)
    seg_rel = jnp.concatenate([pick(seg_blocks, rank ^ bits) for bits in (0, 2, 1, 3)])
    hot = (seg_rel[None, :] == slot_ids[:, None]).astype(bf16)
    (h1,) = call(
        norm_kernel,
        "first_norm",
        (places,),
        (own_both, other_both, norm_gains),
        (sds((seq, D), bf16),),
    )
    a_other = (a_x, swap_y(a_x))
    wT0, qkvT0, oT0, lse0 = attend(
        flag, fars[0], tab, h1, order((high_a, a_y)), near0, segk, segq, ()
    )
    ud_x = swap_x(high_ud)
    ud_y = swap_y(high_ud)
    wT1, qkvT1, oT1, lse1 = attend(
        flag, fars[1], tab, h1, order(a_other), near1, segk, segq, ()
    )

    keep, send = call(
        project_kernel,
        "project",
        (places,),
        (oT0, oT1, wT0, wT1),
        (sds(half, f32), sds(half, bf16)),
        (pltpu.VMEM((seq, 2 * width), bf16),),
    )
    x2, h2 = call(
        middle_kernel,
        "second_norm",
        (),
        (own_both, keep, swap_core(send), norm_gains),
        (sds(half, f32), sds(half, bf16)),
    )
    h2_other = swap_core(h2)
    picked_u, picked_d = call(
        pick_kernel,
        "pick_ud",
        (),
        (ud_x, ud_y),
        (sds((high, shard_rows, units), bf16),) * 2,
        gates=(h2,),
    )
    u_xy = swap_y(picked_u)
    d_xy = swap_x(picked_d)
    act0, d_pre0, dh_part, pool_part = call(
        feed_own_kernel,
        "feed_own",
        (tab,),
        (h2, h2_other, own_both, other_both, *order((high_ud, ud_y)), hot, x2),
        (
            sds((seq, units), bf16),
            sds((seq, units), bf16),
            sds((seq, D), f32),
            sds((SEGS, D), f32),
        ),
        [pltpu.VMEM((D, units), bf16)] * 2,
        work=8,
    )

    def weight_grads(act, d_pre, name):
        return call(
            weight_grad_kernel,
            name,
            (bit,),
            (h2, h2_other, own_both, other_both, act, d_pre),
            blocks_out * 2,
            (pltpu.VMEM((2, D, units), bf16),),
            work=4,
        )

    def of_y(grad, wanted):
        blocks = grad.reshape((high, 2, shard_rows) + grad.shape[1:])
        return lax.dynamic_index_in_dim(blocks, wanted, 1, keepdims=False)

    def by_y(grads):
        if aligned:
            return tuple(grads)
        return tuple(of_y(grad, wanted) for grad in grads for wanted in (row_bit, 1 - row_bit))

    def plus(name, *terms, gates=()):
        return call(add_kernel, name, (), terms, (sds(terms[0].shape, bf16),), gates=gates)[0]

    gu0_own, gu0_oth, gd0_own, gd0_oth = by_y(weight_grads(act0, d_pre0, "feed_grads_own"))
    up_y0 = swap_y(gu0_oth)
    if aligned:
        ud_other = (ud_x, u_xy, d_xy)
    else:
        first, second = order((ud_x, jnp.stack([u_xy, d_xy], axis=1)))
        ud_other = (first, second[:, 0], second[:, 1])
    act1, d_pre1, keep, send, pool_part = call(
        feed_other_kernel,
        "feed_other",
        (tab,),
        (h2, h2_other, own_both, other_both, *ud_other, hot, dh_part, pool_part),
        (
            sds((seq, units), bf16),
            sds((seq, units), bf16),
            sds(half, f32),
            sds(half, bf16),
            sds((SEGS, D), f32),
        ),
        [pltpu.VMEM((D, units), bf16)] * 2,
        work=8,
    )
    got = swap_core(send)
    gu1_own, gu1_oth, gd1_own, gd1_oth = by_y(weight_grads(act1, d_pre1, "feed_grads_other"))
    up_y1 = swap_y(gu1_oth)
    down_x1 = swap_x(gd1_oth)
    dx2, da, gain_grad_second = call(
        middle_back_kernel,
        "second_norm_back",
        (),
        (x2, keep, got, own_both, norm_gains),
        (sds(half, f32), sds(half, bf16), sds((1, D), f32)),
    )
    da_other = swap_core(da)
    doT0, doT1, goT0, goT1 = call(
        branch_back_kernel,
        "branch_back",
        (places,),
        (da, da_other, wT0, wT1, oT0, oT1),
        (sds((width, seq), bf16),) * 2 + (sds((width, D), bf16),) * 2,
        (pltpu.VMEM((seq, D), bf16),),
    )
    up_add, down_add, down_own = call(
        add_pairs_kernel,
        "add_ud",
        (),
        (gu1_own, up_y1, gd0_oth, down_x1, gd1_own),
        (sds(gu1_own.shape, bf16),) * 3,
        gates=(doT0,),
    )
    up_x = swap_x(up_add)
    down_y = swap_y(down_add)
    down_x0 = swap_x(down_own)
    dqkvT1, *ga1, dnear1, dfar1 = attend_back(
        flag, fars[1], bit, qkvT1, doT1, lse1, near1, segk, segq, h1, goT1, blocks_out, ()
    )
    ga1_own, ga1_oth = by_y(ga1)
    a_y1 = swap_y(ga1_oth)
    up_total = plus("total_up", gu0_own, up_y0, up_x, gates=(dfar1,))
    up_blocks = over_high(up_total)
    dqkvT0, *ga0, dnear0, dfar0 = attend_back(
        flag, fars[0], bit, qkvT0, doT0, lse0, near0, segk, segq, h1, goT0, blocks_out, ()
    )
    ga0_own, ga0_oth = by_y(ga0)
    a_y0 = swap_y(ga0_oth)
    a_add = plus("add_a", ga1_own, a_y1, gates=(dfar0,))
    a_x1 = swap_x(a_add)
    keep, send = call(
        first_back_kernel,
        "first_back",
        (places,),
        (dqkvT0, dqkvT1, wT0, wT1),
        (sds(half, f32), sds(half, bf16)),
        (pltpu.VMEM((seq, 6 * width), bf16),),
    )
    first_got = swap_core(send)
    down_total = plus("total_down", gd0_own, down_x0, down_y, gates=(dfar0,))
    down_blocks = over_high(down_total)
    (table_grad,) = call(
        bias_grad_kernel,
        "bias_grad",
        (),
        (dnear0, dnear1, dfar0, dfar1),
        (sds((8, 128), f32),),
        (pltpu.VMEM((8, 2 * NEAR), f32),),
    )

    pool_sums = pool_part + swap_core(pool_part)
    counts = jnp.sum((seg_row[None, :] == slot_ids[:, None]).astype(f32), axis=1)
    means = pool_sums / jnp.maximum(counts, 1.0)[:, None]
    mean_keep = lax.dynamic_slice_in_dim(means, rank * width, width, 1)
    mean_send = lax.dynamic_slice_in_dim(means, (rank ^ 2) * width, width, 1)

    tg_own, tg_away, gain_grad_first = call(
        token_grad_kernel,
        "first_norm_back",
        (),
        (own_both, keep, first_got, dx2, norm_gains, mean_send),
        (sds((length, D), f32), sds((length + SEGS, D), f32), sds((1, D), f32)),
    )
    tg_got = swap_x(tg_away)
    a_total = plus("total_a", ga0_own, a_y0, a_x1, gates=(gain_grad_first,))
    a_blocks = over_high(a_total)
    grad_up, up_squares = call(
        finish_kernel,
        "finish_up",
        (),
        (up_blocks,),
        (sds((shard_rows, units), f32), sds((8, 128), f32)),
        gates=(gain_grad_first,),
    )
    grad_downT, down_squares = call(
        finish_kernel,
        "finish_down",
        (),
        (down_blocks,),
        (sds((shard_rows, units), f32), sds((8, 128), f32)),
        gates=(gain_grad_first,),
    )
    devices = dp_size * lax.axis_size("tensor")
    if aligned:
        grad_qkv, grad_out, squares = call(
            finish_a_kernel,
            "finish_a",
            (),
            (a_blocks, up_squares, down_squares),
            (sds(qkv_master.shape, f32), sds(out_master.shape, f32), sds((devices, 8, 128), f32)),
        )
    else:
        grad_a = jnp.sum(a_blocks.astype(f32), axis=0)
        grad_qkv = jnp.stack([grad_a[:, i * width : (i + 1) * width] for i in range(3)])
        grad_out = grad_a[:, 3 * width :].T
        squares = jnp.broadcast_to(
            up_squares + down_squares + jnp.sum(grad_a * grad_a), (devices, 8, 128)
        )

    tokens_grad, pooled = call(
        place_kernel,
        "tokens_grad",
        (side_at,),
        (tg_own, tg_got, mean_keep),
        (sds(tokens.shape, f32), sds((rows, SEGS, width), f32)),
        gates=(squares,),
    )
    bias_part = jnp.zeros(position_bias.shape[::-1], f32)
    for index, shard in enumerate((rank, rank ^ 2)):
        bias_part = lax.dynamic_update_slice(
            bias_part, table_grad[index * heads : (index + 1) * heads, :32], (shard * heads, 0)
        )

    def from_all(value):
        return lax.all_to_all(value, ("dp", "tensor"), 0, 0, tiled=True)

    n_gain, n_bias = norm_gains.size, position_bias.size
    small = jnp.concatenate(
        [gain_grad_first[0], gain_grad_second[0], bias_part.reshape(-1)]
    )
    lanes = -(-small.shape[0] // 1024) * 1024
    small = jnp.pad(small, (0, lanes - small.shape[0])).reshape(lanes // 128, 128)
    small = jnp.sum(from_all(jnp.broadcast_to(small, (devices,) + small.shape)), axis=0)
    small_sum = small
    small = small.reshape(-1)
    grad_gains = small[:n_gain].reshape(norm_gains.shape)
    grad_biasT = small[n_gain : n_gain + n_bias].reshape(position_bias.shape[::-1])

    squares = from_all(squares)

    groups = (
        (qkv_master, grad_qkv, qkv_first, qkv_second),
        (out_master, grad_out, out_first, out_second),
        (up_master, grad_up, up_first, up_second),
        (down_master.T, grad_downT, down_first.T, down_second.T),
        (norm_gains, grad_gains, gain_first, gain_second),
        (position_bias.T, grad_biasT, bias_first.T, bias_second.T),
    )
    operands = [array for group in groups for array in group]
    updates = pl.pallas_call(
        adam_kernel,
        out_shape=[sds(group[0].shape, f32) for group in groups for _ in range(2)]
        + [sds((1, 1), f32)],
        in_specs=[VMEM_SPEC] * 2 + [pl.BlockSpec(memory_space=pltpu.HBM)] * len(operands),
        out_specs=[VMEM_SPEC] * (2 * len(groups)) + [SMEM_SPEC],
        scratch_shapes=[pltpu.VMEM(array.shape, f32) for array in operands]
        + [pltpu.SemaphoreType.DMA((len(operands),))],
        compiler_params=pltpu.CompilerParams(vmem_limit_bytes=60 << 20),
        name="adam",
    )(small_sum, squares, *operands)
    new_qkv, second_qkv, new_out, second_out, new_up, second_up = updates[0:6]
    new_gains, second_gains = updates[8:10]
    new_down, second_down, new_bias, second_bias = (updates[i].T for i in (6, 7, 10, 11))
    grad_down, grad_bias = grad_downT.T, grad_biasT.T
    gradient_norm = updates[12].reshape(())
    return (
        pooled,
        tokens_grad,
        grad_qkv,
        grad_out,
        grad_up,
        grad_down,
        grad_gains,
        grad_bias,
        gradient_norm,
        new_qkv,
        new_out,
        new_up,
        new_down,
        new_gains,
        new_bias,
        second_qkv,
        second_out,
        second_up,
        second_down,
        second_gains,
        second_bias,
    )


def solution(mesh):
    in_specs = (
        P("dp", "tensor", None),
        P("dp", None),
        P("dp", "tensor", None),
        P(None, "dp", "tensor"),
        P("tensor", "dp"),
        P("dp", "tensor"),
        P("tensor", "dp"),
        P(),
        P(),
        P(None, "dp", "tensor"),
        P(None, "dp", "tensor"),
        P("tensor", "dp"),
        P("tensor", "dp"),
        P("dp", "tensor"),
        P("dp", "tensor"),
        P("tensor", "dp"),
        P("tensor", "dp"),
        P(),
        P(),
        P(),
        P(),
    )
    out_specs = (
        P("dp", None, "tensor"),
        P("dp", "tensor", None),
        P(None, "dp", "tensor"),
        P("tensor", "dp"),
        P("dp", "tensor"),
        P("tensor", "dp"),
        P(),
        P(),
        P(),
        P(None, "dp", "tensor"),
        P("tensor", "dp"),
        P("dp", "tensor"),
        P("tensor", "dp"),
        P(),
        P(),
        P(None, "dp", "tensor"),
        P("tensor", "dp"),
        P("dp", "tensor"),
        P("tensor", "dp"),
        P(),
        P(),
    )
    return jax.shard_map(
        per_device, mesh=mesh, in_specs=in_specs, out_specs=out_specs, check_vma=False
    )
```

```python
import functools

import jax
import jax.numpy as jnp
from jax import lax
from jax.experimental import pallas as pl
from jax.experimental.pallas import tpu as pltpu
from jax.sharding import PartitionSpec as P

D = 768
H = 12
DH = 64
FF = 3072
SEGS = 16
STEP = 10

norm_eps = 1e-06
mask_fill = -1000000000.0
clip_level = 1.0
beta_first = 0.9
beta_second = 0.999
adam_eps = 1e-08
decay_rate = 0.1
gelu_scale = 0.7978845608028654
gelu_cubic = 0.044715

bf16 = jnp.bfloat16
f32 = jnp.float32
i32 = jnp.int32

SMALL_ROWS = 2 * D // 128 + H
QB = 256
KC = 128
EDGE = 128
NEAR = QB + 2 * EDGE
VMEM_LIMIT = 20 << 20
FULL_LIMIT = 60 << 20
FEED_LIMIT = 36 << 20
FILL = 1_000_000_000

SMEM_SPEC = pl.BlockSpec(memory_space=pltpu.SMEM)
VMEM_SPEC = pl.BlockSpec(memory_space=pltpu.VMEM)


def sds(shape, dtype):
    return jax.ShapeDtypeStruct(shape, dtype)


def nt(a, b):
    return lax.dot_general(a, b, (((1,), (1,)), ((), ())), preferred_element_type=f32)


def nn(a, b):
    return lax.dot_general(a, b, (((1,), (0,)), ((), ())), preferred_element_type=f32)


def call(body, name, smem, vmem, outs, scratch=(), gates=(), work=0, limit=VMEM_LIMIT):
    first, taken = len(smem) + len(vmem), len(gates)

    def gated(*refs):
        body(*refs[:first], *refs[first + taken :])

    return pl.pallas_call(
        gated if gates else body,
        out_shape=tuple(outs),
        in_specs=[SMEM_SPEC] * len(smem)
        + [VMEM_SPEC] * len(vmem)
        + [pl.BlockSpec(memory_space=pl.ANY)] * taken,
        out_specs=(VMEM_SPEC,) * len(outs),
        scratch_shapes=list(scratch),
        compiler_params=pltpu.CompilerParams(vmem_limit_bytes=limit),
        cost_estimate=pl.CostEstimate(
            flops=max(1, work * FILL), bytes_accessed=1000, transcendentals=0
        ),
        name=name,
    )(*smem, *vmem, *gates)


def bucket_of(offset):
    distance = jnp.abs(offset)
    large = 8 + sum(
        ((distance >= threshold).astype(jnp.int32) for threshold in (12, 16, 23, 32, 46, 64, 91))
    )
    inner_bucket = jnp.where(distance < 8, distance, large)
    return inner_bucket + jnp.where(offset > 0, 16, 0)


def learning_rates_plain():
    return (
        (2.0 * (D * DH) ** (-0.5), 2.0 * D ** (-0.5), 2.0 * D ** (-0.5)),
        0.5 * (H * DH / 16) ** (-0.5),
        0.5 * D ** (-0.5),
        2.0 * FF ** (-0.5),
        0.25,
        0.5,
    )


def adam_update(parameter, gradient, first_moment, second_moment, step_rate, clip_factor):
    clipped = gradient * clip_factor
    first_new = beta_first * first_moment + (1.0 - beta_first) * clipped
    second_new = beta_second * second_moment + (1.0 - beta_second) * clipped * clipped
    first_hat = first_new / (1.0 - beta_first**STEP)
    second_hat = second_new / (1.0 - beta_second**STEP)
    updated = parameter - step_rate * (
        first_hat / (jnp.sqrt(second_hat) + adam_eps) + decay_rate * parameter
    )
    return (updated, second_new)


def swap_core(value):
    return lax.ppermute(value, "tensor", [(i, i ^ 1) for i in range(lax.axis_size("tensor"))])


def swap_x(value):
    return lax.ppermute(value, "tensor", [(i, i ^ 2) for i in range(lax.axis_size("tensor"))])


def swap_dp(value, bits):
    return lax.ppermute(value, "dp", [(i, i ^ bits) for i in range(lax.axis_size("dp"))])


def swap_y(value):
    return swap_dp(value, 1)


def over_high(blocks):
    size = lax.axis_size("dp")
    groups = [[index for index in range(size) if index % 2 == bit] for bit in range(2)]
    return lax.all_to_all(blocks, "dp", 0, 0, tiled=True, axis_index_groups=groups)


def row_places():
    rank = lax.axis_index("tensor")
    return (rank, rank ^ 2, rank ^ 1, rank ^ 3)


def bias_tiles(bias_ref, first_head, heads, near_ref):
    span = 2 * NEAR
    lane = lax.broadcasted_iota(i32, (8, span), 1)
    offset = -EDGE - jnp.where(lane < span // 2, lane, lane - span)
    buckets = bucket_of(offset)
    values = [
        jnp.where(offset > 0, bias_ref[31, first_head + h], bias_ref[15, first_head + h])
        for h in range(heads)
    ]
    for bucket in list(range(15)) + list(range(17, 31)):
        here = buckets == bucket
        values = [
            jnp.where(here, bias_ref[bucket, first_head + h], values[h]) for h in range(heads)
        ]
    for h in range(heads):
        line = jnp.broadcast_to(values[h][0:1, :], (NEAR, span))
        near_ref[h] = pltpu.roll(line, 0, 1, stride=1, stride_axis=0)[:, :QB]


def rms_of(values):
    return lax.rsqrt(jnp.mean(values * values, axis=-1, keepdims=True) + norm_eps)


def blocks_of(rows, kind):
    return tuple(ref.at[kind] for ref in rows)


def norm_kernel(keep_ref, got_ref, keep_oth_ref, got_oth_ref, gain_ref, h_ref):
    length = keep_ref.shape[1]
    blocks = blocks_of((keep_ref, got_ref, keep_oth_ref, got_oth_ref), 0)
    for place, block in zip(row_places(), blocks):
        start = pl.multiple_of(place * length, length)
        values = block[...].astype(f32)
        h_ref[pl.ds(start, length), :] = (values * rms_of(values) * gain_ref[0:1, :]).astype(bf16)


def place_weights(pieces, target, kind=None):
    bit = lax.axis_index("dp") % 2
    for index, piece in enumerate(pieces):
        rows = piece.shape[-2]
        lowest = bit if index == 0 else 1 - bit
        for slot in range(piece.shape[0]):
            start = pl.multiple_of((2 * slot + lowest) * rows, 16)
            target[pl.ds(start, rows), :] = piece[slot] if kind is None else piece[slot, kind]


def split_rows(source, own_ref, other_ref):
    rows = own_ref.shape[1]
    bit = lax.axis_index("dp") % 2
    for block in range(own_ref.shape[0]):
        start = pl.multiple_of((2 * block + bit) * rows, 16)
        own_ref[block] = source[pl.ds(start, rows), :]
        start = pl.multiple_of((2 * block + 1 - bit) * rows, 16)
        other_ref[block] = source[pl.ds(start, rows), :]


def sub_sum(values):
    return jnp.sum(values.reshape(values.shape[0] // 8, 8, values.shape[1]), axis=0)


def sub_max(values):
    return jnp.max(values.reshape(values.shape[0] // 8, 8, values.shape[1]), axis=0)


def blocks_even(seq):
    return (seq // QB) % 2 == 0


def near_row(block, chunk):
    start = chunk * KC - block * QB + EDGE
    return start if 0 <= start and start + KC <= NEAR else None


def same_segment(seg_keys, keys, seg_query):
    seg_key = seg_keys[keys, :]
    return jnp.concatenate([seg_key] * (QB // seg_key.shape[1]), axis=1) == seg_query


def segments(seg_ref):
    line = seg_ref[pl.ds(lax.axis_index("tensor") // 2, 1), :]
    return line, jnp.broadcast_to(line, (128, line.shape[1])).T


def one_item(seg_smem_ref):
    side = lax.axis_index("tensor") // 2
    return seg_smem_ref[side, 0] == seg_smem_ref[side, seg_smem_ref.shape[1] - 1]


def head_of(shift, heads):
    return (lax.axis_index("tensor") ^ shift) * heads


def attend_kernel(
    shift, seg_smem_ref, bias_ref, h_ref, piece_a_ref, piece_b_ref, seg_ref,
    wT_ref, qkvT_ref, oT_ref, lse_ref, w_buf, k_buf, s_buf, p_buf, near_ref, segk_ref,
):
    seq = h_ref.shape[0]
    heads = near_ref.shape[0]
    width = oT_ref.shape[0]
    first_head = head_of(shift, heads)
    bias_tiles(bias_ref, first_head, heads, near_ref)
    size = width // heads
    chunks = seq // KC
    assert blocks_even(seq)
    place_weights((piece_a_ref, piece_b_ref), w_buf)
    wT_ref[...] = w_buf[...].T
    qkvT_ref[...] = nt(wT_ref[0 : 3 * width, :], h_ref[...]).astype(bf16)
    blocks = seq // QB

    def rows(part, h):
        return pl.ds(pl.multiple_of(part * width + h * size, size), size)

    def score(h, block):
        s_buf[block % 2] = nn(k_buf[h % 2], qkvT_ref[rows(0, h), block * QB : (block + 1) * QB])

    def soften(h, block, masked):
        slot = block % 2
        qs = slice(block * QB, (block + 1) * QB)
        top = jnp.full((8, QB), -3e38, f32)
        for chunk in range(chunks):
            ks = slice(chunk * KC, (chunk + 1) * KC)
            row = near_row(block, chunk)
            if row is None:
                scores = s_buf[slot, ks, :] + bias_ref[15 if chunk * KC < block * QB else 31, first_head + h]
            else:
                scores = s_buf[slot, ks, :] + near_ref[h, row : row + KC, :]
            if masked:
                scores = jnp.where(same_segment(segk_ref, ks, segq[:, qs]), scores, mask_fill)
            s_buf[slot, ks, :] = scores
            top = jnp.maximum(top, sub_max(scores))
        top = jnp.max(top, axis=0, keepdims=True)
        total = jnp.zeros((8, QB), f32)
        for chunk in range(chunks):
            ks = slice(chunk * KC, (chunk + 1) * KC)
            exps = jnp.exp(s_buf[slot, ks, :] - top)
            s_buf[slot, ks, :] = exps
            total = total + sub_sum(exps)
        total = jnp.sum(total, axis=0, keepdims=True)
        scale = 1.0 / total
        for chunk in range(chunks):
            ks = slice(chunk * KC, (chunk + 1) * KC)
            p_buf[slot, ks, :] = (s_buf[slot, ks, :] * scale).astype(bf16)
        lse_ref[pl.ds(h, 1), qs] = top + jnp.log(total)

    def mix(h, block):
        qs = slice(block * QB, (block + 1) * QB)
        oT_ref[rows(0, h), qs] = nn(qkvT_ref[rows(2, h), :], p_buf[block % 2]).astype(bf16)

    segq, seg_keys = segments(seg_ref)

    def run(masked):
        if masked:
            segk_ref[...] = seg_keys
        k_buf[0] = qkvT_ref[rows(1, 0), :].T
        score(0, 0)

        def head(h, carried):
            for block in range(blocks):
                if block + 1 < blocks:
                    score(h, block + 1)
                else:
                    later = jnp.minimum(h + 1, heads - 1)
                    k_buf[(h + 1) % 2] = qkvT_ref[rows(1, later), :].T
                    s_buf[0] = nn(k_buf[(h + 1) % 2], qkvT_ref[rows(0, later), 0:QB])
                soften(h, block, masked)
                if block:
                    mix(h, block - 1)
            mix(h, blocks - 1)
            return carried

        lax.fori_loop(0, heads, head, 0)

    single = one_item(seg_smem_ref)

    @pl.when(single)
    def _():
        run(False)

    @pl.when(jnp.logical_not(single))
    def _():
        run(True)


def attend(shift, seg, bias, h, pieces):
    seq = h.shape[0]
    cols = pieces[0].shape[2]
    width = cols // 4
    heads = bias.shape[1] // 4
    return call(
        functools.partial(attend_kernel, shift),
        "attend",
        (seg, bias),
        (h, *pieces, seg),
        (sds((cols, D), bf16), sds((3 * width, seq), bf16), sds((width, seq), bf16), sds((8, seq), f32)),
        (
            pltpu.VMEM((D, cols), bf16),
            pltpu.VMEM((2, seq, width // heads), bf16),
            pltpu.VMEM((2, seq, QB), f32),
            pltpu.VMEM((2, seq, QB), bf16),
            pltpu.VMEM((heads, NEAR, QB), f32),
            pltpu.VMEM((seq, 128), i32),
        ),
    )


def attend_back_kernel(
    shift, seg_smem_ref, bias_ref, qkvT_ref, doT_ref, lse_ref, seg_ref, h_ref, goT_ref,
    dqkvT_ref, own_ref, other_ref, dbias_ref,
    kv_buf, s_buf, dp_buf, ds_buf, pt_buf, dt_buf, dk_buf, dv_buf, g_buf, near_ref, segk_ref,
    dnear_ref, dfar_ref, line_buf,
):
    width, seq = doT_ref.shape
    heads = near_ref.shape[0]
    first_head = head_of(shift, heads)
    bias_tiles(bias_ref, first_head, heads, near_ref)
    segq, seg_keys = segments(seg_ref)
    size = width // heads
    blocks = seq // QB
    chunks = seq // KC
    assert blocks_even(seq)

    def rows(part, h):
        return pl.ds(pl.multiple_of(part * width + h * size, size), size)

    def key_values(h, turn):
        kv_buf[turn] = jnp.concatenate([qkvT_ref[rows(1, h), :], qkvT_ref[rows(2, h), :]], axis=0).T

    def products(h, turn, block):
        slot = block % 2
        qs = slice(block * QB, (block + 1) * QB)
        zeros = jnp.zeros((size, QB), bf16)
        s_buf[slot] = nn(kv_buf[turn], jnp.concatenate([qkvT_ref[rows(0, h), qs], zeros], axis=0))
        dp_buf[slot] = nn(kv_buf[turn], jnp.concatenate([zeros, doT_ref[rows(0, h), qs]], axis=0))

    def soften(h, block, masked):
        slot = block % 2
        qs = slice(block * QB, (block + 1) * QB)
        lse = lse_ref[pl.ds(h, 1), qs]
        lse_left = lse - bias_ref[15, first_head + h]
        lse_right = lse - bias_ref[31, first_head + h]
        dots = jnp.zeros((8, QB), f32)
        for chunk in range(chunks):
            ks = slice(chunk * KC, (chunk + 1) * KC)
            row = near_row(block, chunk)
            if row is None:
                scores = s_buf[slot, ks, :] - (lse_left if chunk * KC < block * QB else lse_right)
            else:
                scores = s_buf[slot, ks, :] + near_ref[h, row : row + KC, :] - lse
            probs = jnp.exp(scores)
            if masked:
                probs = jnp.where(same_segment(segk_ref, ks, segq[:, qs]), probs, 0.0)
            s_buf[slot, ks, :] = probs
            pt_buf[slot, :, ks] = probs.astype(bf16).T
            dots = dots + sub_sum(probs * dp_buf[slot, ks, :])
        dots = jnp.sum(dots, axis=0, keepdims=True)
        for chunk in range(chunks):
            ks = slice(chunk * KC, (chunk + 1) * KC)
            d_scores = (s_buf[slot, ks, :] * (dp_buf[slot, ks, :] - dots)).astype(bf16)
            ds_buf[slot, ks, :] = d_scores
            dt_buf[slot, :, ks] = d_scores.T
            row = near_row(block, chunk)
            if row is not None:
                if block == 0 or (block == 1 and row == 0):
                    dnear_ref[h, row : row + KC, :] = d_scores.astype(f32)
                else:
                    dnear_ref[h, row : row + KC, :] += d_scores.astype(f32)

    def outputs(h, block):
        slot = block % 2
        qs = slice(block * QB, (block + 1) * QB)
        dqkvT_ref[rows(0, h), qs] = nn(qkvT_ref[rows(1, h), :], ds_buf[slot]).astype(bf16)
        d_keys = nn(
            jnp.concatenate([qkvT_ref[rows(0, h), qs], jnp.ones((16, QB), bf16)], axis=0),
            dt_buf[slot],
        )
        d_values = nn(doT_ref[rows(0, h), qs], pt_buf[slot])
        if block == 0:
            dk_buf[...] = d_keys[0:size]
            dv_buf[...] = d_values
        elif block + 1 < blocks:
            dk_buf[...] += d_keys[0:size]
            dv_buf[...] += d_values
        else:
            dqkvT_ref[rows(1, h), :] = (dk_buf[...] + d_keys[0:size]).astype(bf16)
            dqkvT_ref[rows(2, h), :] = (dv_buf[...] + d_values).astype(bf16)
        sums = d_keys[size : size + 1]
        left_end = max(0, block * QB - EDGE)
        right_start = min(seq, block * QB + QB + EDGE)
        lane = lax.broadcasted_iota(i32, (1, 128), 1)
        line = jnp.zeros((1, 128), f32)
        if left_end:
            line = jnp.where(lane == 0, jnp.sum(sums[:, :left_end], axis=1, keepdims=True), line)
        if right_start < seq:
            line = jnp.where(lane == 1, jnp.sum(sums[:, right_start:], axis=1, keepdims=True), line)
        if block == 0:
            dfar_ref[pl.ds(h, 1), :] = line
        else:
            dfar_ref[pl.ds(h, 1), :] += line

    def run(masked):
        if masked:
            segk_ref[...] = seg_keys
        key_values(0, 0)
        products(0, 0, 0)

        def head(h, carried):
            for block in range(blocks):
                if block + 1 < blocks:
                    products(h, h % 2, block + 1)
                else:
                    later = jnp.minimum(h + 1, heads - 1)
                    key_values(later, (h + 1) % 2)
                    products(later, (h + 1) % 2, 0)
                soften(h, block, masked)
                if block:
                    outputs(h, block - 1)
            outputs(h, blocks - 1)
            return carried

        lax.fori_loop(0, heads, head, 0)

    single = one_item(seg_smem_ref)

    @pl.when(single)
    def _():
        run(False)

    @pl.when(jnp.logical_not(single))
    def _():
        run(True)

    dfar_ref[heads:, :] = jnp.zeros((8 - heads, 128), f32)
    grad = jnp.concatenate([nn(dqkvT_ref[...], h_ref[...]).astype(bf16), goT_ref[...]], axis=0)
    if other_ref is None:
        own_ref[...] = grad.T
    else:
        g_buf[...] = grad.T
        split_rows(g_buf, own_ref, other_ref)
    bias_gradients(dnear_ref, dfar_ref, line_buf, dbias_ref)


def attend_back(shift, seg, bias, qkvT, doT, lse, h, goT, grad_outs, gates):
    width, seq = doT.shape
    heads = bias.shape[1] // 4
    size = width // heads
    body = functools.partial(attend_back_kernel, shift)
    if len(grad_outs) == 1:

        def body(*refs):
            attend_back_kernel(shift, *refs[:10], None, *refs[10:])

    return call(
        body,
        "attend_back",
        (seg, bias),
        (qkvT, doT, lse, seg, h, goT),
        (sds(qkvT.shape, bf16), *grad_outs, sds((8, 128), f32)),
        (
            pltpu.VMEM((2, seq, 2 * size), bf16),
            pltpu.VMEM((2, seq, QB), f32),
            pltpu.VMEM((2, seq, QB), f32),
            pltpu.VMEM((2, seq, QB), bf16),
            pltpu.VMEM((2, QB, seq), bf16),
            pltpu.VMEM((2, QB, seq), bf16),
            pltpu.VMEM((size, seq), f32),
            pltpu.VMEM((size, seq), f32),
            pltpu.VMEM((D, 4 * width), bf16),
            pltpu.VMEM((heads, NEAR, QB), f32),
            pltpu.VMEM((seq, 128), i32),
            pltpu.VMEM((heads, NEAR, QB), f32),
            pltpu.VMEM((8, 128), f32),
            pltpu.VMEM((8, 2 * NEAR), f32),
        ),
        gates,
    )


def project_kernel(oT0_ref, oT1_ref, wT0_ref, wT1_ref, keep_ref, send_ref, o_buf):
    width = oT0_ref.shape[0]
    length = keep_ref.shape[0] // 2
    o_buf[...] = jnp.concatenate([oT0_ref[...], oT1_ref[...]], axis=0).T
    w = jnp.concatenate([wT0_ref[3 * width :, :], wT1_ref[3 * width :, :]], axis=0)
    for index, place in enumerate(row_places()):
        start = pl.multiple_of(place * length, length)
        part = nn(o_buf[pl.ds(start, length), :], w)
        rows = slice((index % 2) * length, (index % 2 + 1) * length)
        if index < 2:
            keep_ref[rows, :] = part
        else:
            send_ref[rows, :] = part.astype(send_ref.dtype)


def middle_kernel(keep_row_ref, got_row_ref, part_ref, got_ref, gain_ref, x2_ref, h_ref):
    length = keep_row_ref.shape[1]
    for index, block in enumerate((keep_row_ref.at[0], got_row_ref.at[0])):
        rows = slice(index * length, (index + 1) * length)
        values = block[...].astype(f32) + part_ref[rows, :] + got_ref[rows, :].astype(f32)
        x2_ref[rows, :] = values
        h_ref[rows, :] = (values * rms_of(values) * gain_ref[1:2, :]).astype(bf16)


def split3(values):
    high = values.astype(bf16)
    rest = values - high.astype(f32)
    mid = rest.astype(bf16)
    low = (rest - mid.astype(f32)).astype(bf16)
    return high, mid, low


def feed_rows(h, cot, u_buf, d_buf, act_ref, dpre_ref, rows):
    pre = nn(h, u_buf[...])
    d_act = nn(cot, d_buf[...])
    square = pre * pre
    bent = jnp.tanh(gelu_scale * pre * (1.0 + gelu_cubic * square))
    half_up = 0.5 * (1.0 + bent)
    act_ref[rows, :] = (pre * half_up).astype(bf16)
    slope = half_up + (0.5 * gelu_scale) * pre * (1.0 - bent * bent) * (
        1.0 + (3.0 * gelu_cubic) * square
    )
    d_pre = (d_act * slope).astype(bf16)
    dpre_ref[rows, :] = d_pre
    return nt(d_pre, u_buf[...])


def pooled_units(hot, act_ref, d_buf):
    pooled = None
    for term in split3(nn(hot, act_ref[...])):
        part = nt(term, d_buf[...])
        pooled = part if pooled is None else pooled + part
    return pooled


def weight_grads(h_refs, cots, act_ref, dpre_ref, outs, g_buf):
    hT = jnp.concatenate([ref[...] for ref in h_refs], axis=0).T
    cotT = jnp.concatenate([block[...] for block in cots], axis=0).T
    if len(outs) == 2:
        outs[0][...] = nn(hT, dpre_ref[...]).astype(bf16)
        outs[1][...] = nn(cotT, act_ref[...]).astype(bf16)
    else:
        g_buf[0] = nn(hT, dpre_ref[...]).astype(bf16)
        split_rows(g_buf.at[0], outs[0], outs[1])
        g_buf[1] = nn(cotT, act_ref[...]).astype(bf16)
        split_rows(g_buf.at[1], outs[2], outs[3])


def feed_own_kernel(
    h_own_ref, h_oth_ref, keep_ref, got_ref, keep_oth_ref, got_oth_ref,
    a_ref, b_ref, seg_ref, x2_ref, dh_ref, pooled_ref, hot_ref, *refs
):
    *outs, u_buf, d_buf, act_buf, dpre_buf, g_buf = refs
    place_weights((a_ref, b_ref), u_buf, 0)
    place_weights((a_ref, b_ref), d_buf, 1)
    length = keep_ref.shape[1]
    cots = blocks_of((keep_ref, got_ref, keep_oth_ref, got_oth_ref), 1)
    line = seg_ref[pl.ds(lax.axis_index("tensor") // 2, 1), :]
    seq = line.shape[1]
    item = lax.broadcasted_iota(i32, (SEGS, seq), 0)
    whole = (jnp.broadcast_to(line, (SEGS, seq)) == item).astype(f32)
    for index, place in enumerate(row_places()):
        part = jnp.zeros((SEGS, length), f32)
        for block in range(4):
            part = jnp.where(place == block, whole[:, block * length : (block + 1) * length], part)
        hot_ref[:, index * length : (index + 1) * length] = part.astype(bf16)
    for index in range(4):
        rows = slice(index * length, (index + 1) * length)
        half = slice((index % 2) * length, (index % 2 + 1) * length)
        h = (h_own_ref if index < 2 else h_oth_ref)[half, :]
        dh_ref[rows, :] = feed_rows(h, cots[index][...], u_buf, d_buf, act_buf, dpre_buf, rows)
    hot = hot_ref[...]
    pooled = pooled_units(hot, act_buf, d_buf)
    for term in split3(x2_ref[...]):
        pooled = pooled + nn(hot[:, 0 : 2 * length], term)
    pooled_ref[...] = pooled
    weight_grads((h_own_ref, h_oth_ref), cots, act_buf, dpre_buf, outs, g_buf)


def feed_other_kernel(
    h_own_ref, h_oth_ref, keep_ref, got_ref, keep_oth_ref, got_oth_ref,
    a_ref, ub_ref, db_ref, hot_ref, dh_ref, pool_ref,
    part_ref, send_ref, pooled_ref, *refs
):
    *outs, u_buf, d_buf, act_buf, dpre_buf, g_buf = refs
    place_weights((a_ref,), u_buf, 0)
    place_weights((a_ref,), d_buf, 1)
    bit = lax.axis_index("dp") % 2
    for source, target in ((ub_ref, u_buf), (db_ref, d_buf)):
        count = source.shape[1]
        for slot in range(source.shape[0]):
            start = pl.multiple_of((2 * slot + 1 - bit) * count, 16)
            target[pl.ds(start, count), :] = source[slot]
    length = keep_ref.shape[1]
    cots = blocks_of((keep_ref, got_ref, keep_oth_ref, got_oth_ref), 1)
    for index in (2, 3, 0, 1):
        rows = slice(index * length, (index + 1) * length)
        half = slice((index % 2) * length, (index % 2 + 1) * length)
        h = (h_own_ref if index < 2 else h_oth_ref)[half, :]
        total = dh_ref[rows, :] + feed_rows(
            h, cots[index][...], u_buf, d_buf, act_buf, dpre_buf, rows
        )
        if index < 2:
            part_ref[half, :] = total
        else:
            send_ref[half, :] = total.astype(send_ref.dtype)
    pooled_ref[...] = pool_ref[...] + pooled_units(hot_ref[...], act_buf, d_buf)
    weight_grads((h_own_ref, h_oth_ref), cots, act_buf, dpre_buf, outs, g_buf)


def norm_back(values, gain, upstream):
    scale = rms_of(values)
    normed = values * scale
    gain_grad = jnp.sum(upstream * normed, axis=0, keepdims=True)
    scaled = upstream * gain
    inner = jnp.mean(scaled * normed, axis=-1, keepdims=True)
    return scale * (scaled - normed * inner), gain_grad


def middle_back_kernel(
    x2_ref, part_ref, got_ref, keep_row_ref, got_row_ref, gain_ref, dx2_ref, da_ref, gain_grad_ref
):
    length = x2_ref.shape[0] // 2
    for index, cot in enumerate((keep_row_ref.at[1], got_row_ref.at[1])):
        rows = slice(index * length, (index + 1) * length)
        d_values, gain_grad = norm_back(
            x2_ref[rows, :], gain_ref[1:2, :], part_ref[rows, :] + got_ref[rows, :].astype(f32)
        )
        dx2 = cot[...].astype(f32) + d_values
        dx2_ref[rows, :] = dx2
        da_ref[rows, :] = dx2.astype(bf16)
        if index == 0:
            gain_grad_ref[...] = gain_grad
        else:
            gain_grad_ref[...] += gain_grad


def branch_back_kernel(
    da_own_ref, da_oth_ref, wT0_ref, wT1_ref, oT0_ref, oT1_ref,
    doT0_ref, doT1_ref, g0_ref, g1_ref, da_buf,
):
    width = oT0_ref.shape[0]
    length = da_own_ref.shape[0] // 2
    for index, place in enumerate(row_places()):
        start = pl.multiple_of(place * length, length)
        half = slice((index % 2) * length, (index % 2 + 1) * length)
        da_buf[pl.ds(start, length), :] = (da_own_ref if index < 2 else da_oth_ref)[half, :]
    da = da_buf[...]
    doT0_ref[...] = nt(wT0_ref[3 * width :, :], da).astype(bf16)
    doT1_ref[...] = nt(wT1_ref[3 * width :, :], da).astype(bf16)
    g0_ref[...] = nn(oT0_ref[...], da).astype(bf16)
    g1_ref[...] = nn(oT1_ref[...], da).astype(bf16)


def first_back_kernel(d0_ref, d1_ref, wT0_ref, wT1_ref, keep_ref, send_ref, d_buf):
    rows3 = d0_ref.shape[0]
    length = keep_ref.shape[0] // 2
    d_buf[...] = jnp.concatenate([d0_ref[...], d1_ref[...]], axis=0).T
    w = jnp.concatenate([wT0_ref[0:rows3, :], wT1_ref[0:rows3, :]], axis=0)
    places = row_places()
    for index in (2, 3, 0, 1):
        start = pl.multiple_of(places[index] * length, length)
        part = nn(d_buf[pl.ds(start, length), :], w)
        rows = slice((index % 2) * length, (index % 2 + 1) * length)
        if index < 2:
            keep_ref[rows, :] = part
        else:
            send_ref[rows, :] = part.astype(send_ref.dtype)


def token_grad_kernel(
    keep_row_ref, got_row_ref, part_ref, got_ref, dx2_ref, gain_ref, pool_ref, pool_got_ref, hot_ref,
    own_ref, away_ref, gain_grad_ref, mean_ref
):
    length = keep_row_ref.shape[1]
    away_ref[length:, :] = jnp.zeros((away_ref.shape[0] - length, away_ref.shape[1]), f32)
    counts = jnp.sum(hot_ref[...].astype(f32), axis=1, keepdims=True)
    means = (pool_ref[...] + pool_got_ref[...]) / jnp.maximum(counts, 1.0)
    rank = lax.axis_index("tensor")
    width = mean_ref.shape[1]
    mine, sent = jnp.zeros(mean_ref.shape, f32), jnp.zeros(mean_ref.shape, f32)
    for shard in range(4):
        part = means[:, shard * width : (shard + 1) * width]
        mine = jnp.where(rank == shard, part, mine)
        sent = jnp.where(rank ^ 2 == shard, part, sent)
    mean_ref[...] = mine
    away_ref[length:, 0:width] = sent
    for index, block in enumerate((keep_row_ref.at[0], got_row_ref.at[0])):
        rows = slice(index * length, (index + 1) * length)
        d_values, gain_grad = norm_back(
            block[...].astype(f32), gain_ref[0:1, :], part_ref[rows, :] + got_ref[rows, :].astype(f32)
        )
        if index == 0:
            own_ref[...] = dx2_ref[rows, :] + d_values
            gain_grad_ref[...] = gain_grad
        else:
            away_ref[0:length, :] = dx2_ref[rows, :] + d_values
            gain_grad_ref[...] += gain_grad


def bias_gradients(dnear_ref, dfar_ref, line_buf, grad_ref):
    heads = dnear_ref.shape[0]
    span = 2 * NEAR
    line_buf[...] = jnp.zeros_like(line_buf)
    for h in range(heads):
        values = dnear_ref[h]
        rows = NEAR
        while rows > 1:
            rows //= 2
            low, high = values[:rows], values[rows:]
            if rows % 128 == 0:
                pad = jnp.zeros((rows, rows), f32)
                values = jnp.concatenate([pad, low], axis=1) + jnp.concatenate([high, pad], axis=1)
            else:
                if values.shape[1] < span:
                    pad = jnp.zeros((rows, span - values.shape[1]), f32)
                    low = jnp.concatenate([pad, low], axis=1)
                    high = jnp.concatenate([pad, high], axis=1)
                values = low + pltpu.roll(high, span - rows, 1)
        line_buf[h : h + 1, :] = values
    lines = line_buf[...]
    col = lax.broadcasted_iota(i32, lines.shape, 1)
    buckets = bucket_of(span - QB - EDGE - col)
    far = dfar_ref[...]
    lane = lax.broadcasted_iota(i32, (8, 128), 1)
    left = jnp.sum(jnp.where(lane == 0, far, 0.0), axis=1, keepdims=True)
    right = jnp.sum(jnp.where(lane == 1, far, 0.0), axis=1, keepdims=True)
    grad = jnp.where(lane == 15, left, jnp.where(lane == 31, right, 0.0))
    for bucket in range(32):
        if bucket != 16:
            total = jnp.sum(jnp.where(buckets == bucket, lines, 0.0), axis=1, keepdims=True)
            grad = jnp.where(lane == bucket, grad + total, grad)
    grad_ref[...] = grad


def pack_kernel(qkv_ref, out_ref, tokens_ref, cot_ref, pack_ref, keep_ref, send_ref):
    packed = jnp.concatenate([qkv_ref[0], qkv_ref[1], qkv_ref[2], out_ref[...].T], axis=1).astype(bf16)
    for slot in range(pack_ref.shape[0]):
        pack_ref[slot] = packed
    rows_kernel(tokens_ref, cot_ref, keep_ref, send_ref)


def pack_ud_kernel(up_ref, down_ref, pack_ref):
    up, down = up_ref[...].astype(bf16), down_ref[...].astype(bf16)
    for slot in range(pack_ref.shape[0]):
        pack_ref[slot, 0] = up
        pack_ref[slot, 1] = down


def rows_kernel(tokens_ref, cot_ref, keep_ref, send_ref):
    side = lax.axis_index("tensor") // 2
    keep_ref[0] = tokens_ref[side]
    keep_ref[1] = cot_ref[side]
    send_ref[0] = tokens_ref[1 - side]
    send_ref[1] = cot_ref[1 - side]


def place_kernel(own_ref, got_ref, mean_ref, out_ref, pooled_ref):
    side = lax.axis_index("tensor") // 2
    length, width = own_ref.shape[0], mean_ref.shape[1]
    out_ref[side] = own_ref[...]
    out_ref[1 - side] = got_ref[0:length, :]
    pooled_ref[side] = mean_ref[...]
    pooled_ref[1 - side] = got_ref[length:, 0:width]


def pick_kernel(from_x_ref, from_y_ref, up_ref, down_ref):
    up_ref[...] = from_x_ref[:, 0]
    down_ref[...] = from_y_ref[:, 1]


def total_of(refs):
    total = refs[0][...].astype(f32)
    for ref in refs[1:]:
        total = total + ref[...].astype(f32)
    return total


def add_kernel(*refs):
    *terms, sum_ref, token_ref = refs
    sum_ref[...] = total_of(terms).astype(bf16)
    token_ref[...] = jnp.zeros_like(token_ref)


def send_kernel(*refs):
    *terms, own_ref, sent1_ref, sent2_ref, sent3_ref, token_ref, sum_buf = refs
    sum_buf[...] = total_of(terms)
    place = lax.axis_index("dp") // 2
    own_ref[...] = sum_buf[place]
    for bits, ref in ((1, sent1_ref), (2, sent2_ref), (3, sent3_ref)):
        ref[...] = sum_buf[place ^ bits].astype(bf16)
    token_ref[...] = jnp.zeros_like(token_ref)


def add_pairs_kernel(
    up_ref, up_got_ref, down_ref, down_got_ref, pass_ref, up_sum_ref, down_sum_ref, passed_ref, token_ref
):
    up_sum_ref[...] = total_of((up_ref, up_got_ref)).astype(bf16)
    down_sum_ref[...] = total_of((down_ref, down_got_ref)).astype(bf16)
    passed_ref[...] = pass_ref[...]
    token_ref[...] = jnp.zeros_like(token_ref)


def sum_blocks(ref):
    total = ref[0].astype(f32)
    for slot in range(1, ref.shape[0]):
        total = total + ref[slot].astype(f32)
    return total


def finish_kernel(*refs):
    *terms, grad_ref, squares_ref = refs
    total = total_of(terms) if len(terms) > 1 else sum_blocks(terms[0])
    grad_ref[...] = total
    squares_ref[...] = jnp.broadcast_to(jnp.sum(total * total, axis=(0, 1), keepdims=True), (8, 128))


def finish_a_kernel(blocks_ref, up_ref, down_ref, qkv_ref, out_ref, squares_ref):
    total = sum_blocks(blocks_ref)
    width = qkv_ref.shape[2]
    for part in range(3):
        qkv_ref[part] = total[:, part * width : (part + 1) * width]
    out_ref[...] = total[:, 3 * width :].T
    squares = up_ref[...] + down_ref[...] + jnp.sum(total * total, axis=(0, 1), keepdims=True)
    for slot in range(squares_ref.shape[0]):
        squares_ref[slot] = squares


def small_kernel(first_ref, second_ref, own_bias_ref, other_bias_ref, out_ref):
    lines = D // 128
    heads = (out_ref.shape[1] - 2 * lines) // 4
    out_ref[0] = jnp.zeros(out_ref.shape[1:], f32)
    for kind, ref in enumerate((first_ref, second_ref)):
        for line in range(lines):
            out_ref[0, kind * lines + line : kind * lines + line + 1, :] = ref[
                :, line * 128 : (line + 1) * 128
            ]
    for shift, ref in ((0, own_bias_ref), (2, other_bias_ref)):
        start = 2 * lines + head_of(shift, heads)
        for h in range(heads):
            out_ref[0, pl.ds(start + h, 1), :] = ref[h : h + 1, :]
    value = out_ref[0]
    for slot in range(1, out_ref.shape[0]):
        out_ref[slot] = value


def adam_kernel(small_ref, squares_ref, *refs):
    *refs, sems = refs
    sources, refs = refs[:22], refs[22:]
    outs, refs = refs[:15], refs[15:]
    copies = [
        pltpu.make_async_copy(source, target, sems.at[index])
        for index, (source, target) in enumerate(zip(sources, refs))
    ]
    for copy in copies:
        copy.start()
    small = jnp.sum(small_ref[...], axis=0)
    lines = D // 128
    gains_ref, bias_ref, norm_ref = outs[12:]
    for kind in range(2):
        for line in range(lines):
            gains_ref[kind : kind + 1, line * 128 : (line + 1) * 128] = small[
                kind * lines + line : kind * lines + line + 1
            ]
    bias_ref[...] = small[2 * lines :, 0 : bias_ref.shape[1]]
    total = jnp.sum(squares_ref[...], axis=0)[0:1, 0:1]
    norm = jnp.sqrt(total + jnp.sum(small * small, axis=(0, 1), keepdims=True))
    norm_ref[0, 0] = jnp.max(norm)
    clip = jnp.minimum(1.0, clip_level / norm)
    for copy in copies:
        copy.wait()
    rates = learning_rates_plain()
    params = [refs[4 * index : 4 * index + 4] for index in range(4)]
    params.append((refs[16], gains_ref, refs[17], refs[18]))
    params.append((refs[19], bias_ref, refs[20], refs[21]))
    for index, (param, grad, first, second) in enumerate(params):
        new, new_second = outs[2 * index], outs[2 * index + 1]
        if isinstance(rates[index], tuple):
            for part, rate in enumerate(rates[index]):
                value, moment = adam_update(
                    param[part], grad[part], first[part], second[part], rate, clip
                )
                new[part] = value
                new_second[part] = moment
        else:
            value, moment = adam_update(
                param[...], grad[...], first[...], second[...], rates[index], clip
            )
            new[...] = value
            new_second[...] = moment


def per_device(
    tokens,
    segment_ids,
    cotangent,
    qkv_master,
    out_master,
    up_master,
    down_master,
    norm_gains,
    position_bias,
    qkv_first,
    qkv_second,
    out_first,
    out_second,
    up_first,
    up_second,
    down_first,
    down_second,
    gain_first,
    gain_second,
    bias_first,
    bias_second,
):
    rank = lax.axis_index("tensor")
    dp_rank = lax.axis_index("dp")
    dp_size = lax.axis_size("dp")
    row_bit = dp_rank % 2
    rows, length = tokens.shape[0], tokens.shape[1]
    seq = segment_ids.shape[1]
    shard_rows, width = qkv_master.shape[1], qkv_master.shape[2]
    units = up_master.shape[1]
    half = (seq // 2, D)
    assert rows == 2 and lax.axis_size("tensor") == 4 and seq == 4 * length
    high = dp_size // 2
    aligned = shard_rows % 16 == 0

    if aligned:
        pack_a, keep_rows, sent_rows = call(
            pack_kernel,
            "pack_a",
            (),
            (qkv_master, out_master, tokens, cotangent),
            (sds((high, shard_rows, D), bf16),) + (sds((2, length, D), bf16),) * 2,
            limit=FULL_LIMIT,
        )
        order = lambda pair: pair
        blocks_out = (sds((high, shard_rows, D), bf16),) * 2
    else:
        packed = jnp.concatenate([*qkv_master, out_master.T], axis=1).astype(bf16)
        pack_a = jnp.broadcast_to(packed, (high,) + packed.shape)
        blocks_out = (sds((D, D), bf16),)
        keep_rows, sent_rows = call(
            rows_kernel, "rows", (), (tokens, cotangent), (sds((2, length, D), bf16),) * 2
        )

        def order(pair):
            own, other = pair
            first = jnp.where(row_bit == 0, own, other)
            second = jnp.where(row_bit == 0, other, own)
            both = jnp.moveaxis(jnp.stack([first, second], axis=1), (0, 1), (-4, -3))
            both = both.reshape(both.shape[:-4] + (D, both.shape[-1]))
            lower, upper = both[..., : D // 2, :], both[..., D // 2 :, :]
            return (
                jnp.where(row_bit == 0, lower, upper)[None],
                jnp.where(row_bit == 0, upper, lower)[None],
            )

    high_a = over_high(pack_a)
    got_rows = swap_x(sent_rows)
    all_rows = (keep_rows, got_rows, swap_core(keep_rows), swap_core(got_rows))
    a_y = swap_y(high_a)
    a_x = swap_x(high_a)
    (pack_ud,) = call(
        pack_ud_kernel,
        "pack_ud",
        (),
        (up_master, down_master.T),
        (sds((high, 2, shard_rows, units), bf16),),
        gates=(high_a, got_rows),
        work=20,
    )
    high_ud = over_high(pack_ud)
    (h1,) = call(norm_kernel, "first_norm", (), (*all_rows, norm_gains), (sds((seq, D), bf16),), work=20)

    a_other = (a_x, swap_y(a_x))
    wT0, qkvT0, oT0, lse0 = attend(0, segment_ids, position_bias, h1, order((high_a, a_y)))
    ud_x = swap_x(high_ud)
    ud_y = swap_y(high_ud)
    wT1, qkvT1, oT1, lse1 = attend(2, segment_ids, position_bias, h1, order(a_other))

    keep, send = call(
        project_kernel,
        "project",
        (),
        (oT0, oT1, wT0, wT1),
        (sds(half, f32), sds(half, bf16)),
        (pltpu.VMEM((seq, 2 * width), bf16),),
    )
    x2, h2 = call(
        middle_kernel,
        "second_norm",
        (),
        (keep_rows, got_rows, keep, swap_core(send), norm_gains),
        (sds(half, f32), sds(half, bf16)),
    )
    h2_other = swap_core(h2)
    picked_u, picked_d = call(
        pick_kernel,
        "pick_ud",
        (),
        (ud_x, ud_y),
        (sds((high, shard_rows, units), bf16),) * 2,
        gates=(h2,),
    )
    u_xy = swap_y(picked_u)
    d_xy = swap_x(picked_d)

    def of_y(grad, wanted):
        blocks = grad.reshape((high, 2, shard_rows) + grad.shape[1:])
        return lax.dynamic_index_in_dim(blocks, wanted, 1, keepdims=False)

    def by_y(grads):
        if aligned:
            return tuple(grads)
        return tuple(of_y(grad, wanted) for grad in grads for wanted in (row_bit, 1 - row_bit))

    def plus(name, *terms, gates=()):
        outs = (sds(terms[0].shape, bf16), sds((8, 128), f32))
        return call(add_kernel, name, (), terms, outs, gates=gates)

    def over_high_bits(name, *terms, gates=()):
        if high != 4:
            total, token = plus(name, *terms, gates=gates)
            return (over_high(total),), token
        block = terms[0].shape[1:]
        own, *sent, token = call(
            send_kernel,
            name,
            (),
            terms,
            (sds(block, f32),) + (sds(block, bf16),) * 3 + (sds((8, 128), f32),),
            (pltpu.VMEM(terms[0].shape, f32),),
            gates=gates,
        )
        return (own, *(swap_dp(piece, 2 * bits) for bits, piece in enumerate(sent, 1))), token

    feed_scratch = (
        *([pltpu.VMEM((D, units), bf16)] * 2),
        *([pltpu.VMEM((seq, units), bf16)] * 2),
        pltpu.VMEM((2, D, units), bf16),
    )
    dh_part, pool_part, hot, *grads = call(
        feed_own_kernel,
        "feed_own",
        (),
        (h2, h2_other, *all_rows, *order((high_ud, ud_y)), segment_ids, x2),
        (sds((seq, D), f32), sds((SEGS, D), f32), sds((SEGS, seq), bf16), *blocks_out, *blocks_out),
        feed_scratch,
        limit=FEED_LIMIT,
    )
    gu0_own, gu0_oth, gd0_own, gd0_oth = by_y(grads)
    up_y0 = swap_y(gu0_oth)
    if aligned:
        ud_other = (ud_x, u_xy, d_xy)
    else:
        first, second = order((ud_x, jnp.stack([u_xy, d_xy], axis=1)))
        ud_other = (first, second[:, 0], second[:, 1])
    keep, send, pool_part, *grads = call(
        feed_other_kernel,
        "feed_other",
        (),
        (h2, h2_other, *all_rows, *ud_other, hot, dh_part, pool_part),
        (sds(half, f32), sds(half, bf16), sds((SEGS, D), f32), *blocks_out, *blocks_out),
        feed_scratch,
        limit=FEED_LIMIT,
    )
    got = swap_core(send)
    gu1_own, gu1_oth, gd1_own, gd1_oth = by_y(grads)
    up_y1 = swap_y(gu1_oth)
    down_x1 = swap_x(gd1_oth)
    dx2, da, gain_grad_second = call(
        middle_back_kernel,
        "second_norm_back",
        (),
        (x2, keep, got, keep_rows, got_rows, norm_gains),
        (sds(half, f32), sds(half, bf16), sds((1, D), f32)),
        work=10,
    )
    da_other = swap_core(da)
    doT0, doT1, goT0, goT1 = call(
        branch_back_kernel,
        "branch_back",
        (),
        (da, da_other, wT0, wT1, oT0, oT1),
        (sds((width, seq), bf16),) * 2 + (sds((width, D), bf16),) * 2,
        (pltpu.VMEM((seq, D), bf16),),
        work=10,
    )
    dqkvT1, *ga1, dbias1 = attend_back(
        2, segment_ids, position_bias, qkvT1, doT1, lse1, h1, goT1, blocks_out, ()
    )
    up_add, down_add, down_own, token = call(
        add_pairs_kernel,
        "add_ud",
        (),
        (gu1_own, up_y1, gd0_oth, down_x1, gd1_own),
        (sds(gu1_own.shape, bf16),) * 3 + (sds((8, 128), f32),),
        gates=(dbias1,),
    )
    up_x = swap_x(up_add)
    down_y = swap_y(down_add)
    down_x0 = swap_x(down_own)
    ga1_own, ga1_oth = by_y(ga1)
    a_y1 = swap_y(ga1_oth)
    dqkvT0, *ga0, dbias0 = attend_back(
        0, segment_ids, position_bias, qkvT0, doT0, lse0, h1, goT0, blocks_out, (token,)
    )
    ga0_own, ga0_oth = by_y(ga0)
    a_y0 = swap_y(ga0_oth)
    a_add, token = plus("add_a", ga1_own, a_y1, gates=(dbias0,))
    a_x1 = swap_x(a_add)
    up_pieces, token = over_high_bits("total_up", gu0_own, up_y0, up_x, gates=(token,))
    keep, send = call(
        first_back_kernel,
        "first_back",
        (),
        (dqkvT0, dqkvT1, wT0, wT1),
        (sds(half, f32), sds(half, bf16)),
        (pltpu.VMEM((seq, 6 * width), bf16),),
        gates=(token,),
    )
    first_got = swap_core(send)
    down_pieces, token = over_high_bits("total_down", gd0_own, down_x0, down_y, gates=(token,))
    tg_own, tg_away, gain_grad_first, mean_keep = call(
        token_grad_kernel,
        "first_norm_back",
        (),
        (keep_rows, got_rows, keep, first_got, dx2, norm_gains, pool_part, swap_core(pool_part), hot),
        (
            sds((length, D), f32),
            sds((length + SEGS, D), f32),
            sds((1, D), f32),
            sds((SEGS, width), f32),
        ),
        work=10,
    )
    tg_got = swap_x(tg_away)
    a_total, _ = plus("total_a", ga0_own, a_y0, a_x1, gates=(gain_grad_first,))
    a_blocks = over_high(a_total)
    grad_up, up_squares = call(
        finish_kernel,
        "finish_up",
        (),
        up_pieces,
        (sds((shard_rows, units), f32), sds((8, 128), f32)),
        gates=(gain_grad_first,),
        work=10,
    )
    grad_downT, down_squares = call(
        finish_kernel,
        "finish_down",
        (),
        down_pieces,
        (sds((shard_rows, units), f32), sds((8, 128), f32)),
        gates=(gain_grad_first,),
        work=10,
    )
    devices = dp_size * lax.axis_size("tensor")
    if aligned:
        grad_qkv, grad_out, squares = call(
            finish_a_kernel,
            "finish_a",
            (),
            (a_blocks, up_squares, down_squares),
            (sds(qkv_master.shape, f32), sds(out_master.shape, f32), sds((devices, 8, 128), f32)),
        )
    else:
        grad_a = jnp.sum(a_blocks.astype(f32), axis=0)
        grad_qkv = jnp.stack([grad_a[:, i * width : (i + 1) * width] for i in range(3)])
        grad_out = grad_a[:, 3 * width :].T
        squares = jnp.broadcast_to(
            up_squares + down_squares + jnp.sum(grad_a * grad_a), (devices, 8, 128)
        )

    tokens_grad, pooled = call(
        place_kernel,
        "tokens_grad",
        (),
        (tg_own, tg_got, mean_keep),
        (sds(tokens.shape, f32), sds((rows, SEGS, width), f32)),
        gates=(squares,),
    )
    def from_all(value):
        return lax.all_to_all(value, ("dp", "tensor"), 0, 0, tiled=True)

    (small,) = call(
        small_kernel,
        "small",
        (),
        (gain_grad_first, gain_grad_second, dbias0, dbias1),
        (sds((devices, SMALL_ROWS, 128), f32),),
        work=10,
    )
    small = from_all(small)
    squares = from_all(squares)
    groups = (
        (qkv_master, grad_qkv, qkv_first, qkv_second),
        (out_master, grad_out, out_first, out_second),
        (up_master, grad_up, up_first, up_second),
        (down_master.T, grad_downT, down_first.T, down_second.T),
        (norm_gains, None, gain_first, gain_second),
        (position_bias.T, None, bias_first.T, bias_second.T),
    )
    operands = [array for group in groups for array in group if array is not None]
    updates = pl.pallas_call(
        adam_kernel,
        out_shape=[sds(group[0].shape, f32) for group in groups for _ in range(2)]
        + [sds(norm_gains.shape, f32), sds(position_bias.shape[::-1], f32), sds((1, 1), f32)],
        in_specs=[VMEM_SPEC] * 2 + [pl.BlockSpec(memory_space=pltpu.HBM)] * len(operands),
        out_specs=[VMEM_SPEC] * (2 * len(groups) + 2) + [SMEM_SPEC],
        scratch_shapes=[pltpu.VMEM(array.shape, f32) for array in operands]
        + [pltpu.SemaphoreType.DMA((len(operands),))],
        compiler_params=pltpu.CompilerParams(vmem_limit_bytes=60 << 20),
        name="adam",
    )(small, squares, *operands)
    new_qkv, second_qkv, new_out, second_out, new_up, second_up = updates[0:6]
    new_gains, second_gains = updates[8:10]
    new_down, second_down, new_bias, second_bias = (updates[i].T for i in (6, 7, 10, 11))
    grad_gains, grad_biasT = updates[12:14]
    grad_down, grad_bias = grad_downT.T, grad_biasT.T
    gradient_norm = updates[14].reshape(())
    return (
        pooled,
        tokens_grad,
        grad_qkv,
        grad_out,
        grad_up,
        grad_down,
        grad_gains,
        grad_bias,
        gradient_norm,
        new_qkv,
        new_out,
        new_up,
        new_down,
        new_gains,
        new_bias,
        second_qkv,
        second_out,
        second_up,
        second_down,
        second_gains,
        second_bias,
    )


def solution(mesh):
    in_specs = (
        P("dp", "tensor", None),
        P("dp", None),
        P("dp", "tensor", None),
        P(None, "dp", "tensor"),
        P("tensor", "dp"),
        P("dp", "tensor"),
        P("tensor", "dp"),
        P(),
        P(),
        P(None, "dp", "tensor"),
        P(None, "dp", "tensor"),
        P("tensor", "dp"),
        P("tensor", "dp"),
        P("dp", "tensor"),
        P("dp", "tensor"),
        P("tensor", "dp"),
        P("tensor", "dp"),
        P(),
        P(),
        P(),
        P(),
    )
    out_specs = (
        P("dp", None, "tensor"),
        P("dp", "tensor", None),
        P(None, "dp", "tensor"),
        P("tensor", "dp"),
        P("dp", "tensor"),
        P("tensor", "dp"),
        P(),
        P(),
        P(),
        P(None, "dp", "tensor"),
        P("tensor", "dp"),
        P("dp", "tensor"),
        P("tensor", "dp"),
        P(),
        P(),
        P(None, "dp", "tensor"),
        P("tensor", "dp"),
        P("dp", "tensor"),
        P("tensor", "dp"),
        P(),
        P(),
    )
    return jax.shard_map(
        per_device, mesh=mesh, in_specs=in_specs, out_specs=out_specs, check_vma=False
    )
```

```python
import functools

import jax
import jax.numpy as jnp
from jax import lax
from jax.experimental import pallas as pl
from jax.experimental.pallas import tpu as pltpu
from jax.sharding import PartitionSpec as P

D = 768
H = 12
DH = 64
FF = 3072
SEGS = 16
STEP = 10

norm_eps = 1e-06
mask_fill = -1000000000.0
clip_level = 1.0
beta_first = 0.9
beta_second = 0.999
adam_eps = 1e-08
decay_rate = 0.1
gelu_scale = 0.7978845608028654
gelu_cubic = 0.044715

bf16 = jnp.bfloat16
f32 = jnp.float32
i32 = jnp.int32

SMALL_ROWS = 2 * D // 128 + H
QB = 256
KC = 128
EDGE = 128
NEAR = QB + 2 * EDGE
VMEM_LIMIT = 20 << 20
FULL_LIMIT = 60 << 20
FEED_LIMIT = 36 << 20
FILL = 1_000_000_000

SMEM_SPEC = pl.BlockSpec(memory_space=pltpu.SMEM)
VMEM_SPEC = pl.BlockSpec(memory_space=pltpu.VMEM)


def sds(shape, dtype):
    return jax.ShapeDtypeStruct(shape, dtype)


def nt(a, b):
    return lax.dot_general(a, b, (((1,), (1,)), ((), ())), preferred_element_type=f32)


def nn(a, b):
    return lax.dot_general(a, b, (((1,), (0,)), ((), ())), preferred_element_type=f32)


def call(body, name, smem, vmem, outs, scratch=(), gates=(), work=0, limit=VMEM_LIMIT):
    first, taken = len(smem) + len(vmem), len(gates)

    def gated(*refs):
        body(*refs[:first], *refs[first + taken :])

    return pl.pallas_call(
        gated if gates else body,
        out_shape=tuple(outs),
        in_specs=[SMEM_SPEC] * len(smem)
        + [VMEM_SPEC] * len(vmem)
        + [pl.BlockSpec(memory_space=pl.ANY)] * taken,
        out_specs=(VMEM_SPEC,) * len(outs),
        scratch_shapes=list(scratch),
        compiler_params=pltpu.CompilerParams(vmem_limit_bytes=limit),
        cost_estimate=pl.CostEstimate(
            flops=max(1, work * FILL), bytes_accessed=1000, transcendentals=0
        ),
        name=name,
    )(*smem, *vmem, *gates)


def bucket_of(offset):
    distance = jnp.abs(offset)
    large = 8 + sum(
        ((distance >= threshold).astype(jnp.int32) for threshold in (12, 16, 23, 32, 46, 64, 91))
    )
    inner_bucket = jnp.where(distance < 8, distance, large)
    return inner_bucket + jnp.where(offset > 0, 16, 0)


def learning_rates_plain():
    return (
        (2.0 * (D * DH) ** (-0.5), 2.0 * D ** (-0.5), 2.0 * D ** (-0.5)),
        0.5 * (H * DH / 16) ** (-0.5),
        0.5 * D ** (-0.5),
        2.0 * FF ** (-0.5),
        0.25,
        0.5,
    )


def adam_update(parameter, gradient, first_moment, second_moment, step_rate, clip_factor):
    clipped = gradient * clip_factor
    first_new = beta_first * first_moment + (1.0 - beta_first) * clipped
    second_new = beta_second * second_moment + (1.0 - beta_second) * clipped * clipped
    first_hat = first_new / (1.0 - beta_first**STEP)
    second_hat = second_new / (1.0 - beta_second**STEP)
    updated = parameter - step_rate * (
        first_hat / (jnp.sqrt(second_hat) + adam_eps) + decay_rate * parameter
    )
    return (updated, second_new)


def swap_core(value):
    return lax.ppermute(value, "tensor", [(i, i ^ 1) for i in range(lax.axis_size("tensor"))])


def swap_x(value):
    return lax.ppermute(value, "tensor", [(i, i ^ 2) for i in range(lax.axis_size("tensor"))])


def swap_dp(value, bits):
    return lax.ppermute(value, "dp", [(i, i ^ bits) for i in range(lax.axis_size("dp"))])


def swap_y(value):
    return swap_dp(value, 1)


def over_high(blocks):
    size = lax.axis_size("dp")
    groups = [[index for index in range(size) if index % 2 == bit] for bit in range(2)]
    return lax.all_to_all(blocks, "dp", 0, 0, tiled=True, axis_index_groups=groups)


def row_places():
    rank = lax.axis_index("tensor")
    return (rank, rank ^ 2, rank ^ 1, rank ^ 3)


def bias_tiles(bias_ref, first_head, heads, near_ref):
    span = 2 * NEAR
    lane = lax.broadcasted_iota(i32, (8, span), 1)
    offset = -EDGE - jnp.where(lane < span // 2, lane, lane - span)
    buckets = bucket_of(offset)
    values = [
        jnp.where(offset > 0, bias_ref[31, first_head + h], bias_ref[15, first_head + h])
        for h in range(heads)
    ]
    for bucket in list(range(15)) + list(range(17, 31)):
        here = buckets == bucket
        values = [
            jnp.where(here, bias_ref[bucket, first_head + h], values[h]) for h in range(heads)
        ]
    for h in range(heads):
        line = jnp.broadcast_to(values[h][0:1, :], (NEAR, span))
        near_ref[h] = pltpu.roll(line, 0, 1, stride=1, stride_axis=0)[:, :QB]


def rms_of(values):
    return lax.rsqrt(jnp.mean(values * values, axis=-1, keepdims=True) + norm_eps)


def blocks_of(rows, kind):
    return tuple(ref.at[kind] for ref in rows)


def norm_kernel(keep_ref, got_ref, keep_oth_ref, got_oth_ref, gain_ref, h_ref, token_ref):
    token_ref[...] = jnp.zeros_like(token_ref)
    length = keep_ref.shape[1]
    blocks = blocks_of((keep_ref, got_ref, keep_oth_ref, got_oth_ref), 0)
    for place, block in zip(row_places(), blocks):
        start = pl.multiple_of(place * length, length)
        values = block[...].astype(f32)
        h_ref[pl.ds(start, length), :] = (values * rms_of(values) * gain_ref[0:1, :]).astype(bf16)


def place_weights(pieces, target, kind=None):
    bit = lax.axis_index("dp") % 2
    for index, piece in enumerate(pieces):
        rows = piece.shape[-2]
        lowest = bit if index == 0 else 1 - bit
        for slot in range(piece.shape[0]):
            start = pl.multiple_of((2 * slot + lowest) * rows, 16)
            target[pl.ds(start, rows), :] = piece[slot] if kind is None else piece[slot, kind]


def split_rows(source, own_ref, other_ref):
    rows = own_ref.shape[1]
    bit = lax.axis_index("dp") % 2
    for block in range(own_ref.shape[0]):
        start = pl.multiple_of((2 * block + bit) * rows, 16)
        own_ref[block] = source[pl.ds(start, rows), :]
        start = pl.multiple_of((2 * block + 1 - bit) * rows, 16)
        other_ref[block] = source[pl.ds(start, rows), :]


def sub_sum(values):
    return jnp.sum(values.reshape(values.shape[0] // 8, 8, values.shape[1]), axis=0)


def sub_max(values):
    return jnp.max(values.reshape(values.shape[0] // 8, 8, values.shape[1]), axis=0)


def blocks_even(seq):
    return (seq // QB) % 2 == 0


def near_row(block, chunk):
    start = chunk * KC - block * QB + EDGE
    return start if 0 <= start and start + KC <= NEAR else None


def same_segment(seg_keys, keys, seg_query):
    seg_key = seg_keys[keys, :]
    return jnp.concatenate([seg_key] * (QB // seg_key.shape[1]), axis=1) == seg_query


def segments(seg_ref):
    line = seg_ref[pl.ds(lax.axis_index("tensor") // 2, 1), :]
    return line, jnp.broadcast_to(line, (128, line.shape[1])).T


def one_item(seg_smem_ref):
    side = lax.axis_index("tensor") // 2
    return seg_smem_ref[side, 0] == seg_smem_ref[side, seg_smem_ref.shape[1] - 1]


def head_of(shift, heads):
    return (lax.axis_index("tensor") ^ shift) * heads


def attend_kernel(
    shift, seg_smem_ref, bias_ref, h_ref, piece_a_ref, piece_b_ref, seg_ref,
    wT_ref, qkvT_ref, oT_ref, lse_ref, w_buf, k_buf, s_buf, p_buf, near_ref, segk_ref,
):
    seq = h_ref.shape[0]
    heads = near_ref.shape[0]
    width = oT_ref.shape[0]
    first_head = head_of(shift, heads)
    bias_tiles(bias_ref, first_head, heads, near_ref)
    size = width // heads
    chunks = seq // KC
    assert blocks_even(seq)
    place_weights((piece_a_ref, piece_b_ref), w_buf)
    wT_ref[...] = w_buf[...].T
    qkvT_ref[...] = nt(wT_ref[0 : 3 * width, :], h_ref[...]).astype(bf16)
    blocks = seq // QB

    def rows(part, h):
        return pl.ds(pl.multiple_of(part * width + h * size, size), size)

    def score(h, block):
        s_buf[block % 2] = nn(k_buf[h % 2], qkvT_ref[rows(0, h), block * QB : (block + 1) * QB])

    def soften(h, block, masked):
        slot = block % 2
        qs = slice(block * QB, (block + 1) * QB)
        top = jnp.full((8, QB), -3e38, f32)
        for chunk in range(chunks):
            ks = slice(chunk * KC, (chunk + 1) * KC)
            row = near_row(block, chunk)
            if row is None:
                scores = s_buf[slot, ks, :] + bias_ref[15 if chunk * KC < block * QB else 31, first_head + h]
            else:
                scores = s_buf[slot, ks, :] + near_ref[h, row : row + KC, :]
            if masked:
                scores = jnp.where(same_segment(segk_ref, ks, segq[:, qs]), scores, mask_fill)
            s_buf[slot, ks, :] = scores
            top = jnp.maximum(top, sub_max(scores))
        top = jnp.max(top, axis=0, keepdims=True)
        total = jnp.zeros((8, QB), f32)
        for chunk in range(chunks):
            ks = slice(chunk * KC, (chunk + 1) * KC)
            exps = jnp.exp(s_buf[slot, ks, :] - top)
            s_buf[slot, ks, :] = exps
            total = total + sub_sum(exps)
        total = jnp.sum(total, axis=0, keepdims=True)
        scale = 1.0 / total
        for chunk in range(chunks):
            ks = slice(chunk * KC, (chunk + 1) * KC)
            p_buf[slot, ks, :] = (s_buf[slot, ks, :] * scale).astype(bf16)
        lse_ref[pl.ds(h, 1), qs] = top + jnp.log(total)

    def mix(h, block):
        qs = slice(block * QB, (block + 1) * QB)
        oT_ref[rows(0, h), qs] = nn(qkvT_ref[rows(2, h), :], p_buf[block % 2]).astype(bf16)

    segq, seg_keys = segments(seg_ref)

    def run(masked):
        if masked:
            segk_ref[...] = seg_keys
        k_buf[0] = qkvT_ref[rows(1, 0), :].T
        score(0, 0)

        def head(h, carried):
            for block in range(blocks):
                if block + 1 < blocks:
                    score(h, block + 1)
                else:
                    later = jnp.minimum(h + 1, heads - 1)
                    k_buf[(h + 1) % 2] = qkvT_ref[rows(1, later), :].T
                    s_buf[0] = nn(k_buf[(h + 1) % 2], qkvT_ref[rows(0, later), 0:QB])
                soften(h, block, masked)
                if block:
                    mix(h, block - 1)
            mix(h, blocks - 1)
            return carried

        lax.fori_loop(0, heads, head, 0)

    single = one_item(seg_smem_ref)

    @pl.when(single)
    def _():
        run(False)

    @pl.when(jnp.logical_not(single))
    def _():
        run(True)


def attend(shift, seg, bias, h, pieces):
    seq = h.shape[0]
    cols = pieces[0].shape[2]
    width = cols // 4
    heads = bias.shape[1] // 4
    return call(
        functools.partial(attend_kernel, shift),
        "attend",
        (seg, bias),
        (h, *pieces, seg),
        (sds((cols, D), bf16), sds((3 * width, seq), bf16), sds((width, seq), bf16), sds((8, seq), f32)),
        (
            pltpu.VMEM((D, cols), bf16),
            pltpu.VMEM((2, seq, width // heads), bf16),
            pltpu.VMEM((2, seq, QB), f32),
            pltpu.VMEM((2, seq, QB), bf16),
            pltpu.VMEM((heads, NEAR, QB), f32),
            pltpu.VMEM((seq, 128), i32),
        ),
    )


def attend_back_kernel(
    shift, seg_smem_ref, bias_ref, qkvT_ref, doT_ref, lse_ref, seg_ref, h_ref, goT_ref,
    dqkvT_ref, own_ref, other_ref, dbias_ref,
    kv_buf, s_buf, dp_buf, ds_buf, pt_buf, dt_buf, dk_buf, dv_buf, g_buf, near_ref, segk_ref,
    dnear_ref, dfar_ref, line_buf,
):
    width, seq = doT_ref.shape
    heads = near_ref.shape[0]
    first_head = head_of(shift, heads)
    bias_tiles(bias_ref, first_head, heads, near_ref)
    segq, seg_keys = segments(seg_ref)
    size = width // heads
    blocks = seq // QB
    chunks = seq // KC
    assert blocks_even(seq)

    def rows(part, h):
        return pl.ds(pl.multiple_of(part * width + h * size, size), size)

    def key_values(h, turn):
        kv_buf[turn] = jnp.concatenate([qkvT_ref[rows(1, h), :], qkvT_ref[rows(2, h), :]], axis=0).T

    def products(h, turn, block):
        slot = block % 2
        qs = slice(block * QB, (block + 1) * QB)
        zeros = jnp.zeros((size, QB), bf16)
        s_buf[slot] = nn(kv_buf[turn], jnp.concatenate([qkvT_ref[rows(0, h), qs], zeros], axis=0))
        dp_buf[slot] = nn(kv_buf[turn], jnp.concatenate([zeros, doT_ref[rows(0, h), qs]], axis=0))

    def soften(h, block, masked):
        slot = block % 2
        qs = slice(block * QB, (block + 1) * QB)
        lse = lse_ref[pl.ds(h, 1), qs]
        lse_left = lse - bias_ref[15, first_head + h]
        lse_right = lse - bias_ref[31, first_head + h]
        dots = jnp.zeros((8, QB), f32)
        for chunk in range(chunks):
            ks = slice(chunk * KC, (chunk + 1) * KC)
            row = near_row(block, chunk)
            if row is None:
                scores = s_buf[slot, ks, :] - (lse_left if chunk * KC < block * QB else lse_right)
            else:
                scores = s_buf[slot, ks, :] + near_ref[h, row : row + KC, :] - lse
            probs = jnp.exp(scores)
            if masked:
                probs = jnp.where(same_segment(segk_ref, ks, segq[:, qs]), probs, 0.0)
            s_buf[slot, ks, :] = probs
            pt_buf[slot, :, ks] = probs.astype(bf16).T
            dots = dots + sub_sum(probs * dp_buf[slot, ks, :])
        dots = jnp.sum(dots, axis=0, keepdims=True)
        for chunk in range(chunks):
            ks = slice(chunk * KC, (chunk + 1) * KC)
            d_scores = (s_buf[slot, ks, :] * (dp_buf[slot, ks, :] - dots)).astype(bf16)
            ds_buf[slot, ks, :] = d_scores
            dt_buf[slot, :, ks] = d_scores.T
            row = near_row(block, chunk)
            if row is not None:
                if block == 0 or (block == 1 and row == 0):
                    dnear_ref[h, row : row + KC, :] = d_scores.astype(f32)
                else:
                    dnear_ref[h, row : row + KC, :] += d_scores.astype(f32)

    def outputs(h, block):
        slot = block % 2
        qs = slice(block * QB, (block + 1) * QB)
        dqkvT_ref[rows(0, h), qs] = nn(qkvT_ref[rows(1, h), :], ds_buf[slot]).astype(bf16)
        d_keys = nn(
            jnp.concatenate([qkvT_ref[rows(0, h), qs], jnp.ones((16, QB), bf16)], axis=0),
            dt_buf[slot],
        )
        d_values = nn(doT_ref[rows(0, h), qs], pt_buf[slot])
        if block == 0:
            dk_buf[...] = d_keys[0:size]
            dv_buf[...] = d_values
        elif block + 1 < blocks:
            dk_buf[...] += d_keys[0:size]
            dv_buf[...] += d_values
        else:
            dqkvT_ref[rows(1, h), :] = (dk_buf[...] + d_keys[0:size]).astype(bf16)
            dqkvT_ref[rows(2, h), :] = (dv_buf[...] + d_values).astype(bf16)
        sums = d_keys[size : size + 1]
        left_end = max(0, block * QB - EDGE)
        right_start = min(seq, block * QB + QB + EDGE)
        lane = lax.broadcasted_iota(i32, (1, 128), 1)
        line = jnp.zeros((1, 128), f32)
        if left_end:
            line = jnp.where(lane == 0, jnp.sum(sums[:, :left_end], axis=1, keepdims=True), line)
        if right_start < seq:
            line = jnp.where(lane == 1, jnp.sum(sums[:, right_start:], axis=1, keepdims=True), line)
        if block == 0:
            dfar_ref[pl.ds(h, 1), :] = line
        else:
            dfar_ref[pl.ds(h, 1), :] += line

    def run(masked):
        if masked:
            segk_ref[...] = seg_keys
        key_values(0, 0)
        products(0, 0, 0)

        def head(h, carried):
            for block in range(blocks):
                if block + 1 < blocks:
                    products(h, h % 2, block + 1)
                else:
                    later = jnp.minimum(h + 1, heads - 1)
                    key_values(later, (h + 1) % 2)
                    products(later, (h + 1) % 2, 0)
                soften(h, block, masked)
                if block:
                    outputs(h, block - 1)
            outputs(h, blocks - 1)
            return carried

        lax.fori_loop(0, heads, head, 0)

    single = one_item(seg_smem_ref)

    @pl.when(single)
    def _():
        run(False)

    @pl.when(jnp.logical_not(single))
    def _():
        run(True)

    dfar_ref[heads:, :] = jnp.zeros((8 - heads, 128), f32)
    grad = jnp.concatenate([nn(dqkvT_ref[...], h_ref[...]).astype(bf16), goT_ref[...]], axis=0)
    if other_ref is None:
        own_ref[...] = grad.T
    else:
        g_buf[...] = grad.T
        split_rows(g_buf, own_ref, other_ref)
    bias_gradients(dnear_ref, dfar_ref, line_buf, dbias_ref)


def attend_back(shift, seg, bias, qkvT, doT, lse, h, goT, grad_outs, gates):
    width, seq = doT.shape
    heads = bias.shape[1] // 4
    size = width // heads
    body = functools.partial(attend_back_kernel, shift)
    if len(grad_outs) == 1:

        def body(*refs):
            attend_back_kernel(shift, *refs[:10], None, *refs[10:])

    return call(
        body,
        "attend_back",
        (seg, bias),
        (qkvT, doT, lse, seg, h, goT),
        (sds(qkvT.shape, bf16), *grad_outs, sds((8, 128), f32)),
        (
            pltpu.VMEM((2, seq, 2 * size), bf16),
            pltpu.VMEM((2, seq, QB), f32),
            pltpu.VMEM((2, seq, QB), f32),
            pltpu.VMEM((2, seq, QB), bf16),
            pltpu.VMEM((2, QB, seq), bf16),
            pltpu.VMEM((2, QB, seq), bf16),
            pltpu.VMEM((size, seq), f32),
            pltpu.VMEM((size, seq), f32),
            pltpu.VMEM((D, 4 * width), bf16),
            pltpu.VMEM((heads, NEAR, QB), f32),
            pltpu.VMEM((seq, 128), i32),
            pltpu.VMEM((heads, NEAR, QB), f32),
            pltpu.VMEM((8, 128), f32),
            pltpu.VMEM((8, 2 * NEAR), f32),
        ),
        gates,
    )


def project_kernel(oT0_ref, oT1_ref, wT0_ref, wT1_ref, keep_ref, send_ref, o_buf):
    width = oT0_ref.shape[0]
    length = keep_ref.shape[0] // 2
    o_buf[...] = jnp.concatenate([oT0_ref[...], oT1_ref[...]], axis=0).T
    w = jnp.concatenate([wT0_ref[3 * width :, :], wT1_ref[3 * width :, :]], axis=0)
    for index, place in enumerate(row_places()):
        start = pl.multiple_of(place * length, length)
        part = nn(o_buf[pl.ds(start, length), :], w)
        rows = slice((index % 2) * length, (index % 2 + 1) * length)
        if index < 2:
            keep_ref[rows, :] = part
        else:
            send_ref[rows, :] = part.astype(send_ref.dtype)


def middle_kernel(keep_row_ref, got_row_ref, part_ref, got_ref, gain_ref, x2_ref, h_ref):
    length = keep_row_ref.shape[1]
    for index, block in enumerate((keep_row_ref.at[0], got_row_ref.at[0])):
        rows = slice(index * length, (index + 1) * length)
        values = block[...].astype(f32) + part_ref[rows, :] + got_ref[rows, :].astype(f32)
        x2_ref[rows, :] = values
        h_ref[rows, :] = (values * rms_of(values) * gain_ref[1:2, :]).astype(bf16)


def split3(values):
    high = values.astype(bf16)
    rest = values - high.astype(f32)
    mid = rest.astype(bf16)
    low = (rest - mid.astype(f32)).astype(bf16)
    return high, mid, low


def feed_rows(h, cot, u_buf, d_buf, act_ref, dpre_ref, rows):
    pre = nn(h, u_buf[...])
    d_act = nn(cot, d_buf[...])
    square = pre * pre
    bent = jnp.tanh(gelu_scale * pre * (1.0 + gelu_cubic * square))
    half_up = 0.5 * (1.0 + bent)
    act_ref[rows, :] = (pre * half_up).astype(bf16)
    slope = half_up + (0.5 * gelu_scale) * pre * (1.0 - bent * bent) * (
        1.0 + (3.0 * gelu_cubic) * square
    )
    d_pre = (d_act * slope).astype(bf16)
    dpre_ref[rows, :] = d_pre
    return nt(d_pre, u_buf[...])


def pooled_units(hot, act_ref, d_buf):
    pooled = None
    for term in split3(nn(hot, act_ref[...])):
        part = nt(term, d_buf[...])
        pooled = part if pooled is None else pooled + part
    return pooled


def weight_grads(h_refs, cots, act_ref, dpre_ref, outs, g_buf):
    hT = jnp.concatenate([ref[...] for ref in h_refs], axis=0).T
    cotT = jnp.concatenate([block[...] for block in cots], axis=0).T
    if len(outs) == 2:
        outs[0][...] = nn(hT, dpre_ref[...]).astype(bf16)
        outs[1][...] = nn(cotT, act_ref[...]).astype(bf16)
    else:
        g_buf[0] = nn(hT, dpre_ref[...]).astype(bf16)
        split_rows(g_buf.at[0], outs[0], outs[1])
        g_buf[1] = nn(cotT, act_ref[...]).astype(bf16)
        split_rows(g_buf.at[1], outs[2], outs[3])


def feed_own_kernel(
    h_own_ref, h_oth_ref, keep_ref, got_ref, keep_oth_ref, got_oth_ref,
    a_ref, b_ref, seg_ref, x2_ref, dh_ref, pooled_ref, hot_ref, *refs
):
    *outs, u_buf, d_buf, act_buf, dpre_buf, g_buf = refs
    place_weights((a_ref, b_ref), u_buf, 0)
    place_weights((a_ref, b_ref), d_buf, 1)
    length = keep_ref.shape[1]
    cots = blocks_of((keep_ref, got_ref, keep_oth_ref, got_oth_ref), 1)
    line = seg_ref[pl.ds(lax.axis_index("tensor") // 2, 1), :]
    seq = line.shape[1]
    item = lax.broadcasted_iota(i32, (SEGS, seq), 0)
    whole = (jnp.broadcast_to(line, (SEGS, seq)) == item).astype(f32)
    for index, place in enumerate(row_places()):
        part = jnp.zeros((SEGS, length), f32)
        for block in range(4):
            part = jnp.where(place == block, whole[:, block * length : (block + 1) * length], part)
        hot_ref[:, index * length : (index + 1) * length] = part.astype(bf16)
    for index in range(4):
        rows = slice(index * length, (index + 1) * length)
        half = slice((index % 2) * length, (index % 2 + 1) * length)
        h = (h_own_ref if index < 2 else h_oth_ref)[half, :]
        dh_ref[rows, :] = feed_rows(h, cots[index][...], u_buf, d_buf, act_buf, dpre_buf, rows)
    hot = hot_ref[...]
    pooled = pooled_units(hot, act_buf, d_buf)
    for term in split3(x2_ref[...]):
        pooled = pooled + nn(hot[:, 0 : 2 * length], term)
    pooled_ref[...] = pooled
    weight_grads((h_own_ref, h_oth_ref), cots, act_buf, dpre_buf, outs, g_buf)


def feed_other_kernel(
    h_own_ref, h_oth_ref, keep_ref, got_ref, keep_oth_ref, got_oth_ref,
    a_ref, ub_ref, db_ref, hot_ref, dh_ref, pool_ref,
    part_ref, send_ref, pooled_ref, *refs
):
    *outs, u_buf, d_buf, act_buf, dpre_buf, g_buf = refs
    place_weights((a_ref,), u_buf, 0)
    place_weights((a_ref,), d_buf, 1)
    bit = lax.axis_index("dp") % 2
    for source, target in ((ub_ref, u_buf), (db_ref, d_buf)):
        count = source.shape[1]
        for slot in range(source.shape[0]):
            start = pl.multiple_of((2 * slot + 1 - bit) * count, 16)
            target[pl.ds(start, count), :] = source[slot]
    length = keep_ref.shape[1]
    cots = blocks_of((keep_ref, got_ref, keep_oth_ref, got_oth_ref), 1)
    for index in (2, 3, 0, 1):
        rows = slice(index * length, (index + 1) * length)
        half = slice((index % 2) * length, (index % 2 + 1) * length)
        h = (h_own_ref if index < 2 else h_oth_ref)[half, :]
        total = dh_ref[rows, :] + feed_rows(
            h, cots[index][...], u_buf, d_buf, act_buf, dpre_buf, rows
        )
        if index < 2:
            part_ref[half, :] = total
        else:
            send_ref[half, :] = total.astype(send_ref.dtype)
    pooled_ref[...] = pool_ref[...] + pooled_units(hot_ref[...], act_buf, d_buf)
    weight_grads((h_own_ref, h_oth_ref), cots, act_buf, dpre_buf, outs, g_buf)


def norm_back(values, gain, upstream):
    scale = rms_of(values)
    normed = values * scale
    gain_grad = jnp.sum(upstream * normed, axis=0, keepdims=True)
    scaled = upstream * gain
    inner = jnp.mean(scaled * normed, axis=-1, keepdims=True)
    return scale * (scaled - normed * inner), gain_grad


def middle_back_kernel(
    x2_ref, part_ref, got_ref, keep_row_ref, got_row_ref, gain_ref, dx2_ref, da_ref, gain_grad_ref
):
    length = x2_ref.shape[0] // 2
    for index, cot in enumerate((keep_row_ref.at[1], got_row_ref.at[1])):
        rows = slice(index * length, (index + 1) * length)
        d_values, gain_grad = norm_back(
            x2_ref[rows, :], gain_ref[1:2, :], part_ref[rows, :] + got_ref[rows, :].astype(f32)
        )
        dx2 = cot[...].astype(f32) + d_values
        dx2_ref[rows, :] = dx2
        da_ref[rows, :] = dx2.astype(bf16)
        if index == 0:
            gain_grad_ref[...] = gain_grad
        else:
            gain_grad_ref[...] += gain_grad


def branch_back_kernel(
    da_own_ref, da_oth_ref, wT0_ref, wT1_ref, oT0_ref, oT1_ref,
    doT0_ref, doT1_ref, g0_ref, g1_ref, da_buf,
):
    width = oT0_ref.shape[0]
    length = da_own_ref.shape[0] // 2
    for index, place in enumerate(row_places()):
        start = pl.multiple_of(place * length, length)
        half = slice((index % 2) * length, (index % 2 + 1) * length)
        da_buf[pl.ds(start, length), :] = (da_own_ref if index < 2 else da_oth_ref)[half, :]
    da = da_buf[...]
    doT0_ref[...] = nt(wT0_ref[3 * width :, :], da).astype(bf16)
    doT1_ref[...] = nt(wT1_ref[3 * width :, :], da).astype(bf16)
    g0_ref[...] = nn(oT0_ref[...], da).astype(bf16)
    g1_ref[...] = nn(oT1_ref[...], da).astype(bf16)


def first_back_kernel(d0_ref, d1_ref, wT0_ref, wT1_ref, keep_ref, send_ref, d_buf):
    rows3 = d0_ref.shape[0]
    length = keep_ref.shape[0] // 2
    d_buf[...] = jnp.concatenate([d0_ref[...], d1_ref[...]], axis=0).T
    w = jnp.concatenate([wT0_ref[0:rows3, :], wT1_ref[0:rows3, :]], axis=0)
    places = row_places()
    for index in (2, 3, 0, 1):
        start = pl.multiple_of(places[index] * length, length)
        part = nn(d_buf[pl.ds(start, length), :], w)
        rows = slice((index % 2) * length, (index % 2 + 1) * length)
        if index < 2:
            keep_ref[rows, :] = part
        else:
            send_ref[rows, :] = part.astype(send_ref.dtype)


def token_grad_kernel(
    keep_row_ref, got_row_ref, part_ref, got_ref, dx2_ref, gain_ref, pool_ref, pool_got_ref, hot_ref,
    own_ref, away_ref, gain_grad_ref, mean_ref
):
    length = keep_row_ref.shape[1]
    away_ref[length:, :] = jnp.zeros((away_ref.shape[0] - length, away_ref.shape[1]), bf16)
    counts = jnp.sum(hot_ref[...].astype(f32), axis=1, keepdims=True)
    means = (pool_ref[...] + pool_got_ref[...]) / jnp.maximum(counts, 1.0)
    rank = lax.axis_index("tensor")
    width = mean_ref.shape[1]
    mine, sent = jnp.zeros(mean_ref.shape, f32), jnp.zeros(mean_ref.shape, f32)
    for shard in range(4):
        part = means[:, shard * width : (shard + 1) * width]
        mine = jnp.where(rank == shard, part, mine)
        sent = jnp.where(rank ^ 2 == shard, part, sent)
    mean_ref[...] = mine
    away_ref[length:, 0:width] = sent.astype(bf16)
    for index, block in enumerate((keep_row_ref.at[0], got_row_ref.at[0])):
        rows = slice(index * length, (index + 1) * length)
        d_values, gain_grad = norm_back(
            block[...].astype(f32), gain_ref[0:1, :], part_ref[rows, :] + got_ref[rows, :].astype(f32)
        )
        if index == 0:
            own_ref[...] = dx2_ref[rows, :] + d_values
            gain_grad_ref[...] = gain_grad
        else:
            away_ref[0:length, :] = (dx2_ref[rows, :] + d_values).astype(bf16)
            gain_grad_ref[...] += gain_grad


def bias_gradients(dnear_ref, dfar_ref, line_buf, grad_ref):
    heads = dnear_ref.shape[0]
    span = 2 * NEAR
    line_buf[...] = jnp.zeros_like(line_buf)
    for h in range(heads):
        values = dnear_ref[h]
        rows = NEAR
        while rows > 1:
            rows //= 2
            low, high = values[:rows], values[rows:]
            if rows % 128 == 0:
                pad = jnp.zeros((rows, rows), f32)
                values = jnp.concatenate([pad, low], axis=1) + jnp.concatenate([high, pad], axis=1)
            else:
                if values.shape[1] < span:
                    pad = jnp.zeros((rows, span - values.shape[1]), f32)
                    low = jnp.concatenate([pad, low], axis=1)
                    high = jnp.concatenate([pad, high], axis=1)
                values = low + pltpu.roll(high, span - rows, 1)
        line_buf[h : h + 1, :] = values
    lines = line_buf[...]
    col = lax.broadcasted_iota(i32, lines.shape, 1)
    buckets = bucket_of(span - QB - EDGE - col)
    far = dfar_ref[...]
    lane = lax.broadcasted_iota(i32, (8, 128), 1)
    left = jnp.sum(jnp.where(lane == 0, far, 0.0), axis=1, keepdims=True)
    right = jnp.sum(jnp.where(lane == 1, far, 0.0), axis=1, keepdims=True)
    grad = jnp.where(lane == 15, left, jnp.where(lane == 31, right, 0.0))
    for bucket in range(32):
        if bucket != 16:
            total = jnp.sum(jnp.where(buckets == bucket, lines, 0.0), axis=1, keepdims=True)
            grad = jnp.where(lane == bucket, grad + total, grad)
    grad_ref[...] = grad


def pack_kernel(qkv_ref, out_ref, tokens_ref, cot_ref, pack_ref, keep_ref, send_ref):
    packed = jnp.concatenate([qkv_ref[0], qkv_ref[1], qkv_ref[2], out_ref[...].T], axis=1).astype(bf16)
    for slot in range(pack_ref.shape[0]):
        pack_ref[slot] = packed
    rows_kernel(tokens_ref, cot_ref, keep_ref, send_ref)


def pack_ud_kernel(up_ref, down_ref, pack_ref):
    up, down = up_ref[...].astype(bf16), down_ref[...].astype(bf16)
    for slot in range(pack_ref.shape[0]):
        pack_ref[slot, 0] = up
        pack_ref[slot, 1] = down


def rows_kernel(tokens_ref, cot_ref, keep_ref, send_ref):
    side = lax.axis_index("tensor") // 2
    keep_ref[0] = tokens_ref[side]
    keep_ref[1] = cot_ref[side]
    send_ref[0] = tokens_ref[1 - side]
    send_ref[1] = cot_ref[1 - side]


def place_kernel(own_ref, got_ref, mean_ref, out_ref, pooled_ref):
    side = lax.axis_index("tensor") // 2
    length, width = own_ref.shape[0], mean_ref.shape[1]
    out_ref[side] = own_ref[...]
    out_ref[1 - side] = got_ref[0:length, :].astype(f32)
    pooled_ref[side] = mean_ref[...]
    pooled_ref[1 - side] = got_ref[length:, 0:width].astype(f32)


def relay_kernel(*refs):
    for source_ref, out_ref in zip(refs[: len(refs) // 2], refs[len(refs) // 2 :]):
        out_ref[...] = source_ref[...]


def pick_kernel(from_x_ref, from_y_ref, up_ref, down_ref):
    up_ref[...] = from_x_ref[:, 0]
    down_ref[...] = from_y_ref[:, 1]


def total_of(refs):
    total = refs[0][...].astype(f32)
    for ref in refs[1:]:
        total = total + ref[...].astype(f32)
    return total


def add_kernel(*refs):
    *terms, sum_ref, token_ref = refs
    sum_ref[...] = total_of(terms).astype(bf16)
    token_ref[...] = jnp.zeros_like(token_ref)


def send_kernel(*refs):
    *terms, own_ref, sent1_ref, sent2_ref, sent3_ref, token_ref, sum_buf = refs
    sum_buf[...] = total_of(terms)
    place = lax.axis_index("dp") // 2
    own_ref[...] = sum_buf[place]
    for bits, ref in ((1, sent1_ref), (2, sent2_ref), (3, sent3_ref)):
        ref[...] = sum_buf[place ^ bits].astype(bf16)
    token_ref[...] = jnp.zeros_like(token_ref)


def add_pairs_kernel(up_ref, up_got_ref, down_ref, down_got_ref, up_sum_ref, down_sum_ref, token_ref):
    up_sum_ref[...] = total_of((up_ref, up_got_ref)).astype(bf16)
    down_sum_ref[...] = total_of((down_ref, down_got_ref)).astype(bf16)
    token_ref[...] = jnp.zeros_like(token_ref)


def sum_blocks(ref):
    total = ref[0].astype(f32)
    for slot in range(1, ref.shape[0]):
        total = total + ref[slot].astype(f32)
    return total


def finish_kernel(*refs):
    *terms, grad_ref, squares_ref = refs
    total = total_of(terms) if len(terms) > 1 else sum_blocks(terms[0])
    grad_ref[...] = total
    squares_ref[...] = jnp.broadcast_to(jnp.sum(total * total, axis=(0, 1), keepdims=True), (8, 128))


def finish_a_kernel(*refs):
    *terms, up_ref, down_ref, qkv_ref, out_ref, squares_ref = refs
    total = total_of(terms) if len(terms) > 1 else sum_blocks(terms[0])
    width = qkv_ref.shape[2]
    for part in range(3):
        qkv_ref[part] = total[:, part * width : (part + 1) * width]
    out_ref[...] = total[:, 3 * width :].T
    squares = up_ref[...] + down_ref[...] + jnp.sum(total * total, axis=(0, 1), keepdims=True)
    for slot in range(squares_ref.shape[0]):
        squares_ref[slot] = squares


def small_kernel(first_ref, second_ref, own_bias_ref, other_bias_ref, out_ref):
    lines = D // 128
    heads = (out_ref.shape[1] - 2 * lines) // 4
    out_ref[0] = jnp.zeros(out_ref.shape[1:], f32)
    for kind, ref in enumerate((first_ref, second_ref)):
        for line in range(lines):
            out_ref[0, kind * lines + line : kind * lines + line + 1, :] = ref[
                :, line * 128 : (line + 1) * 128
            ]
    for shift, ref in ((0, own_bias_ref), (2, other_bias_ref)):
        start = 2 * lines + head_of(shift, heads)
        for h in range(heads):
            out_ref[0, pl.ds(start + h, 1), :] = ref[h : h + 1, :]
    value = out_ref[0]
    for slot in range(1, out_ref.shape[0]):
        out_ref[slot] = value


def adam_kernel(small_ref, squares_ref, *refs):
    *refs, sems = refs
    sources, refs = refs[:22], refs[23:]
    outs, refs = refs[:15], refs[15:]
    copies = [
        pltpu.make_async_copy(source, target, sems.at[index])
        for index, (source, target) in enumerate(zip(sources, refs))
    ]
    for copy in copies:
        copy.start()
    small = jnp.sum(small_ref[...], axis=0)
    lines = D // 128
    gains_ref, bias_ref, norm_ref = outs[12:]
    for kind in range(2):
        for line in range(lines):
            gains_ref[kind : kind + 1, line * 128 : (line + 1) * 128] = small[
                kind * lines + line : kind * lines + line + 1
            ]
    bias_ref[...] = small[2 * lines :, 0 : bias_ref.shape[1]]
    total = jnp.sum(squares_ref[...], axis=0)[0:1, 0:1]
    norm = jnp.sqrt(total + jnp.sum(small * small, axis=(0, 1), keepdims=True))
    norm_ref[0, 0] = jnp.max(norm)
    clip = jnp.minimum(1.0, clip_level / norm)
    for copy in copies:
        copy.wait()
    rates = learning_rates_plain()
    params = [refs[4 * index : 4 * index + 4] for index in range(4)]
    params.append((refs[16], gains_ref, refs[17], refs[18]))
    params.append((refs[19], bias_ref, refs[20], refs[21]))
    for index, (param, grad, first, second) in enumerate(params):
        new, new_second = outs[2 * index], outs[2 * index + 1]
        if isinstance(rates[index], tuple):
            for part, rate in enumerate(rates[index]):
                value, moment = adam_update(
                    param[part], grad[part], first[part], second[part], rate, clip
                )
                new[part] = value
                new_second[part] = moment
        else:
            value, moment = adam_update(
                param[...], grad[...], first[...], second[...], rates[index], clip
            )
            new[...] = value
            new_second[...] = moment


def per_device(
    tokens,
    segment_ids,
    cotangent,
    qkv_master,
    out_master,
    up_master,
    down_master,
    norm_gains,
    position_bias,
    qkv_first,
    qkv_second,
    out_first,
    out_second,
    up_first,
    up_second,
    down_first,
    down_second,
    gain_first,
    gain_second,
    bias_first,
    bias_second,
):
    rank = lax.axis_index("tensor")
    dp_rank = lax.axis_index("dp")
    dp_size = lax.axis_size("dp")
    row_bit = dp_rank % 2
    rows, length = tokens.shape[0], tokens.shape[1]
    seq = segment_ids.shape[1]
    shard_rows, width = qkv_master.shape[1], qkv_master.shape[2]
    units = up_master.shape[1]
    half = (seq // 2, D)
    assert rows == 2 and lax.axis_size("tensor") == 4 and seq == 4 * length
    high = dp_size // 2
    aligned = shard_rows % 16 == 0

    if aligned:
        pack_a, keep_rows, sent_rows = call(
            pack_kernel,
            "pack_a",
            (),
            (qkv_master, out_master, tokens, cotangent),
            (sds((high, shard_rows, D), bf16),) + (sds((2, length, D), bf16),) * 2,
            limit=FULL_LIMIT,
        )
        order = lambda pair: pair
        blocks_out = (sds((high, shard_rows, D), bf16),) * 2
    else:
        packed = jnp.concatenate([*qkv_master, out_master.T], axis=1).astype(bf16)
        pack_a = jnp.broadcast_to(packed, (high,) + packed.shape)
        blocks_out = (sds((D, D), bf16),)
        keep_rows, sent_rows = call(
            rows_kernel, "rows", (), (tokens, cotangent), (sds((2, length, D), bf16),) * 2
        )

        def order(pair):
            own, other = pair
            first = jnp.where(row_bit == 0, own, other)
            second = jnp.where(row_bit == 0, other, own)
            both = jnp.moveaxis(jnp.stack([first, second], axis=1), (0, 1), (-4, -3))
            both = both.reshape(both.shape[:-4] + (D, both.shape[-1]))
            lower, upper = both[..., : D // 2, :], both[..., D // 2 :, :]
            return (
                jnp.where(row_bit == 0, lower, upper)[None],
                jnp.where(row_bit == 0, upper, lower)[None],
            )

    high_a = over_high(pack_a)
    got_rows = swap_x(sent_rows)
    all_rows = (keep_rows, got_rows, swap_core(keep_rows), swap_core(got_rows))
    a_y = swap_y(high_a)
    a_x = swap_x(high_a)
    h1, token = call(
        norm_kernel,
        "first_norm",
        (),
        (*all_rows, norm_gains),
        (sds((seq, D), bf16), sds((8, 128), f32)),
    )
    (pack_ud,) = call(
        pack_ud_kernel,
        "pack_ud",
        (),
        (up_master, down_master.T),
        (sds((high, 2, shard_rows, units), bf16),),
        gates=(token,),
    )
    high_ud = over_high(pack_ud)

    a_other = (a_x, swap_y(a_x))
    wT0, qkvT0, oT0, lse0 = attend(0, segment_ids, position_bias, h1, order((high_a, a_y)))
    (relay_ud,) = call(relay_kernel, "relay_ud", (), (high_ud,), (sds(high_ud.shape, bf16),), gates=(lse0,))
    ud_x = swap_x(relay_ud)
    ud_y = swap_y(relay_ud)
    wT1, qkvT1, oT1, lse1 = attend(2, segment_ids, position_bias, h1, order(a_other))

    keep, send = call(
        project_kernel,
        "project",
        (),
        (oT0, oT1, wT0, wT1),
        (sds(half, f32), sds(half, bf16)),
        (pltpu.VMEM((seq, 2 * width), bf16),),
    )
    x2, h2 = call(
        middle_kernel,
        "second_norm",
        (),
        (keep_rows, got_rows, keep, swap_core(send), norm_gains),
        (sds(half, f32), sds(half, bf16)),
    )
    h2_other = swap_core(h2)
    picked_u, picked_d = call(
        pick_kernel,
        "pick_ud",
        (),
        (ud_x, ud_y),
        (sds((high, shard_rows, units), bf16),) * 2,
        gates=(h2,),
    )
    u_xy = swap_y(picked_u)
    d_xy = swap_x(picked_d)

    def of_y(grad, wanted):
        blocks = grad.reshape((high, 2, shard_rows) + grad.shape[1:])
        return lax.dynamic_index_in_dim(blocks, wanted, 1, keepdims=False)

    def by_y(grads):
        if aligned:
            return tuple(grads)
        return tuple(of_y(grad, wanted) for grad in grads for wanted in (row_bit, 1 - row_bit))

    def plus(name, *terms, gates=()):
        outs = (sds(terms[0].shape, bf16), sds((8, 128), f32))
        return call(add_kernel, name, (), terms, outs, gates=gates)

    def over_high_bits(name, *terms, gates=()):
        if high != 4:
            total, token = plus(name, *terms, gates=gates)
            return (over_high(total),), token
        block = terms[0].shape[1:]
        own, *sent, token = call(
            send_kernel,
            name,
            (),
            terms,
            (sds(block, f32),) + (sds(block, bf16),) * 3 + (sds((8, 128), f32),),
            (pltpu.VMEM(terms[0].shape, f32),),
            gates=gates,
        )
        return (own, *(swap_dp(piece, 2 * bits) for bits, piece in enumerate(sent, 1))), token

    feed_scratch = (
        *([pltpu.VMEM((D, units), bf16)] * 2),
        *([pltpu.VMEM((seq, units), bf16)] * 2),
        pltpu.VMEM((2, D, units), bf16),
    )
    dh_part, pool_part, hot, *grads = call(
        feed_own_kernel,
        "feed_own",
        (),
        (h2, h2_other, *all_rows, *order((relay_ud, ud_y)), segment_ids, x2),
        (sds((seq, D), f32), sds((SEGS, D), f32), sds((SEGS, seq), bf16), *blocks_out, *blocks_out),
        feed_scratch,
        limit=FEED_LIMIT,
    )
    gu0_own, gu0_oth, gd0_own, gd0_oth = by_y(grads)
    if aligned:
        ud_other = (ud_x, u_xy, d_xy)
    else:
        first, second = order((ud_x, jnp.stack([u_xy, d_xy], axis=1)))
        ud_other = (first, second[:, 0], second[:, 1])
    keep, send, pool_part, *grads = call(
        feed_other_kernel,
        "feed_other",
        (),
        (h2, h2_other, *all_rows, *ud_other, hot, dh_part, pool_part),
        (sds(half, f32), sds(half, bf16), sds((SEGS, D), f32), *blocks_out, *blocks_out),
        feed_scratch,
        limit=FEED_LIMIT,
    )
    got = swap_core(send)
    gu1_own, gu1_oth, gd1_own, gd1_oth = by_y(grads)
    up_y1 = swap_y(gu1_oth)
    down_x1 = swap_x(gd1_oth)
    dx2, da, gain_grad_second = call(
        middle_back_kernel,
        "second_norm_back",
        (),
        (x2, keep, got, keep_rows, got_rows, norm_gains),
        (sds(half, f32), sds(half, bf16), sds((1, D), f32)),
        work=10,
    )
    da_other = swap_core(da)
    doT0, doT1, goT0, goT1 = call(
        branch_back_kernel,
        "branch_back",
        (),
        (da, da_other, wT0, wT1, oT0, oT1),
        (sds((width, seq), bf16),) * 2 + (sds((width, D), bf16),) * 2,
        (pltpu.VMEM((seq, D), bf16),),
        work=10,
    )
    up_late, down_late = call(
        relay_kernel,
        "relay_grads",
        (),
        (gu0_oth, gd1_own),
        (sds(gu0_oth.shape, bf16),) * 2,
        gates=(doT0,),
    )
    up_y0 = swap_y(up_late)
    down_x0 = swap_x(down_late)
    dqkvT1, *ga1, dbias1 = attend_back(
        2, segment_ids, position_bias, qkvT1, doT1, lse1, h1, goT1, blocks_out, ()
    )
    up_add, down_add, token = call(
        add_pairs_kernel,
        "add_ud",
        (),
        (gu1_own, up_y1, gd0_oth, down_x1),
        (sds(gu1_own.shape, bf16),) * 2 + (sds((8, 128), f32),),
        gates=(dbias1,),
    )
    up_x = swap_x(up_add)
    down_y = swap_y(down_add)
    ga1_own, ga1_oth = by_y(ga1)
    a_y1 = swap_y(ga1_oth)
    dqkvT0, *ga0, dbias0 = attend_back(
        0, segment_ids, position_bias, qkvT0, doT0, lse0, h1, goT0, blocks_out, (token,)
    )
    ga0_own, ga0_oth = by_y(ga0)
    a_y0 = swap_y(ga0_oth)
    up_pieces, token = over_high_bits("total_up", gu0_own, up_y0, up_x, gates=(dbias0,))
    down_pieces, token = over_high_bits("total_down", gd0_own, down_x0, down_y, gates=(token,))
    a_add, token = plus("add_a", ga1_own, a_y1, gates=(token,))
    a_x1 = swap_x(a_add)
    keep, send = call(
        first_back_kernel,
        "first_back",
        (),
        (dqkvT0, dqkvT1, wT0, wT1),
        (sds(half, f32), sds(half, bf16)),
        (pltpu.VMEM((seq, 6 * width), bf16),),
        gates=(token,),
    )
    first_got = swap_core(send)
    tg_own, tg_away, gain_grad_first, mean_keep = call(
        token_grad_kernel,
        "first_norm_back",
        (),
        (keep_rows, got_rows, keep, first_got, dx2, norm_gains, pool_part, swap_core(pool_part), hot),
        (
            sds((length, D), f32),
            sds((length + SEGS, D), bf16),
            sds((1, D), f32),
            sds((SEGS, width), f32),
        ),
        work=10,
    )
    tg_got = swap_x(tg_away)
    a_pieces, _ = over_high_bits("total_a", ga0_own, a_y0, a_x1, gates=(gain_grad_first,))
    grad_up, up_squares = call(
        finish_kernel,
        "finish_up",
        (),
        up_pieces,
        (sds((shard_rows, units), f32), sds((8, 128), f32)),
        gates=(gain_grad_first,),
        work=10,
    )
    grad_downT, down_squares = call(
        finish_kernel,
        "finish_down",
        (),
        down_pieces,
        (sds((shard_rows, units), f32), sds((8, 128), f32)),
        gates=(gain_grad_first,),
        work=10,
    )
    devices = dp_size * lax.axis_size("tensor")
    def from_all(value):
        return lax.all_to_all(value, ("dp", "tensor"), 0, 0, tiled=True)

    (small,) = call(
        small_kernel,
        "small",
        (),
        (gain_grad_first, gain_grad_second, dbias0, dbias1),
        (sds((devices, SMALL_ROWS, 128), f32),),
        work=10,
    )
    small = from_all(small)
    if aligned:
        grad_qkv, grad_out, squares = call(
            finish_a_kernel,
            "finish_a",
            (),
            (*a_pieces, up_squares, down_squares),
            (sds(qkv_master.shape, f32), sds(out_master.shape, f32), sds((devices, 8, 128), f32)),
            gates=(small,),
        )
    else:
        grad_a = jnp.sum(a_pieces[0].astype(f32), axis=0)
        grad_qkv = jnp.stack([grad_a[:, i * width : (i + 1) * width] for i in range(3)])
        grad_out = grad_a[:, 3 * width :].T
        squares = jnp.broadcast_to(
            up_squares + down_squares + jnp.sum(grad_a * grad_a), (devices, 8, 128)
        )

    tokens_grad, pooled = call(
        place_kernel,
        "tokens_grad",
        (),
        (tg_own, tg_got, mean_keep),
        (sds(tokens.shape, f32), sds((rows, SEGS, width), f32)),
        gates=(squares,),
    )
    squares = from_all(squares)
    groups = (
        (qkv_master, grad_qkv, qkv_first, qkv_second),
        (out_master, grad_out, out_first, out_second),
        (up_master, grad_up, up_first, up_second),
        (down_master.T, grad_downT, down_first.T, down_second.T),
        (norm_gains, None, gain_first, gain_second),
        (position_bias.T, None, bias_first.T, bias_second.T),
    )
    operands = [array for group in groups for array in group if array is not None]
    updates = pl.pallas_call(
        adam_kernel,
        out_shape=[sds(group[0].shape, f32) for group in groups for _ in range(2)]
        + [sds(norm_gains.shape, f32), sds(position_bias.shape[::-1], f32), sds((1, 1), f32)],
        in_specs=[VMEM_SPEC] * 2 + [pl.BlockSpec(memory_space=pltpu.HBM)] * (len(operands) + 1),
        out_specs=[VMEM_SPEC] * (2 * len(groups) + 2) + [SMEM_SPEC],
        scratch_shapes=[pltpu.VMEM(array.shape, f32) for array in operands]
        + [pltpu.SemaphoreType.DMA((len(operands),))],
        compiler_params=pltpu.CompilerParams(vmem_limit_bytes=60 << 20),
        name="adam",
    )(small, squares, *operands, pooled)
    new_qkv, second_qkv, new_out, second_out, new_up, second_up = updates[0:6]
    new_gains, second_gains = updates[8:10]
    new_down, second_down, new_bias, second_bias = (updates[i].T for i in (6, 7, 10, 11))
    grad_gains, grad_biasT = updates[12:14]
    grad_down, grad_bias = grad_downT.T, grad_biasT.T
    gradient_norm = updates[14].reshape(())
    return (
        pooled,
        tokens_grad,
        grad_qkv,
        grad_out,
        grad_up,
        grad_down,
        grad_gains,
        grad_bias,
        gradient_norm,
        new_qkv,
        new_out,
        new_up,
        new_down,
        new_gains,
        new_bias,
        second_qkv,
        second_out,
        second_up,
        second_down,
        second_gains,
        second_bias,
    )


def solution(mesh):
    in_specs = (
        P("dp", "tensor", None),
        P("dp", None),
        P("dp", "tensor", None),
        P(None, "dp", "tensor"),
        P("tensor", "dp"),
        P("dp", "tensor"),
        P("tensor", "dp"),
        P(),
        P(),
        P(None, "dp", "tensor"),
        P(None, "dp", "tensor"),
        P("tensor", "dp"),
        P("tensor", "dp"),
        P("dp", "tensor"),
        P("dp", "tensor"),
        P("tensor", "dp"),
        P("tensor", "dp"),
        P(),
        P(),
        P(),
        P(),
    )
    out_specs = (
        P("dp", None, "tensor"),
        P("dp", "tensor", None),
        P(None, "dp", "tensor"),
        P("tensor", "dp"),
        P("dp", "tensor"),
        P("tensor", "dp"),
        P(),
        P(),
        P(),
        P(None, "dp", "tensor"),
        P("tensor", "dp"),
        P("dp", "tensor"),
        P("tensor", "dp"),
        P(),
        P(),
        P(None, "dp", "tensor"),
        P("tensor", "dp"),
        P("dp", "tensor"),
        P("tensor", "dp"),
        P(),
        P(),
    )
    return jax.shard_map(
        per_device, mesh=mesh, in_specs=in_specs, out_specs=out_specs, check_vma=False
    )
```

```python
import functools

import jax
import jax.numpy as jnp
from jax import lax
from jax.experimental import pallas as pl
from jax.experimental.pallas import tpu as pltpu
from jax.sharding import PartitionSpec as P

D = 768
H = 12
DH = 64
FF = 3072
SEGS = 16
STEP = 10

norm_eps = 1e-06
mask_fill = -1000000000.0
clip_level = 1.0
beta_first = 0.9
beta_second = 0.999
adam_eps = 1e-08
decay_rate = 0.1
gelu_scale = 0.7978845608028654
gelu_cubic = 0.044715

bf16 = jnp.bfloat16
f32 = jnp.float32
i32 = jnp.int32

SMALL_ROWS = 16
BUCKETS = 32
QB = 256
KC = 128
EDGE = 128
NEAR = QB + 2 * EDGE
VMEM_LIMIT = 20 << 20
FULL_LIMIT = 60 << 20
FEED_LIMIT = 36 << 20
FILL = 1_000_000_000

SMEM_SPEC = pl.BlockSpec(memory_space=pltpu.SMEM)
VMEM_SPEC = pl.BlockSpec(memory_space=pltpu.VMEM)


def sds(shape, dtype):
    return jax.ShapeDtypeStruct(shape, dtype)


def nt(a, b):
    return lax.dot_general(a, b, (((1,), (1,)), ((), ())), preferred_element_type=f32)


def nn(a, b):
    return lax.dot_general(a, b, (((1,), (0,)), ((), ())), preferred_element_type=f32)


def call(body, name, smem, vmem, outs, scratch=(), gates=(), work=0, limit=VMEM_LIMIT):
    first, taken = len(smem) + len(vmem), len(gates)

    def gated(*refs):
        body(*refs[:first], *refs[first + taken :])

    return pl.pallas_call(
        gated if gates else body,
        out_shape=tuple(outs),
        in_specs=[SMEM_SPEC] * len(smem)
        + [VMEM_SPEC] * len(vmem)
        + [pl.BlockSpec(memory_space=pl.ANY)] * taken,
        out_specs=(VMEM_SPEC,) * len(outs),
        scratch_shapes=list(scratch),
        compiler_params=pltpu.CompilerParams(vmem_limit_bytes=limit),
        cost_estimate=pl.CostEstimate(
            flops=max(1, work * FILL), bytes_accessed=1000, transcendentals=0
        ),
        name=name,
    )(*smem, *vmem, *gates)


def bucket_of(offset):
    distance = jnp.abs(offset)
    large = 8 + sum(
        ((distance >= threshold).astype(jnp.int32) for threshold in (12, 16, 23, 32, 46, 64, 91))
    )
    inner_bucket = jnp.where(distance < 8, distance, large)
    return inner_bucket + jnp.where(offset > 0, 16, 0)


def learning_rates_plain():
    return (
        (2.0 * (D * DH) ** (-0.5), 2.0 * D ** (-0.5), 2.0 * D ** (-0.5)),
        0.5 * (H * DH / 16) ** (-0.5),
        0.5 * D ** (-0.5),
        2.0 * FF ** (-0.5),
        0.25,
        0.5,
    )


def adam_update(parameter, gradient, first_moment, second_moment, step_rate, clip_factor):
    clipped = gradient * clip_factor
    first_new = beta_first * first_moment + (1.0 - beta_first) * clipped
    second_new = beta_second * second_moment + (1.0 - beta_second) * clipped * clipped
    first_hat = first_new / (1.0 - beta_first**STEP)
    second_hat = second_new / (1.0 - beta_second**STEP)
    updated = parameter - step_rate * (
        first_hat / (jnp.sqrt(second_hat) + adam_eps) + decay_rate * parameter
    )
    return (updated, second_new)


def swap_core(value):
    return lax.ppermute(value, "tensor", [(i, i ^ 1) for i in range(lax.axis_size("tensor"))])


def swap_x(value):
    return lax.ppermute(value, "tensor", [(i, i ^ 2) for i in range(lax.axis_size("tensor"))])


def swap_dp(value, bits):
    return lax.ppermute(value, "dp", [(i, i ^ bits) for i in range(lax.axis_size("dp"))])


def swap_y(value):
    return swap_dp(value, 1)


def over_high(blocks):
    size = lax.axis_size("dp")
    groups = [[index for index in range(size) if index % 2 == bit] for bit in range(2)]
    return lax.all_to_all(blocks, "dp", 0, 0, tiled=True, axis_index_groups=groups)


def row_places():
    rank = lax.axis_index("tensor")
    return (rank, rank ^ 2, rank ^ 1, rank ^ 3)


def bias_tiles(bias_ref, first_head, heads, near_ref):
    span = 2 * NEAR
    lane = lax.broadcasted_iota(i32, (8, span), 1)
    offset = -EDGE - jnp.where(lane < span // 2, lane, lane - span)
    buckets = bucket_of(offset)
    values = [
        jnp.where(offset > 0, bias_ref[31, first_head + h], bias_ref[15, first_head + h])
        for h in range(heads)
    ]
    for bucket in list(range(15)) + list(range(17, 31)):
        here = buckets == bucket
        values = [
            jnp.where(here, bias_ref[bucket, first_head + h], values[h]) for h in range(heads)
        ]
    for h in range(heads):
        line = jnp.broadcast_to(values[h][0:1, :], (NEAR, span))
        near_ref[h] = pltpu.roll(line, 0, 1, stride=1, stride_axis=0)[:, :QB]


def rms_of(values):
    return lax.rsqrt(jnp.mean(values * values, axis=-1, keepdims=True) + norm_eps)


def blocks_of(rows, kind):
    return tuple(ref.at[kind] for ref in rows)


def norm_kernel(keep_ref, got_ref, keep_oth_ref, got_oth_ref, gain_ref, h_ref, token_ref):
    token_ref[...] = jnp.zeros_like(token_ref)
    length = keep_ref.shape[1]
    blocks = blocks_of((keep_ref, got_ref, keep_oth_ref, got_oth_ref), 0)
    for place, block in zip(row_places(), blocks):
        start = pl.multiple_of(place * length, length)
        values = block[...].astype(f32)
        h_ref[pl.ds(start, length), :] = (values * rms_of(values) * gain_ref[0:1, :]).astype(bf16)


def place_weights(pieces, target, kind=None):
    bit = lax.axis_index("dp") % 2
    for index, piece in enumerate(pieces):
        rows = piece.shape[-2]
        lowest = bit if index == 0 else 1 - bit
        for slot in range(piece.shape[0]):
            start = pl.multiple_of((2 * slot + lowest) * rows, 16)
            target[pl.ds(start, rows), :] = piece[slot] if kind is None else piece[slot, kind]


def split_rows(source, own_ref, other_ref):
    rows = own_ref.shape[1]
    bit = lax.axis_index("dp") % 2
    for block in range(own_ref.shape[0]):
        start = pl.multiple_of((2 * block + bit) * rows, 16)
        own_ref[block] = source[pl.ds(start, rows), :]
        start = pl.multiple_of((2 * block + 1 - bit) * rows, 16)
        other_ref[block] = source[pl.ds(start, rows), :]


def sub_sum(values):
    return jnp.sum(values.reshape(values.shape[0] // 8, 8, values.shape[1]), axis=0)


def sub_max(values):
    return jnp.max(values.reshape(values.shape[0] // 8, 8, values.shape[1]), axis=0)


def blocks_even(seq):
    return (seq // QB) % 2 == 0


def near_row(block, chunk):
    start = chunk * KC - block * QB + EDGE
    return start if 0 <= start and start + KC <= NEAR else None


def same_segment(seg_keys, keys, seg_query):
    seg_key = seg_keys[keys, :]
    return jnp.concatenate([seg_key] * (QB // seg_key.shape[1]), axis=1) == seg_query


def segments(seg_ref):
    line = seg_ref[pl.ds(lax.axis_index("tensor") // 2, 1), :]
    return line, jnp.broadcast_to(line, (128, line.shape[1])).T


def one_item(seg_smem_ref):
    side = lax.axis_index("tensor") // 2
    return seg_smem_ref[side, 0] == seg_smem_ref[side, seg_smem_ref.shape[1] - 1]


def head_of(shift, heads):
    return (lax.axis_index("tensor") ^ shift) * heads


def attend_kernel(
    shift, seg_smem_ref, bias_ref, h_ref, piece_a_ref, piece_b_ref, seg_ref,
    wT_ref, qkvT_ref, oT_ref, lse_ref, w_buf, k_buf, s_buf, p_buf, near_ref, segk_ref,
):
    seq = h_ref.shape[0]
    heads = near_ref.shape[0]
    width = oT_ref.shape[0]
    first_head = head_of(shift, heads)
    bias_tiles(bias_ref, first_head, heads, near_ref)
    size = width // heads
    chunks = seq // KC
    assert blocks_even(seq)
    place_weights((piece_a_ref, piece_b_ref), w_buf)
    wT_ref[...] = w_buf[...].T
    qkvT_ref[...] = nt(wT_ref[0 : 3 * width, :], h_ref[...]).astype(bf16)
    blocks = seq // QB

    def rows(part, h):
        return pl.ds(pl.multiple_of(part * width + h * size, size), size)

    def score(h, block):
        s_buf[block % 2] = nn(k_buf[h % 2], qkvT_ref[rows(0, h), block * QB : (block + 1) * QB])

    def soften(h, block, masked):
        slot = block % 2
        qs = slice(block * QB, (block + 1) * QB)
        top = jnp.full((8, QB), -3e38, f32)
        for chunk in range(chunks):
            ks = slice(chunk * KC, (chunk + 1) * KC)
            row = near_row(block, chunk)
            if row is None:
                scores = s_buf[slot, ks, :] + bias_ref[15 if chunk * KC < block * QB else 31, first_head + h]
            else:
                scores = s_buf[slot, ks, :] + near_ref[h, row : row + KC, :]
            if masked:
                scores = jnp.where(same_segment(segk_ref, ks, segq[:, qs]), scores, mask_fill)
            s_buf[slot, ks, :] = scores
            top = jnp.maximum(top, sub_max(scores))
        top = jnp.max(top, axis=0, keepdims=True)
        total = jnp.zeros((8, QB), f32)
        for chunk in range(chunks):
            ks = slice(chunk * KC, (chunk + 1) * KC)
            exps = jnp.exp(s_buf[slot, ks, :] - top)
            s_buf[slot, ks, :] = exps
            total = total + sub_sum(exps)
        total = jnp.sum(total, axis=0, keepdims=True)
        scale = 1.0 / total
        for chunk in range(chunks):
            ks = slice(chunk * KC, (chunk + 1) * KC)
            p_buf[slot, ks, :] = (s_buf[slot, ks, :] * scale).astype(bf16)
        lse_ref[pl.ds(h, 1), qs] = top + jnp.log(total)

    def mix(h, block):
        qs = slice(block * QB, (block + 1) * QB)
        oT_ref[rows(0, h), qs] = nn(qkvT_ref[rows(2, h), :], p_buf[block % 2]).astype(bf16)

    segq, seg_keys = segments(seg_ref)

    def run(masked):
        if masked:
            segk_ref[...] = seg_keys
        k_buf[0] = qkvT_ref[rows(1, 0), :].T
        score(0, 0)

        def head(h, carried):
            for block in range(blocks):
                if block + 1 < blocks:
                    score(h, block + 1)
                else:
                    later = jnp.minimum(h + 1, heads - 1)
                    k_buf[(h + 1) % 2] = qkvT_ref[rows(1, later), :].T
                    s_buf[0] = nn(k_buf[(h + 1) % 2], qkvT_ref[rows(0, later), 0:QB])
                soften(h, block, masked)
                if block:
                    mix(h, block - 1)
            mix(h, blocks - 1)
            return carried

        lax.fori_loop(0, heads, head, 0)

    single = one_item(seg_smem_ref)

    @pl.when(single)
    def _():
        run(False)

    @pl.when(jnp.logical_not(single))
    def _():
        run(True)


def attend(shift, seg, bias, h, pieces):
    seq = h.shape[0]
    cols = pieces[0].shape[2]
    width = cols // 4
    heads = bias.shape[1] // 4
    return call(
        functools.partial(attend_kernel, shift),
        "attend",
        (seg, bias),
        (h, *pieces, seg),
        (sds((cols, D), bf16), sds((3 * width, seq), bf16), sds((width, seq), bf16), sds((8, seq), f32)),
        (
            pltpu.VMEM((D, cols), bf16),
            pltpu.VMEM((2, seq, width // heads), bf16),
            pltpu.VMEM((2, seq, QB), f32),
            pltpu.VMEM((2, seq, QB), bf16),
            pltpu.VMEM((heads, NEAR, QB), f32),
            pltpu.VMEM((seq, 128), i32),
        ),
    )


def attend_back_kernel(
    shift, seg_smem_ref, bias_ref, qkvT_ref, doT_ref, lse_ref, seg_ref, h_ref, goT_ref,
    dqkvT_ref, own_ref, other_ref, dbias_ref,
    kv_buf, s_buf, dp_buf, ds_buf, pt_buf, dt_buf, dk_buf, dv_buf, g_buf, near_ref, segk_ref,
    dnear_ref, dfar_ref, line_buf,
):
    width, seq = doT_ref.shape
    heads = near_ref.shape[0]
    first_head = head_of(shift, heads)
    bias_tiles(bias_ref, first_head, heads, near_ref)
    segq, seg_keys = segments(seg_ref)
    size = width // heads
    blocks = seq // QB
    chunks = seq // KC
    assert blocks_even(seq)

    def rows(part, h):
        return pl.ds(pl.multiple_of(part * width + h * size, size), size)

    def key_values(h, turn):
        kv_buf[turn] = jnp.concatenate([qkvT_ref[rows(1, h), :], qkvT_ref[rows(2, h), :]], axis=0).T

    def products(h, turn, block):
        slot = block % 2
        qs = slice(block * QB, (block + 1) * QB)
        zeros = jnp.zeros((size, QB), bf16)
        s_buf[slot] = nn(kv_buf[turn], jnp.concatenate([qkvT_ref[rows(0, h), qs], zeros], axis=0))
        dp_buf[slot] = nn(kv_buf[turn], jnp.concatenate([zeros, doT_ref[rows(0, h), qs]], axis=0))

    def soften(h, block, masked):
        slot = block % 2
        qs = slice(block * QB, (block + 1) * QB)
        lse = lse_ref[pl.ds(h, 1), qs]
        lse_left = lse - bias_ref[15, first_head + h]
        lse_right = lse - bias_ref[31, first_head + h]
        dots = jnp.zeros((8, QB), f32)
        for chunk in range(chunks):
            ks = slice(chunk * KC, (chunk + 1) * KC)
            row = near_row(block, chunk)
            if row is None:
                scores = s_buf[slot, ks, :] - (lse_left if chunk * KC < block * QB else lse_right)
            else:
                scores = s_buf[slot, ks, :] + near_ref[h, row : row + KC, :] - lse
            probs = jnp.exp(scores)
            if masked:
                probs = jnp.where(same_segment(segk_ref, ks, segq[:, qs]), probs, 0.0)
            s_buf[slot, ks, :] = probs
            pt_buf[slot, :, ks] = probs.astype(bf16).T
            dots = dots + sub_sum(probs * dp_buf[slot, ks, :])
        dots = jnp.sum(dots, axis=0, keepdims=True)
        for chunk in range(chunks):
            ks = slice(chunk * KC, (chunk + 1) * KC)
            d_scores = (s_buf[slot, ks, :] * (dp_buf[slot, ks, :] - dots)).astype(bf16)
            ds_buf[slot, ks, :] = d_scores
            dt_buf[slot, :, ks] = d_scores.T
            row = near_row(block, chunk)
            if row is not None:
                if block == 0 or (block == 1 and row == 0):
                    dnear_ref[h, row : row + KC, :] = d_scores.astype(f32)
                else:
                    dnear_ref[h, row : row + KC, :] += d_scores.astype(f32)

    def outputs(h, block):
        slot = block % 2
        qs = slice(block * QB, (block + 1) * QB)
        dqkvT_ref[rows(0, h), qs] = nn(qkvT_ref[rows(1, h), :], ds_buf[slot]).astype(bf16)
        d_keys = nn(
            jnp.concatenate([qkvT_ref[rows(0, h), qs], jnp.ones((16, QB), bf16)], axis=0),
            dt_buf[slot],
        )
        d_values = nn(doT_ref[rows(0, h), qs], pt_buf[slot])
        if block == 0:
            dk_buf[...] = d_keys[0:size]
            dv_buf[...] = d_values
        elif block + 1 < blocks:
            dk_buf[...] += d_keys[0:size]
            dv_buf[...] += d_values
        else:
            dqkvT_ref[rows(1, h), :] = (dk_buf[...] + d_keys[0:size]).astype(bf16)
            dqkvT_ref[rows(2, h), :] = (dv_buf[...] + d_values).astype(bf16)
        sums = d_keys[size : size + 1]
        left_end = max(0, block * QB - EDGE)
        right_start = min(seq, block * QB + QB + EDGE)
        lane = lax.broadcasted_iota(i32, (1, 128), 1)
        line = jnp.zeros((1, 128), f32)
        if left_end:
            line = jnp.where(lane == 0, jnp.sum(sums[:, :left_end], axis=1, keepdims=True), line)
        if right_start < seq:
            line = jnp.where(lane == 1, jnp.sum(sums[:, right_start:], axis=1, keepdims=True), line)
        if block == 0:
            dfar_ref[pl.ds(h, 1), :] = line
        else:
            dfar_ref[pl.ds(h, 1), :] += line

    def run(masked):
        if masked:
            segk_ref[...] = seg_keys
        key_values(0, 0)
        products(0, 0, 0)

        def head(h, carried):
            for block in range(blocks):
                if block + 1 < blocks:
                    products(h, h % 2, block + 1)
                else:
                    later = jnp.minimum(h + 1, heads - 1)
                    key_values(later, (h + 1) % 2)
                    products(later, (h + 1) % 2, 0)
                soften(h, block, masked)
                if block:
                    outputs(h, block - 1)
            outputs(h, blocks - 1)
            return carried

        lax.fori_loop(0, heads, head, 0)

    single = one_item(seg_smem_ref)

    @pl.when(single)
    def _():
        run(False)

    @pl.when(jnp.logical_not(single))
    def _():
        run(True)

    dfar_ref[heads:, :] = jnp.zeros((8 - heads, 128), f32)
    grad = jnp.concatenate([nn(dqkvT_ref[...], h_ref[...]).astype(bf16), goT_ref[...]], axis=0)
    if other_ref is None:
        own_ref[...] = grad.T
    else:
        g_buf[...] = grad.T
        split_rows(g_buf, own_ref, other_ref)
    bias_gradients(dnear_ref, dfar_ref, line_buf, dbias_ref)


def attend_back(shift, seg, bias, qkvT, doT, lse, h, goT, grad_outs, gates):
    width, seq = doT.shape
    heads = bias.shape[1] // 4
    size = width // heads
    body = functools.partial(attend_back_kernel, shift)
    if len(grad_outs) == 1:

        def body(*refs):
            attend_back_kernel(shift, *refs[:10], None, *refs[10:])

    return call(
        body,
        "attend_back",
        (seg, bias),
        (qkvT, doT, lse, seg, h, goT),
        (sds(qkvT.shape, bf16), *grad_outs, sds((8, 128), f32)),
        (
            pltpu.VMEM((2, seq, 2 * size), bf16),
            pltpu.VMEM((2, seq, QB), f32),
            pltpu.VMEM((2, seq, QB), f32),
            pltpu.VMEM((2, seq, QB), bf16),
            pltpu.VMEM((2, QB, seq), bf16),
            pltpu.VMEM((2, QB, seq), bf16),
            pltpu.VMEM((size, seq), f32),
            pltpu.VMEM((size, seq), f32),
            pltpu.VMEM((D, 4 * width), bf16),
            pltpu.VMEM((heads, NEAR, QB), f32),
            pltpu.VMEM((seq, 128), i32),
            pltpu.VMEM((heads, NEAR, QB), f32),
            pltpu.VMEM((8, 128), f32),
            pltpu.VMEM((8, 2 * NEAR), f32),
        ),
        gates,
    )


def project_kernel(oT0_ref, oT1_ref, wT0_ref, wT1_ref, keep_ref, send_ref, o_buf):
    width = oT0_ref.shape[0]
    length = keep_ref.shape[0] // 2
    o_buf[...] = jnp.concatenate([oT0_ref[...], oT1_ref[...]], axis=0).T
    w = jnp.concatenate([wT0_ref[3 * width :, :], wT1_ref[3 * width :, :]], axis=0)
    for index, place in enumerate(row_places()):
        start = pl.multiple_of(place * length, length)
        part = nn(o_buf[pl.ds(start, length), :], w)
        rows = slice((index % 2) * length, (index % 2 + 1) * length)
        if index < 2:
            keep_ref[rows, :] = part
        else:
            send_ref[rows, :] = part.astype(send_ref.dtype)


def middle_kernel(keep_row_ref, got_row_ref, part_ref, got_ref, gain_ref, x2_ref, h_ref):
    length = keep_row_ref.shape[1]
    for index, block in enumerate((keep_row_ref.at[0], got_row_ref.at[0])):
        rows = slice(index * length, (index + 1) * length)
        values = block[...].astype(f32) + part_ref[rows, :] + got_ref[rows, :].astype(f32)
        x2_ref[rows, :] = values
        h_ref[rows, :] = (values * rms_of(values) * gain_ref[1:2, :]).astype(bf16)


def split3(values):
    high = values.astype(bf16)
    rest = values - high.astype(f32)
    mid = rest.astype(bf16)
    low = (rest - mid.astype(f32)).astype(bf16)
    return high, mid, low


def feed_rows(h, cot, u_buf, d_buf, act_ref, dpre_ref, rows):
    pre = nn(h, u_buf[...])
    d_act = nn(cot, d_buf[...])
    square = pre * pre
    bent = jnp.tanh(gelu_scale * pre * (1.0 + gelu_cubic * square))
    half_up = 0.5 * (1.0 + bent)
    act_ref[rows, :] = (pre * half_up).astype(bf16)
    slope = half_up + (0.5 * gelu_scale) * pre * (1.0 - bent * bent) * (
        1.0 + (3.0 * gelu_cubic) * square
    )
    d_pre = (d_act * slope).astype(bf16)
    dpre_ref[rows, :] = d_pre
    return nt(d_pre, u_buf[...])


def pooled_units(hot, act_ref, d_buf):
    pooled = None
    for term in split3(nn(hot, act_ref[...])):
        part = nt(term, d_buf[...])
        pooled = part if pooled is None else pooled + part
    return pooled


def weight_grads(h_refs, cots, act_ref, dpre_ref, outs, g_buf):
    hT = jnp.concatenate([ref[...] for ref in h_refs], axis=0).T
    cotT = jnp.concatenate([block[...] for block in cots], axis=0).T
    if len(outs) == 2:
        outs[0][...] = nn(hT, dpre_ref[...]).astype(bf16)
        outs[1][...] = nn(cotT, act_ref[...]).astype(bf16)
    else:
        g_buf[0] = nn(hT, dpre_ref[...]).astype(bf16)
        split_rows(g_buf.at[0], outs[0], outs[1])
        g_buf[1] = nn(cotT, act_ref[...]).astype(bf16)
        split_rows(g_buf.at[1], outs[2], outs[3])


def feed_own_kernel(
    h_own_ref, h_oth_ref, keep_ref, got_ref, keep_oth_ref, got_oth_ref,
    a_ref, b_ref, seg_ref, x2_ref, dh_ref, pooled_ref, hot_ref, *refs
):
    *outs, u_buf, d_buf, act_buf, dpre_buf, g_buf = refs
    place_weights((a_ref, b_ref), u_buf, 0)
    place_weights((a_ref, b_ref), d_buf, 1)
    length = keep_ref.shape[1]
    cots = blocks_of((keep_ref, got_ref, keep_oth_ref, got_oth_ref), 1)
    line = seg_ref[pl.ds(lax.axis_index("tensor") // 2, 1), :]
    seq = line.shape[1]
    item = lax.broadcasted_iota(i32, (SEGS, seq), 0)
    whole = (jnp.broadcast_to(line, (SEGS, seq)) == item).astype(f32)
    for index, place in enumerate(row_places()):
        part = jnp.zeros((SEGS, length), f32)
        for block in range(4):
            part = jnp.where(place == block, whole[:, block * length : (block + 1) * length], part)
        hot_ref[:, index * length : (index + 1) * length] = part.astype(bf16)
    for index in range(4):
        rows = slice(index * length, (index + 1) * length)
        half = slice((index % 2) * length, (index % 2 + 1) * length)
        h = (h_own_ref if index < 2 else h_oth_ref)[half, :]
        dh_ref[rows, :] = feed_rows(h, cots[index][...], u_buf, d_buf, act_buf, dpre_buf, rows)
    hot = hot_ref[...]
    pooled = pooled_units(hot, act_buf, d_buf)
    for term in split3(x2_ref[...]):
        pooled = pooled + nn(hot[:, 0 : 2 * length], term)
    pooled_ref[...] = pooled
    weight_grads((h_own_ref, h_oth_ref), cots, act_buf, dpre_buf, outs, g_buf)


def feed_other_kernel(
    h_own_ref, h_oth_ref, keep_ref, got_ref, keep_oth_ref, got_oth_ref,
    a_ref, ub_ref, db_ref, hot_ref, dh_ref, pool_ref,
    part_ref, send_ref, pooled_ref, *refs
):
    *outs, u_buf, d_buf, act_buf, dpre_buf, g_buf = refs
    place_weights((a_ref,), u_buf, 0)
    place_weights((a_ref,), d_buf, 1)
    bit = lax.axis_index("dp") % 2
    for source, target in ((ub_ref, u_buf), (db_ref, d_buf)):
        count = source.shape[1]
        for slot in range(source.shape[0]):
            start = pl.multiple_of((2 * slot + 1 - bit) * count, 16)
            target[pl.ds(start, count), :] = source[slot]
    length = keep_ref.shape[1]
    cots = blocks_of((keep_ref, got_ref, keep_oth_ref, got_oth_ref), 1)
    for index in (2, 3, 0, 1):
        rows = slice(index * length, (index + 1) * length)
        half = slice((index % 2) * length, (index % 2 + 1) * length)
        h = (h_own_ref if index < 2 else h_oth_ref)[half, :]
        total = dh_ref[rows, :] + feed_rows(
            h, cots[index][...], u_buf, d_buf, act_buf, dpre_buf, rows
        )
        if index < 2:
            part_ref[half, :] = total
        else:
            send_ref[half, :] = total.astype(send_ref.dtype)
    pooled_ref[...] = pool_ref[...] + pooled_units(hot_ref[...], act_buf, d_buf)
    weight_grads((h_own_ref, h_oth_ref), cots, act_buf, dpre_buf, outs, g_buf)


def norm_back(values, gain, upstream):
    scale = rms_of(values)
    normed = values * scale
    gain_grad = jnp.sum(upstream * normed, axis=0, keepdims=True)
    scaled = upstream * gain
    inner = jnp.mean(scaled * normed, axis=-1, keepdims=True)
    return scale * (scaled - normed * inner), gain_grad


def middle_back_kernel(
    x2_ref, part_ref, got_ref, keep_row_ref, got_row_ref, gain_ref, dx2_ref, da_ref, gain_grad_ref
):
    length = x2_ref.shape[0] // 2
    for index, cot in enumerate((keep_row_ref.at[1], got_row_ref.at[1])):
        rows = slice(index * length, (index + 1) * length)
        d_values, gain_grad = norm_back(
            x2_ref[rows, :], gain_ref[1:2, :], part_ref[rows, :] + got_ref[rows, :].astype(f32)
        )
        dx2 = cot[...].astype(f32) + d_values
        dx2_ref[rows, :] = dx2
        da_ref[rows, :] = dx2.astype(bf16)
        if index == 0:
            gain_grad_ref[...] = gain_grad
        else:
            gain_grad_ref[...] += gain_grad


def branch_back_kernel(
    da_own_ref, da_oth_ref, wT0_ref, wT1_ref, oT0_ref, oT1_ref,
    doT0_ref, doT1_ref, g0_ref, g1_ref, da_buf,
):
    width = oT0_ref.shape[0]
    length = da_own_ref.shape[0] // 2
    for index, place in enumerate(row_places()):
        start = pl.multiple_of(place * length, length)
        half = slice((index % 2) * length, (index % 2 + 1) * length)
        da_buf[pl.ds(start, length), :] = (da_own_ref if index < 2 else da_oth_ref)[half, :]
    da = da_buf[...]
    doT0_ref[...] = nt(wT0_ref[3 * width :, :], da).astype(bf16)
    doT1_ref[...] = nt(wT1_ref[3 * width :, :], da).astype(bf16)
    g0_ref[...] = nn(oT0_ref[...], da).astype(bf16)
    g1_ref[...] = nn(oT1_ref[...], da).astype(bf16)


def first_back_kernel(d0_ref, d1_ref, wT0_ref, wT1_ref, keep_ref, send_ref, token_ref, d_buf):
    token_ref[...] = jnp.zeros_like(token_ref)
    rows3 = d0_ref.shape[0]
    length = keep_ref.shape[0] // 2
    d_buf[...] = jnp.concatenate([d0_ref[...], d1_ref[...]], axis=0).T
    w = jnp.concatenate([wT0_ref[0:rows3, :], wT1_ref[0:rows3, :]], axis=0)
    places = row_places()
    for index in (2, 3, 0, 1):
        start = pl.multiple_of(places[index] * length, length)
        part = nn(d_buf[pl.ds(start, length), :], w)
        rows = slice((index % 2) * length, (index % 2 + 1) * length)
        if index < 2:
            keep_ref[rows, :] = part
        else:
            send_ref[rows, :] = part.astype(send_ref.dtype)


def token_grad_kernel(
    keep_row_ref, got_row_ref, part_ref, got_ref, dx2_ref, gain_ref, pool_ref, pool_got_ref, hot_ref,
    own_ref, away_ref, gain_grad_ref, mean_ref
):
    length = keep_row_ref.shape[1]
    away_ref[length:, :] = jnp.zeros((away_ref.shape[0] - length, away_ref.shape[1]), bf16)
    counts = jnp.sum(hot_ref[...].astype(f32), axis=1, keepdims=True)
    means = (pool_ref[...] + pool_got_ref[...]) / jnp.maximum(counts, 1.0)
    rank = lax.axis_index("tensor")
    width = mean_ref.shape[1]
    mine, sent = jnp.zeros(mean_ref.shape, f32), jnp.zeros(mean_ref.shape, f32)
    for shard in range(4):
        part = means[:, shard * width : (shard + 1) * width]
        mine = jnp.where(rank == shard, part, mine)
        sent = jnp.where(rank ^ 2 == shard, part, sent)
    mean_ref[...] = mine
    away_ref[length:, 0:width] = sent.astype(bf16)
    for index, block in enumerate((keep_row_ref.at[0], got_row_ref.at[0])):
        rows = slice(index * length, (index + 1) * length)
        d_values, gain_grad = norm_back(
            block[...].astype(f32), gain_ref[0:1, :], part_ref[rows, :] + got_ref[rows, :].astype(f32)
        )
        if index == 0:
            own_ref[...] = dx2_ref[rows, :] + d_values
            gain_grad_ref[...] = gain_grad
        else:
            away_ref[0:length, :] = (dx2_ref[rows, :] + d_values).astype(bf16)
            gain_grad_ref[...] += gain_grad


def bias_gradients(dnear_ref, dfar_ref, line_buf, grad_ref):
    heads = dnear_ref.shape[0]
    span = 2 * NEAR
    line_buf[...] = jnp.zeros_like(line_buf)
    for h in range(heads):
        values = dnear_ref[h]
        rows = NEAR
        while rows > 1:
            rows //= 2
            low, high = values[:rows], values[rows:]
            if rows % 128 == 0:
                pad = jnp.zeros((rows, rows), f32)
                values = jnp.concatenate([pad, low], axis=1) + jnp.concatenate([high, pad], axis=1)
            else:
                if values.shape[1] < span:
                    pad = jnp.zeros((rows, span - values.shape[1]), f32)
                    low = jnp.concatenate([pad, low], axis=1)
                    high = jnp.concatenate([pad, high], axis=1)
                values = low + pltpu.roll(high, span - rows, 1)
        line_buf[h : h + 1, :] = values
    lines = line_buf[...]
    col = lax.broadcasted_iota(i32, lines.shape, 1)
    buckets = bucket_of(span - QB - EDGE - col)
    far = dfar_ref[...]
    lane = lax.broadcasted_iota(i32, (8, 128), 1)
    left = jnp.sum(jnp.where(lane == 0, far, 0.0), axis=1, keepdims=True)
    right = jnp.sum(jnp.where(lane == 1, far, 0.0), axis=1, keepdims=True)
    grad = jnp.where(lane == 15, left, jnp.where(lane == 31, right, 0.0))
    for bucket in range(32):
        if bucket != 16:
            total = jnp.sum(jnp.where(buckets == bucket, lines, 0.0), axis=1, keepdims=True)
            grad = jnp.where(lane == bucket, grad + total, grad)
    grad_ref[...] = grad


def pack_kernel(qkv_ref, out_ref, tokens_ref, cot_ref, pack_ref, keep_ref, send_ref):
    packed = jnp.concatenate([qkv_ref[0], qkv_ref[1], qkv_ref[2], out_ref[...].T], axis=1).astype(bf16)
    for slot in range(pack_ref.shape[0]):
        pack_ref[slot] = packed
    rows_kernel(tokens_ref, cot_ref, keep_ref, send_ref)


def pack_ud_kernel(up_ref, down_ref, pack_ref):
    up, down = up_ref[...].astype(bf16), down_ref[...].astype(bf16)
    for slot in range(pack_ref.shape[0]):
        pack_ref[slot, 0] = up
        pack_ref[slot, 1] = down


def rows_kernel(tokens_ref, cot_ref, keep_ref, send_ref):
    side = lax.axis_index("tensor") // 2
    keep_ref[0] = tokens_ref[side]
    keep_ref[1] = cot_ref[side]
    send_ref[0] = tokens_ref[1 - side]
    send_ref[1] = cot_ref[1 - side]


def place_kernel(own_ref, got_ref, mean_ref, out_ref, pooled_ref):
    side = lax.axis_index("tensor") // 2
    length, width = own_ref.shape[0], mean_ref.shape[1]
    out_ref[side] = own_ref[...]
    out_ref[1 - side] = got_ref[0:length, :].astype(f32)
    pooled_ref[side] = mean_ref[...]
    pooled_ref[1 - side] = got_ref[length:, 0:width].astype(f32)


def relay_kernel(*refs):
    for source_ref, out_ref in zip(refs[: len(refs) // 2], refs[len(refs) // 2 :]):
        out_ref[...] = source_ref[...]


def pick_kernel(from_x_ref, from_y_ref, up_ref, down_ref):
    up_ref[...] = from_x_ref[:, 0]
    down_ref[...] = from_y_ref[:, 1]


def total_of(refs):
    total = refs[0][...].astype(f32)
    for ref in refs[1:]:
        total = total + ref[...].astype(f32)
    return total


def add_kernel(*refs):
    *terms, sum_ref, token_ref = refs
    sum_ref[...] = total_of(terms).astype(bf16)
    token_ref[...] = jnp.zeros_like(token_ref)


def send_kernel(*refs):
    *terms, own_ref, sent1_ref, sent2_ref, sent3_ref, token_ref, sum_buf = refs
    sum_buf[...] = total_of(terms)
    place = lax.axis_index("dp") // 2
    own_ref[...] = sum_buf[place]
    for bits, ref in ((1, sent1_ref), (2, sent2_ref), (3, sent3_ref)):
        ref[...] = sum_buf[place ^ bits].astype(bf16)
    token_ref[...] = jnp.zeros_like(token_ref)


def add_pairs_kernel(up_ref, up_got_ref, down_ref, down_got_ref, up_sum_ref, down_sum_ref, token_ref):
    up_sum_ref[...] = total_of((up_ref, up_got_ref)).astype(bf16)
    down_sum_ref[...] = total_of((down_ref, down_got_ref)).astype(bf16)
    token_ref[...] = jnp.zeros_like(token_ref)


def sum_blocks(ref):
    total = ref[0].astype(f32)
    for slot in range(1, ref.shape[0]):
        total = total + ref[slot].astype(f32)
    return total


def finish_kernel(*refs):
    *terms, grad_ref, squares_ref = refs
    total = total_of(terms) if len(terms) > 1 else sum_blocks(terms[0])
    grad_ref[...] = total
    squares_ref[...] = jnp.broadcast_to(jnp.sum(total * total, axis=(0, 1), keepdims=True), (8, 128))


def finish_a_kernel(*refs):
    *terms, up_ref, down_ref, qkv_ref, out_ref, squares_ref = refs
    total = total_of(terms) if len(terms) > 1 else sum_blocks(terms[0])
    width = qkv_ref.shape[2]
    for part in range(3):
        qkv_ref[part] = total[:, part * width : (part + 1) * width]
    out_ref[...] = total[:, 3 * width :].T
    squares_ref[...] = (
        up_ref[...] + down_ref[...] + jnp.sum(total * total, axis=(0, 1), keepdims=True)
    )


def small_kernel(first_ref, second_ref, own_bias_ref, other_bias_ref, squares_ref, out_ref):
    lines = D // 128
    heads = H // 4
    for kind, ref in enumerate((first_ref, second_ref)):
        for line in range(lines):
            out_ref[0, kind * lines + line : kind * lines + line + 1, :] = ref[
                :, line * 128 : (line + 1) * 128
            ]
    terms = [jnp.zeros((1, BUCKETS), f32) for _ in range(H)]
    for shift, ref in ((0, own_bias_ref), (2, other_bias_ref)):
        start = head_of(shift, heads)
        for h in range(heads):
            term = ref[h : h + 1, 0:BUCKETS]
            terms = [jnp.where(start + h == head, term, kept) for head, kept in enumerate(terms)]
    across = 128 // BUCKETS
    for line in range(H // across):
        out_ref[0, 2 * lines + line : 2 * lines + line + 1, :] = jnp.concatenate(
            terms[line * across : (line + 1) * across], axis=1
        )
    lane = lax.broadcasted_iota(i32, (1, 128), 1)
    out_ref[0, SMALL_ROWS - 1 :, :] = jnp.where(lane == 0, squares_ref[0:1, :], 0.0)
    value = out_ref[0]
    for slot in range(1, out_ref.shape[0]):
        out_ref[slot] = value


def adam_kernel(small_ref, *refs):
    sources, refs = refs[:22], refs[23:]
    outs, refs = refs[:15], refs[15:]
    held, kept, (in_sems, out_sems) = refs[:22], refs[22:30], refs[30:]
    copies = [
        pltpu.make_async_copy(source, target, in_sems.at[index])
        for index, (source, target) in enumerate(zip(sources, held))
    ]
    for copy in copies:
        copy.start()
    small = jnp.sum(small_ref[...], axis=0)
    lines = D // 128
    gains_ref, bias_ref, norm_ref = outs[12:]
    for kind in range(2):
        for line in range(lines):
            gains_ref[kind : kind + 1, line * 128 : (line + 1) * 128] = small[
                kind * lines + line : kind * lines + line + 1
            ]
    across = 128 // BUCKETS
    for head in range(H):
        bias_ref[head : head + 1, :] = small[
            2 * lines + head // across : 2 * lines + head // across + 1,
            (head % across) * BUCKETS : (head % across + 1) * BUCKETS,
        ]
    whole = small[: SMALL_ROWS - 1]
    total = small[SMALL_ROWS - 1 :, 0:1]
    norm = jnp.sqrt(total + jnp.sum(whole * whole, axis=(0, 1), keepdims=True))
    norm_ref[0, 0] = jnp.max(norm)
    clip = jnp.minimum(1.0, clip_level / norm)
    rates = learning_rates_plain()
    results = []
    for index in (0, 2, 3, 1):
        param, grad, first, second = held[4 * index : 4 * index + 4]
        for copy in copies[4 * index : 4 * index + 4]:
            copy.wait()
        new, new_second = kept[2 * index : 2 * index + 2]
        if isinstance(rates[index], tuple):
            for part, rate in enumerate(rates[index]):
                value, moment = adam_update(
                    param[part], grad[part], first[part], second[part], rate, clip
                )
                new[part] = value
                new_second[part] = moment
        else:
            value, moment = adam_update(
                param[...], grad[...], first[...], second[...], rates[index], clip
            )
            new[...] = value
            new_second[...] = moment
        for place in (2 * index, 2 * index + 1):
            result = pltpu.make_async_copy(kept[place], outs[place], out_sems.at[place])
            result.start()
            results.append(result)
    for copy in copies[16:]:
        copy.wait()
    for index, (param, grad, first, second) in (
        (4, (held[16], gains_ref, held[17], held[18])),
        (5, (held[19], bias_ref, held[20], held[21])),
    ):
        value, moment = adam_update(
            param[...], grad[...], first[...], second[...], rates[index], clip
        )
        outs[2 * index][...] = value
        outs[2 * index + 1][...] = moment
    for result in results:
        result.wait()


def per_device(
    tokens,
    segment_ids,
    cotangent,
    qkv_master,
    out_master,
    up_master,
    down_master,
    norm_gains,
    position_bias,
    qkv_first,
    qkv_second,
    out_first,
    out_second,
    up_first,
    up_second,
    down_first,
    down_second,
    gain_first,
    gain_second,
    bias_first,
    bias_second,
):
    rank = lax.axis_index("tensor")
    dp_rank = lax.axis_index("dp")
    dp_size = lax.axis_size("dp")
    row_bit = dp_rank % 2
    rows, length = tokens.shape[0], tokens.shape[1]
    seq = segment_ids.shape[1]
    shard_rows, width = qkv_master.shape[1], qkv_master.shape[2]
    units = up_master.shape[1]
    half = (seq // 2, D)
    assert rows == 2 and lax.axis_size("tensor") == 4 and seq == 4 * length
    high = dp_size // 2
    aligned = shard_rows % 16 == 0

    if aligned:
        pack_a, keep_rows, sent_rows = call(
            pack_kernel,
            "pack_a",
            (),
            (qkv_master, out_master, tokens, cotangent),
            (sds((high, shard_rows, D), bf16),) + (sds((2, length, D), bf16),) * 2,
            limit=FULL_LIMIT,
        )
        order = lambda pair: pair
        blocks_out = (sds((high, shard_rows, D), bf16),) * 2
    else:
        packed = jnp.concatenate([*qkv_master, out_master.T], axis=1).astype(bf16)
        pack_a = jnp.broadcast_to(packed, (high,) + packed.shape)
        blocks_out = (sds((D, D), bf16),)
        keep_rows, sent_rows = call(
            rows_kernel, "rows", (), (tokens, cotangent), (sds((2, length, D), bf16),) * 2
        )

        def order(pair):
            own, other = pair
            first = jnp.where(row_bit == 0, own, other)
            second = jnp.where(row_bit == 0, other, own)
            both = jnp.moveaxis(jnp.stack([first, second], axis=1), (0, 1), (-4, -3))
            both = both.reshape(both.shape[:-4] + (D, both.shape[-1]))
            lower, upper = both[..., : D // 2, :], both[..., D // 2 :, :]
            return (
                jnp.where(row_bit == 0, lower, upper)[None],
                jnp.where(row_bit == 0, upper, lower)[None],
            )

    high_a = over_high(pack_a)
    got_rows = swap_x(sent_rows)
    all_rows = (keep_rows, got_rows, swap_core(keep_rows), swap_core(got_rows))
    a_y = swap_y(high_a)
    a_x = swap_x(high_a)
    h1, token = call(
        norm_kernel,
        "first_norm",
        (),
        (*all_rows, norm_gains),
        (sds((seq, D), bf16), sds((8, 128), f32)),
    )
    (pack_ud,) = call(
        pack_ud_kernel,
        "pack_ud",
        (),
        (up_master, down_master.T),
        (sds((high, 2, shard_rows, units), bf16),),
        gates=(token,),
    )
    high_ud = over_high(pack_ud)

    a_other = (a_x, swap_y(a_x))
    wT0, qkvT0, oT0, lse0 = attend(0, segment_ids, position_bias, h1, order((high_a, a_y)))
    (relay_ud,) = call(relay_kernel, "relay_ud", (), (high_ud,), (sds(high_ud.shape, bf16),), gates=(lse0,))
    ud_x = swap_x(relay_ud)
    ud_y = swap_y(relay_ud)
    wT1, qkvT1, oT1, lse1 = attend(2, segment_ids, position_bias, h1, order(a_other))

    keep, send = call(
        project_kernel,
        "project",
        (),
        (oT0, oT1, wT0, wT1),
        (sds(half, f32), sds(half, bf16)),
        (pltpu.VMEM((seq, 2 * width), bf16),),
    )
    x2, h2 = call(
        middle_kernel,
        "second_norm",
        (),
        (keep_rows, got_rows, keep, swap_core(send), norm_gains),
        (sds(half, f32), sds(half, bf16)),
    )
    h2_other = swap_core(h2)
    picked_u, picked_d = call(
        pick_kernel,
        "pick_ud",
        (),
        (ud_x, ud_y),
        (sds((high, shard_rows, units), bf16),) * 2,
        gates=(h2,),
    )
    u_xy = swap_y(picked_u)
    d_xy = swap_x(picked_d)

    def of_y(grad, wanted):
        blocks = grad.reshape((high, 2, shard_rows) + grad.shape[1:])
        return lax.dynamic_index_in_dim(blocks, wanted, 1, keepdims=False)

    def by_y(grads):
        if aligned:
            return tuple(grads)
        return tuple(of_y(grad, wanted) for grad in grads for wanted in (row_bit, 1 - row_bit))

    def plus(name, *terms, gates=()):
        outs = (sds(terms[0].shape, bf16), sds((8, 128), f32))
        return call(add_kernel, name, (), terms, outs, gates=gates)

    def over_high_bits(name, *terms, gates=()):
        if high != 4:
            total, token = plus(name, *terms, gates=gates)
            return (over_high(total),), token
        block = terms[0].shape[1:]
        own, *sent, token = call(
            send_kernel,
            name,
            (),
            terms,
            (sds(block, f32),) + (sds(block, bf16),) * 3 + (sds((8, 128), f32),),
            (pltpu.VMEM(terms[0].shape, f32),),
            gates=gates,
        )
        return (own, *(swap_dp(piece, 2 * bits) for bits, piece in enumerate(sent, 1))), token

    feed_scratch = (
        *([pltpu.VMEM((D, units), bf16)] * 2),
        *([pltpu.VMEM((seq, units), bf16)] * 2),
        pltpu.VMEM((2, D, units), bf16),
    )
    dh_part, pool_part, hot, *grads = call(
        feed_own_kernel,
        "feed_own",
        (),
        (h2, h2_other, *all_rows, *order((relay_ud, ud_y)), segment_ids, x2),
        (sds((seq, D), f32), sds((SEGS, D), f32), sds((SEGS, seq), bf16), *blocks_out, *blocks_out),
        feed_scratch,
        limit=FEED_LIMIT,
    )
    gu0_own, gu0_oth, gd0_own, gd0_oth = by_y(grads)
    if aligned:
        ud_other = (ud_x, u_xy, d_xy)
    else:
        first, second = order((ud_x, jnp.stack([u_xy, d_xy], axis=1)))
        ud_other = (first, second[:, 0], second[:, 1])
    keep, send, pool_part, *grads = call(
        feed_other_kernel,
        "feed_other",
        (),
        (h2, h2_other, *all_rows, *ud_other, hot, dh_part, pool_part),
        (sds(half, f32), sds(half, bf16), sds((SEGS, D), f32), *blocks_out, *blocks_out),
        feed_scratch,
        limit=FEED_LIMIT,
    )
    got = swap_core(send)
    gu1_own, gu1_oth, gd1_own, gd1_oth = by_y(grads)
    up_y1 = swap_y(gu1_oth)
    down_x1 = swap_x(gd1_oth)
    dx2, da, gain_grad_second = call(
        middle_back_kernel,
        "second_norm_back",
        (),
        (x2, keep, got, keep_rows, got_rows, norm_gains),
        (sds(half, f32), sds(half, bf16), sds((1, D), f32)),
        work=10,
    )
    da_other = swap_core(da)
    doT0, doT1, goT0, goT1 = call(
        branch_back_kernel,
        "branch_back",
        (),
        (da, da_other, wT0, wT1, oT0, oT1),
        (sds((width, seq), bf16),) * 2 + (sds((width, D), bf16),) * 2,
        (pltpu.VMEM((seq, D), bf16),),
        work=10,
    )
    up_late, down_late = call(
        relay_kernel,
        "relay_grads",
        (),
        (gu0_oth, gd1_own),
        (sds(gu0_oth.shape, bf16),) * 2,
        gates=(doT0,),
    )
    up_y0 = swap_y(up_late)
    down_x0 = swap_x(down_late)
    dqkvT1, *ga1, dbias1 = attend_back(
        2, segment_ids, position_bias, qkvT1, doT1, lse1, h1, goT1, blocks_out, ()
    )
    up_add, down_add, token = call(
        add_pairs_kernel,
        "add_ud",
        (),
        (gu1_own, up_y1, gd0_oth, down_x1),
        (sds(gu1_own.shape, bf16),) * 2 + (sds((8, 128), f32),),
        gates=(dbias1,),
    )
    up_x = swap_x(up_add)
    down_y = swap_y(down_add)
    ga1_own, ga1_oth = by_y(ga1)
    a_y1 = swap_y(ga1_oth)
    dqkvT0, *ga0, dbias0 = attend_back(
        0, segment_ids, position_bias, qkvT0, doT0, lse0, h1, goT0, blocks_out, (token,)
    )
    ga0_own, ga0_oth = by_y(ga0)
    a_y0 = swap_y(ga0_oth)
    token = dbias0
    up_pieces, token = over_high_bits("total_up", gu0_own, up_y0, up_x, gates=(token,))
    down_pieces, token = over_high_bits("total_down", gd0_own, down_x0, down_y, gates=(token,))
    grad_up, up_squares = call(
        finish_kernel,
        "finish_up",
        (),
        up_pieces,
        (sds((shard_rows, units), f32), sds((8, 128), f32)),
        gates=(token,),
    )
    token = up_squares
    a_add, token = plus("add_a", ga1_own, a_y1, gates=(token,))
    a_x1 = swap_x(a_add)
    keep, send, token = call(
        first_back_kernel,
        "first_back",
        (),
        (dqkvT0, dqkvT1, wT0, wT1),
        (sds(half, f32), sds(half, bf16), sds((8, 128), f32)),
        (pltpu.VMEM((seq, 6 * width), bf16),),
        gates=(token,),
    )
    first_got = swap_core(send)
    grad_downT, down_squares = call(
        finish_kernel,
        "finish_down",
        (),
        down_pieces,
        (sds((shard_rows, units), f32), sds((8, 128), f32)),
        gates=(token,),
    )
    token = down_squares
    a_pieces, token = over_high_bits("total_a", ga0_own, a_y0, a_x1, gates=(token,))
    tg_own, tg_away, gain_grad_first, mean_keep = call(
        token_grad_kernel,
        "first_norm_back",
        (),
        (keep_rows, got_rows, keep, first_got, dx2, norm_gains, pool_part, swap_core(pool_part), hot),
        (
            sds((length, D), f32),
            sds((length + SEGS, D), bf16),
            sds((1, D), f32),
            sds((SEGS, width), f32),
        ),
        gates=(token,),
    )
    tg_got = swap_x(tg_away)
    devices = dp_size * lax.axis_size("tensor")
    def from_all(value):
        return lax.all_to_all(value, ("dp", "tensor"), 0, 0, tiled=True)

    if aligned:
        grad_qkv, grad_out, squares = call(
            finish_a_kernel,
            "finish_a",
            (),
            (*a_pieces, up_squares, down_squares),
            (sds(qkv_master.shape, f32), sds(out_master.shape, f32), sds((8, 128), f32)),
            gates=(gain_grad_first,),
        )
    else:
        grad_a = jnp.sum(a_pieces[0].astype(f32), axis=0)
        grad_qkv = jnp.stack([grad_a[:, i * width : (i + 1) * width] for i in range(3)])
        grad_out = grad_a[:, 3 * width :].T
        squares = jnp.broadcast_to(
            up_squares + down_squares + jnp.sum(grad_a * grad_a), (8, 128)
        )

    (small,) = call(
        small_kernel,
        "small",
        (),
        (gain_grad_first, gain_grad_second, dbias0, dbias1, squares),
        (sds((devices, SMALL_ROWS, 128), f32),),
    )
    small_all = from_all(small)
    tokens_grad, pooled = call(
        place_kernel,
        "tokens_grad",
        (),
        (tg_own, tg_got, mean_keep),
        (sds(tokens.shape, f32), sds((rows, SEGS, width), f32)),
        gates=(small,),
    )
    groups = (
        (qkv_master, grad_qkv, qkv_first, qkv_second),
        (out_master, grad_out, out_first, out_second),
        (up_master, grad_up, up_first, up_second),
        (down_master.T, grad_downT, down_first.T, down_second.T),
        (norm_gains, None, gain_first, gain_second),
        (position_bias.T, None, bias_first.T, bias_second.T),
    )
    operands = [array for group in groups for array in group if array is not None]
    updates = pl.pallas_call(
        adam_kernel,
        out_shape=[sds(group[0].shape, f32) for group in groups for _ in range(2)]
        + [sds(norm_gains.shape, f32), sds(position_bias.shape[::-1], f32), sds((1, 1), f32)],
        in_specs=[VMEM_SPEC] + [pl.BlockSpec(memory_space=pltpu.HBM)] * (len(operands) + 1),
        out_specs=[pl.BlockSpec(memory_space=pltpu.HBM)] * 8 + [VMEM_SPEC] * 6 + [SMEM_SPEC],
        scratch_shapes=[pltpu.VMEM(array.shape, f32) for array in operands]
        + [pltpu.VMEM(group[0].shape, f32) for group in groups[:4] for _ in range(2)]
        + [pltpu.SemaphoreType.DMA((len(operands),)), pltpu.SemaphoreType.DMA((8,))],
        compiler_params=pltpu.CompilerParams(vmem_limit_bytes=60 << 20),
        name="adam",
    )(small_all, *operands, pooled)
    new_qkv, second_qkv, new_out, second_out, new_up, second_up = updates[0:6]
    new_gains, second_gains = updates[8:10]
    new_down, second_down, new_bias, second_bias = (updates[i].T for i in (6, 7, 10, 11))
    grad_gains, grad_biasT = updates[12:14]
    grad_down, grad_bias = grad_downT.T, grad_biasT.T
    gradient_norm = updates[14].reshape(())
    return (
        pooled,
        tokens_grad,
        grad_qkv,
        grad_out,
        grad_up,
        grad_down,
        grad_gains,
        grad_bias,
        gradient_norm,
        new_qkv,
        new_out,
        new_up,
        new_down,
        new_gains,
        new_bias,
        second_qkv,
        second_out,
        second_up,
        second_down,
        second_gains,
        second_bias,
    )


def solution(mesh):
    in_specs = (
        P("dp", "tensor", None),
        P("dp", None),
        P("dp", "tensor", None),
        P(None, "dp", "tensor"),
        P("tensor", "dp"),
        P("dp", "tensor"),
        P("tensor", "dp"),
        P(),
        P(),
        P(None, "dp", "tensor"),
        P(None, "dp", "tensor"),
        P("tensor", "dp"),
        P("tensor", "dp"),
        P("dp", "tensor"),
        P("dp", "tensor"),
        P("tensor", "dp"),
        P("tensor", "dp"),
        P(),
        P(),
        P(),
        P(),
    )
    out_specs = (
        P("dp", None, "tensor"),
        P("dp", "tensor", None),
        P(None, "dp", "tensor"),
        P("tensor", "dp"),
        P("dp", "tensor"),
        P("tensor", "dp"),
        P(),
        P(),
        P(),
        P(None, "dp", "tensor"),
        P("tensor", "dp"),
        P("dp", "tensor"),
        P("tensor", "dp"),
        P(),
        P(),
        P(None, "dp", "tensor"),
        P("tensor", "dp"),
        P("dp", "tensor"),
        P("tensor", "dp"),
        P(),
        P(),
    )
    return jax.shard_map(
        per_device, mesh=mesh, in_specs=in_specs, out_specs=out_specs, check_vma=False
    )
```

```python
import functools

import jax
import jax.numpy as jnp
from jax import lax
from jax.experimental import pallas as pl
from jax.experimental.pallas import tpu as pltpu
from jax.sharding import PartitionSpec as P

D = 768
H = 12
DH = 64
FF = 3072
SEGS = 16
STEP = 10

norm_eps = 1e-06
mask_fill = -1000000000.0
clip_level = 1.0
beta_first = 0.9
beta_second = 0.999
adam_eps = 1e-08
decay_rate = 0.1
gelu_scale = 0.7978845608028654
gelu_cubic = 0.044715

bf16 = jnp.bfloat16
f32 = jnp.float32
i32 = jnp.int32

SMALL_ROWS = 16
BUCKETS = 32
QB = 256
KC = 128
EDGE = 128
NEAR = QB + 2 * EDGE
VMEM_LIMIT = 20 << 20
FULL_LIMIT = 60 << 20
FEED_LIMIT = 36 << 20
FILL = 1_000_000_000

SMEM_SPEC = pl.BlockSpec(memory_space=pltpu.SMEM)
VMEM_SPEC = pl.BlockSpec(memory_space=pltpu.VMEM)


def sds(shape, dtype):
    return jax.ShapeDtypeStruct(shape, dtype)


def nt(a, b):
    return lax.dot_general(a, b, (((1,), (1,)), ((), ())), preferred_element_type=f32)


def nn(a, b):
    return lax.dot_general(a, b, (((1,), (0,)), ((), ())), preferred_element_type=f32)


def call(body, name, smem, vmem, outs, scratch=(), gates=(), work=0, limit=VMEM_LIMIT):
    first, taken = len(smem) + len(vmem), len(gates)

    def gated(*refs):
        body(*refs[:first], *refs[first + taken :])

    return pl.pallas_call(
        gated if gates else body,
        out_shape=tuple(outs),
        in_specs=[SMEM_SPEC] * len(smem)
        + [VMEM_SPEC] * len(vmem)
        + [pl.BlockSpec(memory_space=pl.ANY)] * taken,
        out_specs=(VMEM_SPEC,) * len(outs),
        scratch_shapes=list(scratch),
        compiler_params=pltpu.CompilerParams(vmem_limit_bytes=limit),
        cost_estimate=pl.CostEstimate(
            flops=max(1, work * FILL), bytes_accessed=1000, transcendentals=0
        ),
        name=name,
    )(*smem, *vmem, *gates)


def bucket_of(offset):
    distance = jnp.abs(offset)
    large = 8 + sum(
        ((distance >= threshold).astype(jnp.int32) for threshold in (12, 16, 23, 32, 46, 64, 91))
    )
    inner_bucket = jnp.where(distance < 8, distance, large)
    return inner_bucket + jnp.where(offset > 0, 16, 0)


def learning_rates_plain():
    return (
        (2.0 * (D * DH) ** (-0.5), 2.0 * D ** (-0.5), 2.0 * D ** (-0.5)),
        0.5 * (H * DH / 16) ** (-0.5),
        0.5 * D ** (-0.5),
        2.0 * FF ** (-0.5),
        0.25,
        0.5,
    )


def adam_update(parameter, gradient, first_moment, second_moment, step_rate, clip_factor):
    clipped = gradient * clip_factor
    first_new = beta_first * first_moment + (1.0 - beta_first) * clipped
    second_new = beta_second * second_moment + (1.0 - beta_second) * clipped * clipped
    first_hat = first_new / (1.0 - beta_first**STEP)
    second_hat = second_new / (1.0 - beta_second**STEP)
    updated = parameter - step_rate * (
        first_hat / (jnp.sqrt(second_hat) + adam_eps) + decay_rate * parameter
    )
    return (updated, second_new)


def swap_core(value):
    return lax.ppermute(value, "tensor", [(i, i ^ 1) for i in range(lax.axis_size("tensor"))])


def swap_x(value):
    return lax.ppermute(value, "tensor", [(i, i ^ 2) for i in range(lax.axis_size("tensor"))])


def swap_dp(value, bits):
    return lax.ppermute(value, "dp", [(i, i ^ bits) for i in range(lax.axis_size("dp"))])


def swap_y(value):
    return swap_dp(value, 1)


def over_high(blocks):
    size = lax.axis_size("dp")
    groups = [[index for index in range(size) if index % 2 == bit] for bit in range(2)]
    return lax.all_to_all(blocks, "dp", 0, 0, tiled=True, axis_index_groups=groups)


def row_places():
    rank = lax.axis_index("tensor")
    return (rank, rank ^ 2, rank ^ 1, rank ^ 3)


def bias_tiles(bias_ref, first_head, heads, near_ref):
    span = 2 * NEAR
    lane = lax.broadcasted_iota(i32, (8, span), 1)
    offset = -EDGE - jnp.where(lane < span // 2, lane, lane - span)
    buckets = bucket_of(offset)
    values = [
        jnp.where(offset > 0, bias_ref[first_head + h, 31], bias_ref[first_head + h, 15])
        for h in range(heads)
    ]
    for bucket in list(range(15)) + list(range(17, 31)):
        here = buckets == bucket
        values = [
            jnp.where(here, bias_ref[first_head + h, bucket], values[h]) for h in range(heads)
        ]
    for h in range(heads):
        line = jnp.broadcast_to(values[h][0:1, :], (NEAR, span))
        near_ref[h] = pltpu.roll(line, 0, 1, stride=1, stride_axis=0)[:, :QB]


def rms_of(values):
    return lax.rsqrt(jnp.mean(values * values, axis=-1, keepdims=True) + norm_eps)


def norm_kernel(keep_ref, got_ref, keep_oth_ref, got_oth_ref, gain_ref, h_ref, token_ref):
    token_ref[...] = jnp.zeros_like(token_ref)
    length = keep_ref.shape[0]
    blocks = (keep_ref, got_ref, keep_oth_ref, got_oth_ref)
    for place, block in zip(row_places(), blocks):
        start = pl.multiple_of(place * length, length)
        values = block[...].astype(f32)
        h_ref[pl.ds(start, length), :] = (values * rms_of(values) * gain_ref[0:1, :]).astype(bf16)


def place_weights(pieces, target, kind=None):
    bit = lax.axis_index("dp") % 2
    for index, piece in enumerate(pieces):
        rows = piece.shape[-2]
        lowest = bit if index == 0 else 1 - bit
        for slot in range(piece.shape[0]):
            start = pl.multiple_of((2 * slot + lowest) * rows, 16)
            target[pl.ds(start, rows), :] = piece[slot] if kind is None else piece[slot, kind]


def split_rows(source, own_ref, other_ref):
    rows = own_ref.shape[1]
    bit = lax.axis_index("dp") % 2
    for block in range(own_ref.shape[0]):
        start = pl.multiple_of((2 * block + bit) * rows, 16)
        own_ref[block] = source[pl.ds(start, rows), :]
        start = pl.multiple_of((2 * block + 1 - bit) * rows, 16)
        other_ref[block] = source[pl.ds(start, rows), :]


def sub_sum(values):
    return jnp.sum(values.reshape(values.shape[0] // 8, 8, values.shape[1]), axis=0)


def sub_max(values):
    return jnp.max(values.reshape(values.shape[0] // 8, 8, values.shape[1]), axis=0)


def blocks_even(seq):
    return (seq // QB) % 2 == 0


def near_row(block, chunk):
    start = chunk * KC - block * QB + EDGE
    return start if 0 <= start and start + KC <= NEAR else None


def same_segment(seg_keys, keys, seg_query):
    seg_key = seg_keys[keys, :]
    return jnp.concatenate([seg_key] * (QB // seg_key.shape[1]), axis=1) == seg_query


def segments(seg_ref):
    return seg_ref[pl.ds(lax.axis_index("tensor") // 2, 1), :]


def one_item(seg_smem_ref):
    side = lax.axis_index("tensor") // 2
    return seg_smem_ref[side, 0] == seg_smem_ref[side, seg_smem_ref.shape[1] - 1]


def head_of(shift, heads):
    return (lax.axis_index("tensor") ^ shift) * heads


def attend_kernel(
    shift, seg_smem_ref, bias_ref, h_ref, piece_a_ref, piece_b_ref, seg_ref,
    wT_ref, qkvT_ref, oT_ref, lse_ref, w_buf, k_buf, s_buf, p_buf, near_ref, segk_ref,
):
    seq = h_ref.shape[0]
    heads = near_ref.shape[0]
    width = oT_ref.shape[0]
    first_head = head_of(shift, heads)
    bias_tiles(bias_ref, first_head, heads, near_ref)
    size = width // heads
    chunks = seq // KC
    assert blocks_even(seq)
    place_weights((piece_a_ref, piece_b_ref), w_buf)
    wT_ref[...] = w_buf[...].T
    qkvT_ref[...] = nt(wT_ref[0 : 3 * width, :], h_ref[...]).astype(bf16)
    blocks = seq // QB

    def rows(part, h):
        return pl.ds(pl.multiple_of(part * width + h * size, size), size)

    def score(h, block):
        s_buf[block % 2] = nn(k_buf[h % 2], qkvT_ref[rows(0, h), block * QB : (block + 1) * QB])

    def soften(h, block, masked):
        slot = block % 2
        qs = slice(block * QB, (block + 1) * QB)
        top = jnp.full((8, QB), -3e38, f32)
        for chunk in range(chunks):
            ks = slice(chunk * KC, (chunk + 1) * KC)
            row = near_row(block, chunk)
            if row is None:
                scores = s_buf[slot, ks, :] + bias_ref[first_head + h, 15 if chunk * KC < block * QB else 31]
            else:
                scores = s_buf[slot, ks, :] + near_ref[h, row : row + KC, :]
            if masked:
                scores = jnp.where(same_segment(segk_ref, ks, segq[:, qs]), scores, mask_fill)
            s_buf[slot, ks, :] = scores
            top = jnp.maximum(top, sub_max(scores))
        top = jnp.max(top, axis=0, keepdims=True)
        total = jnp.zeros((8, QB), f32)
        for chunk in range(chunks):
            ks = slice(chunk * KC, (chunk + 1) * KC)
            exps = jnp.exp(s_buf[slot, ks, :] - top)
            s_buf[slot, ks, :] = exps
            total = total + sub_sum(exps)
        total = jnp.sum(total, axis=0, keepdims=True)
        scale = 1.0 / total
        for chunk in range(chunks):
            ks = slice(chunk * KC, (chunk + 1) * KC)
            p_buf[slot, ks, :] = (s_buf[slot, ks, :] * scale).astype(bf16)
        lse_ref[pl.ds(h, 1), qs] = top + jnp.log(total)

    def mix(h, block):
        qs = slice(block * QB, (block + 1) * QB)
        oT_ref[rows(0, h), qs] = nn(qkvT_ref[rows(2, h), :], p_buf[block % 2]).astype(bf16)

    segq = segments(seg_ref)

    def run(masked):
        if masked:
            segk_ref[...] = jnp.broadcast_to(segq, (128, seq)).T
        k_buf[0] = qkvT_ref[rows(1, 0), :].T
        score(0, 0)

        def head(h, carried):
            for block in range(blocks):
                if block + 1 < blocks:
                    score(h, block + 1)
                else:
                    later = jnp.minimum(h + 1, heads - 1)
                    k_buf[(h + 1) % 2] = qkvT_ref[rows(1, later), :].T
                    s_buf[0] = nn(k_buf[(h + 1) % 2], qkvT_ref[rows(0, later), 0:QB])
                soften(h, block, masked)
                if block:
                    mix(h, block - 1)
            mix(h, blocks - 1)
            return carried

        lax.fori_loop(0, heads, head, 0)

    single = one_item(seg_smem_ref)

    @pl.when(single)
    def _():
        run(False)

    @pl.when(jnp.logical_not(single))
    def _():
        run(True)


def attend(shift, seg, bias, h, pieces):
    seq = h.shape[0]
    cols = pieces[0].shape[2]
    width = cols // 4
    heads = bias.shape[0] // 4
    return call(
        functools.partial(attend_kernel, shift),
        "attend",
        (seg, bias),
        (h, *pieces, seg),
        (sds((cols, D), bf16), sds((3 * width, seq), bf16), sds((width, seq), bf16), sds((8, seq), f32)),
        (
            pltpu.VMEM((D, cols), bf16),
            pltpu.VMEM((2, seq, width // heads), bf16),
            pltpu.VMEM((2, seq, QB), f32),
            pltpu.VMEM((2, seq, QB), bf16),
            pltpu.VMEM((heads, NEAR, QB), f32),
            pltpu.VMEM((seq, 128), i32),
        ),
    )


def attend_back_kernel(
    shift, seg_smem_ref, bias_ref, qkvT_ref, doT_ref, lse_ref, seg_ref, h_ref, goT_ref,
    dqkvT_ref, own_ref, other_ref, dbias_ref,
    kv_buf, s_buf, dp_buf, ds_buf, pt_buf, dt_buf, dk_buf, dv_buf, g_buf, near_ref, segk_ref,
    dnear_ref, dfar_ref, line_buf,
):
    width, seq = doT_ref.shape
    heads = near_ref.shape[0]
    first_head = head_of(shift, heads)
    bias_tiles(bias_ref, first_head, heads, near_ref)
    segq = segments(seg_ref)
    size = width // heads
    blocks = seq // QB
    chunks = seq // KC
    assert blocks_even(seq)

    def rows(part, h):
        return pl.ds(pl.multiple_of(part * width + h * size, size), size)

    def key_values(h, turn):
        kv_buf[turn] = jnp.concatenate([qkvT_ref[rows(1, h), :], qkvT_ref[rows(2, h), :]], axis=0).T

    def products(h, turn, block):
        slot = block % 2
        qs = slice(block * QB, (block + 1) * QB)
        zeros = jnp.zeros((size, QB), bf16)
        s_buf[slot] = nn(kv_buf[turn], jnp.concatenate([qkvT_ref[rows(0, h), qs], zeros], axis=0))
        dp_buf[slot] = nn(kv_buf[turn], jnp.concatenate([zeros, doT_ref[rows(0, h), qs]], axis=0))

    def soften(h, block, masked):
        slot = block % 2
        qs = slice(block * QB, (block + 1) * QB)
        lse = lse_ref[pl.ds(h, 1), qs]
        lse_left = lse - bias_ref[first_head + h, 15]
        lse_right = lse - bias_ref[first_head + h, 31]
        dots = jnp.zeros((8, QB), f32)
        for chunk in range(chunks):
            ks = slice(chunk * KC, (chunk + 1) * KC)
            row = near_row(block, chunk)
            if row is None:
                scores = s_buf[slot, ks, :] - (lse_left if chunk * KC < block * QB else lse_right)
            else:
                scores = s_buf[slot, ks, :] + near_ref[h, row : row + KC, :] - lse
            probs = jnp.exp(scores)
            if masked:
                probs = jnp.where(same_segment(segk_ref, ks, segq[:, qs]), probs, 0.0)
            s_buf[slot, ks, :] = probs
            pt_buf[slot, :, ks] = probs.astype(bf16).T
            dots = dots + sub_sum(probs * dp_buf[slot, ks, :])
        dots = jnp.sum(dots, axis=0, keepdims=True)
        for chunk in range(chunks):
            ks = slice(chunk * KC, (chunk + 1) * KC)
            d_scores = (s_buf[slot, ks, :] * (dp_buf[slot, ks, :] - dots)).astype(bf16)
            ds_buf[slot, ks, :] = d_scores
            dt_buf[slot, :, ks] = d_scores.T
            row = near_row(block, chunk)
            if row is not None:
                if block == 0 or (block == 1 and row == 0):
                    dnear_ref[h, row : row + KC, :] = d_scores.astype(f32)
                else:
                    dnear_ref[h, row : row + KC, :] += d_scores.astype(f32)

    def outputs(h, block):
        slot = block % 2
        qs = slice(block * QB, (block + 1) * QB)
        dqkvT_ref[rows(0, h), qs] = nn(qkvT_ref[rows(1, h), :], ds_buf[slot]).astype(bf16)
        d_keys = nn(
            jnp.concatenate([qkvT_ref[rows(0, h), qs], jnp.ones((16, QB), bf16)], axis=0),
            dt_buf[slot],
        )
        d_values = nn(doT_ref[rows(0, h), qs], pt_buf[slot])
        if block == 0:
            dk_buf[...] = d_keys[0:size]
            dv_buf[...] = d_values
        elif block + 1 < blocks:
            dk_buf[...] += d_keys[0:size]
            dv_buf[...] += d_values
        else:
            dqkvT_ref[rows(1, h), :] = (dk_buf[...] + d_keys[0:size]).astype(bf16)
            dqkvT_ref[rows(2, h), :] = (dv_buf[...] + d_values).astype(bf16)
        sums = d_keys[size : size + 1]
        left_end = max(0, block * QB - EDGE)
        right_start = min(seq, block * QB + QB + EDGE)
        lane = lax.broadcasted_iota(i32, (1, 128), 1)
        line = jnp.zeros((1, 128), f32)
        if left_end:
            line = jnp.where(lane == 0, jnp.sum(sums[:, :left_end], axis=1, keepdims=True), line)
        if right_start < seq:
            line = jnp.where(lane == 1, jnp.sum(sums[:, right_start:], axis=1, keepdims=True), line)
        if block == 0:
            dfar_ref[pl.ds(h, 1), :] = line
        else:
            dfar_ref[pl.ds(h, 1), :] += line

    def run(masked):
        if masked:
            segk_ref[...] = jnp.broadcast_to(segq, (128, seq)).T
        key_values(0, 0)
        products(0, 0, 0)

        def head(h, carried):
            for block in range(blocks):
                if block + 1 < blocks:
                    products(h, h % 2, block + 1)
                else:
                    later = jnp.minimum(h + 1, heads - 1)
                    key_values(later, (h + 1) % 2)
                    products(later, (h + 1) % 2, 0)
                soften(h, block, masked)
                if block:
                    outputs(h, block - 1)
            outputs(h, blocks - 1)
            return carried

        lax.fori_loop(0, heads, head, 0)

    single = one_item(seg_smem_ref)

    @pl.when(single)
    def _():
        run(False)

    @pl.when(jnp.logical_not(single))
    def _():
        run(True)

    dfar_ref[heads:, :] = jnp.zeros((8 - heads, 128), f32)
    grad = jnp.concatenate([nn(dqkvT_ref[...], h_ref[...]).astype(bf16), goT_ref[...]], axis=0)
    if other_ref is None:
        own_ref[...] = grad.T
    else:
        g_buf[...] = grad.T
        split_rows(g_buf, own_ref, other_ref)
    bias_gradients(dnear_ref, dfar_ref, line_buf, dbias_ref)


def attend_back(shift, seg, bias, qkvT, doT, lse, h, goT, grad_outs, gates):
    width, seq = doT.shape
    heads = bias.shape[0] // 4
    size = width // heads
    body = functools.partial(attend_back_kernel, shift)
    if len(grad_outs) == 1:

        def body(*refs):
            attend_back_kernel(shift, *refs[:10], None, *refs[10:])

    return call(
        body,
        "attend_back",
        (seg, bias),
        (qkvT, doT, lse, seg, h, goT),
        (sds(qkvT.shape, bf16), *grad_outs, sds((8, 128), f32)),
        (
            pltpu.VMEM((2, seq, 2 * size), bf16),
            pltpu.VMEM((2, seq, QB), f32),
            pltpu.VMEM((2, seq, QB), f32),
            pltpu.VMEM((2, seq, QB), bf16),
            pltpu.VMEM((2, QB, seq), bf16),
            pltpu.VMEM((2, QB, seq), bf16),
            pltpu.VMEM((size, seq), f32),
            pltpu.VMEM((size, seq), f32),
            pltpu.VMEM((D, 4 * width), bf16),
            pltpu.VMEM((heads, NEAR, QB), f32),
            pltpu.VMEM((seq, 128), i32),
            pltpu.VMEM((heads, NEAR, QB), f32),
            pltpu.VMEM((8, 128), f32),
            pltpu.VMEM((8, 2 * NEAR), f32),
        ),
        gates,
    )


def project_kernel(oT0_ref, oT1_ref, wT0_ref, wT1_ref, keep_ref, send_ref, o_buf):
    width = oT0_ref.shape[0]
    length = keep_ref.shape[0] // 2
    o_buf[...] = jnp.concatenate([oT0_ref[...], oT1_ref[...]], axis=0).T
    w = jnp.concatenate([wT0_ref[3 * width :, :], wT1_ref[3 * width :, :]], axis=0)
    for index, place in enumerate(row_places()):
        start = pl.multiple_of(place * length, length)
        part = nn(o_buf[pl.ds(start, length), :], w)
        rows = slice((index % 2) * length, (index % 2 + 1) * length)
        if index < 2:
            keep_ref[rows, :] = part
        else:
            send_ref[rows, :] = part.astype(send_ref.dtype)


def middle_kernel(keep_row_ref, got_row_ref, part_ref, got_ref, gain_ref, x2_ref, h_ref):
    length = keep_row_ref.shape[0]
    for index, block in enumerate((keep_row_ref, got_row_ref)):
        rows = slice(index * length, (index + 1) * length)
        values = block[...].astype(f32) + part_ref[rows, :] + got_ref[rows, :].astype(f32)
        x2_ref[rows, :] = values
        h_ref[rows, :] = (values * rms_of(values) * gain_ref[1:2, :]).astype(bf16)


def split3(values):
    high = values.astype(bf16)
    rest = values - high.astype(f32)
    mid = rest.astype(bf16)
    low = (rest - mid.astype(f32)).astype(bf16)
    return high, mid, low


def feed_rows(h, cot, u_buf, d_buf, act_ref, dpre_ref, rows):
    pre = nn(h, u_buf[...])
    d_act = nn(cot, d_buf[...])
    square = pre * pre
    bent = jnp.tanh(gelu_scale * pre * (1.0 + gelu_cubic * square))
    half_up = 0.5 * (1.0 + bent)
    act_ref[rows, :] = (pre * half_up).astype(bf16)
    slope = half_up + (0.5 * gelu_scale) * pre * (1.0 - bent * bent) * (
        1.0 + (3.0 * gelu_cubic) * square
    )
    d_pre = (d_act * slope).astype(bf16)
    dpre_ref[rows, :] = d_pre
    return nt(d_pre, u_buf[...])


def pooled_units(hot, act_ref, d_buf):
    pooled = None
    for term in split3(nn(hot, act_ref[...])):
        part = nt(term, d_buf[...])
        pooled = part if pooled is None else pooled + part
    return pooled


def weight_grads(h_refs, cots, act_ref, dpre_ref, outs, g_buf):
    hT = jnp.concatenate([ref[...] for ref in h_refs], axis=0).T
    cotT = jnp.concatenate([block[...] for block in cots], axis=0).T
    if len(outs) == 2:
        outs[0][...] = nn(hT, dpre_ref[...]).astype(bf16)
        outs[1][...] = nn(cotT, act_ref[...]).astype(bf16)
    else:
        g_buf[0] = nn(hT, dpre_ref[...]).astype(bf16)
        split_rows(g_buf.at[0], outs[0], outs[1])
        g_buf[1] = nn(cotT, act_ref[...]).astype(bf16)
        split_rows(g_buf.at[1], outs[2], outs[3])


def feed_own_kernel(
    h_own_ref, h_oth_ref, keep_ref, got_ref, keep_oth_ref, got_oth_ref,
    a_ref, b_ref, seg_ref, x2_ref, dh_ref, pooled_ref, hot_ref, *refs
):
    *outs, u_buf, d_buf, act_buf, dpre_buf, g_buf = refs
    place_weights((a_ref, b_ref), u_buf, 0)
    place_weights((a_ref, b_ref), d_buf, 1)
    length = keep_ref.shape[0]
    cots = (keep_ref, got_ref, keep_oth_ref, got_oth_ref)
    line = seg_ref[pl.ds(lax.axis_index("tensor") // 2, 1), :]
    seq = line.shape[1]
    item = lax.broadcasted_iota(i32, (SEGS, seq), 0)
    whole = (jnp.broadcast_to(line, (SEGS, seq)) == item).astype(f32)
    for index, place in enumerate(row_places()):
        part = jnp.zeros((SEGS, length), f32)
        for block in range(4):
            part = jnp.where(place == block, whole[:, block * length : (block + 1) * length], part)
        hot_ref[:, index * length : (index + 1) * length] = part.astype(bf16)
    for index in range(4):
        rows = slice(index * length, (index + 1) * length)
        half = slice((index % 2) * length, (index % 2 + 1) * length)
        h = (h_own_ref if index < 2 else h_oth_ref)[half, :]
        dh_ref[rows, :] = feed_rows(h, cots[index][...], u_buf, d_buf, act_buf, dpre_buf, rows)
    hot = hot_ref[...]
    pooled = pooled_units(hot, act_buf, d_buf)
    for term in split3(x2_ref[...]):
        pooled = pooled + nn(hot[:, 0 : 2 * length], term)
    pooled_ref[...] = pooled
    weight_grads((h_own_ref, h_oth_ref), cots, act_buf, dpre_buf, outs, g_buf)


def feed_other_kernel(
    h_own_ref, h_oth_ref, keep_ref, got_ref, keep_oth_ref, got_oth_ref,
    a_ref, ub_ref, db_ref, hot_ref, dh_ref, pool_ref,
    part_ref, send_ref, pooled_ref, *refs
):
    *outs, u_buf, d_buf, act_buf, dpre_buf, g_buf = refs
    place_weights((a_ref,), u_buf, 0)
    place_weights((a_ref,), d_buf, 1)
    bit = lax.axis_index("dp") % 2
    for source, target in ((ub_ref, u_buf), (db_ref, d_buf)):
        count = source.shape[1]
        for slot in range(source.shape[0]):
            start = pl.multiple_of((2 * slot + 1 - bit) * count, 16)
            target[pl.ds(start, count), :] = source[slot]
    length = keep_ref.shape[0]
    cots = (keep_ref, got_ref, keep_oth_ref, got_oth_ref)
    for index in (2, 3, 0, 1):
        rows = slice(index * length, (index + 1) * length)
        half = slice((index % 2) * length, (index % 2 + 1) * length)
        h = (h_own_ref if index < 2 else h_oth_ref)[half, :]
        total = dh_ref[rows, :] + feed_rows(
            h, cots[index][...], u_buf, d_buf, act_buf, dpre_buf, rows
        )
        if index < 2:
            part_ref[half, :] = total
        else:
            send_ref[half, :] = total.astype(send_ref.dtype)
    pooled_ref[...] = pool_ref[...] + pooled_units(hot_ref[...], act_buf, d_buf)
    weight_grads((h_own_ref, h_oth_ref), cots, act_buf, dpre_buf, outs, g_buf)


def norm_back(values, gain, upstream):
    scale = rms_of(values)
    normed = values * scale
    gain_grad = jnp.sum(upstream * normed, axis=0, keepdims=True)
    scaled = upstream * gain
    inner = jnp.mean(scaled * normed, axis=-1, keepdims=True)
    return scale * (scaled - normed * inner), gain_grad


def middle_back_kernel(
    x2_ref, part_ref, got_ref, keep_row_ref, got_row_ref, gain_ref, dx2_ref, da_ref, gain_grad_ref
):
    length = x2_ref.shape[0] // 2
    for index, cot in enumerate((keep_row_ref, got_row_ref)):
        rows = slice(index * length, (index + 1) * length)
        d_values, gain_grad = norm_back(
            x2_ref[rows, :], gain_ref[1:2, :], part_ref[rows, :] + got_ref[rows, :].astype(f32)
        )
        dx2 = cot[...].astype(f32) + d_values
        dx2_ref[rows, :] = dx2
        da_ref[rows, :] = dx2.astype(bf16)
        if index == 0:
            gain_grad_ref[...] = gain_grad
        else:
            gain_grad_ref[...] += gain_grad


def branch_back_kernel(
    da_own_ref, da_oth_ref, wT0_ref, wT1_ref, oT0_ref, oT1_ref,
    doT0_ref, doT1_ref, g0_ref, g1_ref, da_buf,
):
    width = oT0_ref.shape[0]
    length = da_own_ref.shape[0] // 2
    for index, place in enumerate(row_places()):
        start = pl.multiple_of(place * length, length)
        half = slice((index % 2) * length, (index % 2 + 1) * length)
        da_buf[pl.ds(start, length), :] = (da_own_ref if index < 2 else da_oth_ref)[half, :]
    da = da_buf[...]
    doT0_ref[...] = nt(wT0_ref[3 * width :, :], da).astype(bf16)
    doT1_ref[...] = nt(wT1_ref[3 * width :, :], da).astype(bf16)
    g0_ref[...] = nn(oT0_ref[...], da).astype(bf16)
    g1_ref[...] = nn(oT1_ref[...], da).astype(bf16)


def first_back_kernel(d0_ref, d1_ref, wT0_ref, wT1_ref, keep_ref, send_ref, token_ref, d_buf):
    token_ref[...] = jnp.zeros_like(token_ref)
    rows3 = d0_ref.shape[0]
    length = keep_ref.shape[0] // 2
    d_buf[...] = jnp.concatenate([d0_ref[...], d1_ref[...]], axis=0).T
    w = jnp.concatenate([wT0_ref[0:rows3, :], wT1_ref[0:rows3, :]], axis=0)
    places = row_places()
    for index in (2, 3, 0, 1):
        start = pl.multiple_of(places[index] * length, length)
        part = nn(d_buf[pl.ds(start, length), :], w)
        rows = slice((index % 2) * length, (index % 2 + 1) * length)
        if index < 2:
            keep_ref[rows, :] = part
        else:
            send_ref[rows, :] = part.astype(send_ref.dtype)


def token_grad_kernel(
    keep_row_ref, got_row_ref, part_ref, got_ref, dx2_ref, gain_ref, pool_ref, pool_got_ref, hot_ref,
    own_ref, away_ref, gain_grad_ref, mean_ref
):
    length = keep_row_ref.shape[0]
    away_ref[length:, :] = jnp.zeros((away_ref.shape[0] - length, away_ref.shape[1]), bf16)
    counts = jnp.sum(hot_ref[...].astype(f32), axis=1, keepdims=True)
    means = (pool_ref[...] + pool_got_ref[...]) / jnp.maximum(counts, 1.0)
    rank = lax.axis_index("tensor")
    width = mean_ref.shape[1]
    mine, sent = jnp.zeros(mean_ref.shape, f32), jnp.zeros(mean_ref.shape, f32)
    for shard in range(4):
        part = means[:, shard * width : (shard + 1) * width]
        mine = jnp.where(rank == shard, part, mine)
        sent = jnp.where(rank ^ 2 == shard, part, sent)
    mean_ref[...] = mine
    away_ref[length:, 0:width] = sent.astype(bf16)
    for index, block in enumerate((keep_row_ref, got_row_ref)):
        rows = slice(index * length, (index + 1) * length)
        d_values, gain_grad = norm_back(
            block[...].astype(f32), gain_ref[0:1, :], part_ref[rows, :] + got_ref[rows, :].astype(f32)
        )
        if index == 0:
            own_ref[...] = dx2_ref[rows, :] + d_values
            gain_grad_ref[...] = gain_grad
        else:
            away_ref[0:length, :] = (dx2_ref[rows, :] + d_values).astype(bf16)
            gain_grad_ref[...] += gain_grad


def bias_gradients(dnear_ref, dfar_ref, line_buf, grad_ref):
    heads = dnear_ref.shape[0]
    span = 2 * NEAR
    line_buf[...] = jnp.zeros_like(line_buf)
    for h in range(heads):
        values = dnear_ref[h]
        rows = NEAR
        while rows > 1:
            rows //= 2
            low, high = values[:rows], values[rows:]
            if rows % 128 == 0:
                pad = jnp.zeros((rows, rows), f32)
                values = jnp.concatenate([pad, low], axis=1) + jnp.concatenate([high, pad], axis=1)
            else:
                if values.shape[1] < span:
                    pad = jnp.zeros((rows, span - values.shape[1]), f32)
                    low = jnp.concatenate([pad, low], axis=1)
                    high = jnp.concatenate([pad, high], axis=1)
                values = low + pltpu.roll(high, span - rows, 1)
        line_buf[h : h + 1, :] = values
    lines = line_buf[...]
    col = lax.broadcasted_iota(i32, lines.shape, 1)
    buckets = bucket_of(span - QB - EDGE - col)
    far = dfar_ref[...]
    lane = lax.broadcasted_iota(i32, (8, 128), 1)
    left = jnp.sum(jnp.where(lane == 0, far, 0.0), axis=1, keepdims=True)
    right = jnp.sum(jnp.where(lane == 1, far, 0.0), axis=1, keepdims=True)
    grad = jnp.where(lane == 15, left, jnp.where(lane == 31, right, 0.0))
    for bucket in range(32):
        if bucket != 16:
            total = jnp.sum(jnp.where(buckets == bucket, lines, 0.0), axis=1, keepdims=True)
            grad = jnp.where(lane == bucket, grad + total, grad)
    grad_ref[...] = grad


def pack_kernel(qkv_ref, out_ref, tokens_ref, cot_ref, pack_ref, *row_refs):
    packed = jnp.concatenate([qkv_ref[0], qkv_ref[1], qkv_ref[2], out_ref[...].T], axis=1).astype(bf16)
    for slot in range(pack_ref.shape[0]):
        pack_ref[slot] = packed
    rows_kernel(tokens_ref, cot_ref, *row_refs)


def pack_ud_kernel(up_ref, down_ref, pack_ref):
    up, down = up_ref[...].astype(bf16), down_ref[...].astype(bf16)
    for slot in range(pack_ref.shape[0]):
        pack_ref[slot, 0] = up
        pack_ref[slot, 1] = down


def rows_kernel(tokens_ref, cot_ref, keep_tok_ref, send_tok_ref, keep_cot_ref, send_cot_ref):
    side = lax.axis_index("tensor") // 2
    keep_tok_ref[...] = tokens_ref[side]
    send_tok_ref[...] = tokens_ref[1 - side]
    keep_cot_ref[...] = cot_ref[side]
    send_cot_ref[...] = cot_ref[1 - side]


def place_kernel(own_ref, got_ref, mean_ref, out_ref, pooled_ref):
    side = lax.axis_index("tensor") // 2
    length, width = own_ref.shape[0], mean_ref.shape[1]
    out_ref[side] = own_ref[...]
    out_ref[1 - side] = got_ref[0:length, :].astype(f32)
    pooled_ref[side] = mean_ref[...]
    pooled_ref[1 - side] = got_ref[length:, 0:width].astype(f32)


def relay_kernel(*refs):
    for source_ref, out_ref in zip(refs[: len(refs) // 2], refs[len(refs) // 2 :]):
        out_ref[...] = source_ref[...]


def pick_kernel(from_x_ref, from_y_ref, up_ref, down_ref):
    up_ref[...] = from_x_ref[:, 0]
    down_ref[...] = from_y_ref[:, 1]


def total_of(refs):
    total = refs[0][...].astype(f32)
    for ref in refs[1:]:
        total = total + ref[...].astype(f32)
    return total


def add_kernel(*refs):
    *terms, sum_ref, token_ref = refs
    sum_ref[...] = total_of(terms).astype(bf16)
    token_ref[...] = jnp.zeros_like(token_ref)


def send_kernel(*refs):
    *terms, own_ref, sent1_ref, sent2_ref, sent3_ref, token_ref, sum_buf = refs
    sum_buf[...] = total_of(terms)
    place = lax.axis_index("dp") // 2
    own_ref[...] = sum_buf[place]
    for bits, ref in ((1, sent1_ref), (2, sent2_ref), (3, sent3_ref)):
        ref[...] = sum_buf[place ^ bits].astype(bf16)
    token_ref[...] = jnp.zeros_like(token_ref)


def add_pairs_kernel(up_ref, up_got_ref, down_ref, down_got_ref, up_sum_ref, down_sum_ref, token_ref):
    up_sum_ref[...] = total_of((up_ref, up_got_ref)).astype(bf16)
    down_sum_ref[...] = total_of((down_ref, down_got_ref)).astype(bf16)
    token_ref[...] = jnp.zeros_like(token_ref)


def sum_blocks(ref):
    total = ref[0].astype(f32)
    for slot in range(1, ref.shape[0]):
        total = total + ref[slot].astype(f32)
    return total


def finish_kernel(*refs):
    *terms, grad_ref, squares_ref = refs
    total = total_of(terms) if len(terms) > 1 else sum_blocks(terms[0])
    grad_ref[...] = total
    squares_ref[...] = jnp.broadcast_to(jnp.sum(total * total, axis=(0, 1), keepdims=True), (8, 128))


def finish_a_kernel(*refs):
    *terms, up_ref, down_ref, qkv_ref, out_ref, squares_ref = refs
    total = total_of(terms) if len(terms) > 1 else sum_blocks(terms[0])
    width = qkv_ref.shape[2]
    for part in range(3):
        qkv_ref[part] = total[:, part * width : (part + 1) * width]
    out_ref[...] = total[:, 3 * width :].T
    squares_ref[...] = (
        up_ref[...] + down_ref[...] + jnp.sum(total * total, axis=(0, 1), keepdims=True)
    )


def small_kernel(first_ref, second_ref, own_bias_ref, other_bias_ref, squares_ref, out_ref):
    lines = D // 128
    heads = H // 4
    for kind, ref in enumerate((first_ref, second_ref)):
        for line in range(lines):
            out_ref[0, kind * lines + line : kind * lines + line + 1, :] = ref[
                :, line * 128 : (line + 1) * 128
            ]
    terms = [jnp.zeros((1, BUCKETS), f32) for _ in range(H)]
    for shift, ref in ((0, own_bias_ref), (2, other_bias_ref)):
        start = head_of(shift, heads)
        for h in range(heads):
            term = ref[h : h + 1, 0:BUCKETS]
            terms = [jnp.where(start + h == head, term, kept) for head, kept in enumerate(terms)]
    across = 128 // BUCKETS
    for line in range(H // across):
        out_ref[0, 2 * lines + line : 2 * lines + line + 1, :] = jnp.concatenate(
            terms[line * across : (line + 1) * across], axis=1
        )
    lane = lax.broadcasted_iota(i32, (1, 128), 1)
    out_ref[0, SMALL_ROWS - 1 :, :] = jnp.where(lane == 0, squares_ref[0:1, :], 0.0)
    value = out_ref[0]
    for slot in range(1, out_ref.shape[0]):
        out_ref[slot] = value


def adam_kernel(small_ref, *refs):
    sources, refs = refs[:22], refs[23:]
    outs, refs = refs[:15], refs[15:]
    held, kept, (in_sems, out_sems) = refs[:22], refs[22:30], refs[30:]
    copies = [
        pltpu.make_async_copy(source, target, in_sems.at[index])
        for index, (source, target) in enumerate(zip(sources, held))
    ]
    for copy in copies:
        copy.start()
    small = jnp.sum(small_ref[...], axis=0)
    lines = D // 128
    gains_ref, bias_ref, norm_ref = outs[12:]
    for kind in range(2):
        for line in range(lines):
            gains_ref[kind : kind + 1, line * 128 : (line + 1) * 128] = small[
                kind * lines + line : kind * lines + line + 1
            ]
    across = 128 // BUCKETS
    for head in range(H):
        bias_ref[head : head + 1, :] = small[
            2 * lines + head // across : 2 * lines + head // across + 1,
            (head % across) * BUCKETS : (head % across + 1) * BUCKETS,
        ]
    whole = small[: SMALL_ROWS - 1]
    total = small[SMALL_ROWS - 1 :, 0:1]
    norm = jnp.sqrt(total + jnp.sum(whole * whole, axis=(0, 1), keepdims=True))
    norm_ref[0, 0] = jnp.max(norm)
    clip = jnp.minimum(1.0, clip_level / norm)
    rates = learning_rates_plain()
    results = []
    for index in (0, 2, 3, 1):
        param, grad, first, second = held[4 * index : 4 * index + 4]
        for copy in copies[4 * index : 4 * index + 4]:
            copy.wait()
        new, new_second = kept[2 * index : 2 * index + 2]
        if isinstance(rates[index], tuple):
            for part, rate in enumerate(rates[index]):
                value, moment = adam_update(
                    param[part], grad[part], first[part], second[part], rate, clip
                )
                new[part] = value
                new_second[part] = moment
        else:
            value, moment = adam_update(
                param[...], grad[...], first[...], second[...], rates[index], clip
            )
            new[...] = value
            new_second[...] = moment
        for place in (2 * index, 2 * index + 1):
            result = pltpu.make_async_copy(kept[place], outs[place], out_sems.at[place])
            result.start()
            results.append(result)
    for copy in copies[16:]:
        copy.wait()
    for index, (param, grad, first, second) in (
        (4, (held[16], gains_ref, held[17], held[18])),
        (5, (held[19], bias_ref, held[20], held[21])),
    ):
        value, moment = adam_update(
            param[...], grad[...], first[...], second[...], rates[index], clip
        )
        outs[2 * index][...] = value
        outs[2 * index + 1][...] = moment
    for result in results:
        result.wait()


def per_device(
    tokens,
    segment_ids,
    cotangent,
    qkv_master,
    out_master,
    up_master,
    down_master,
    norm_gains,
    position_bias,
    qkv_first,
    qkv_second,
    out_first,
    out_second,
    up_first,
    up_second,
    down_first,
    down_second,
    gain_first,
    gain_second,
    bias_first,
    bias_second,
):
    rank = lax.axis_index("tensor")
    dp_rank = lax.axis_index("dp")
    dp_size = lax.axis_size("dp")
    row_bit = dp_rank % 2
    rows, length = tokens.shape[0], tokens.shape[1]
    seq = segment_ids.shape[1]
    shard_rows, width = qkv_master.shape[1], qkv_master.shape[2]
    units = up_master.shape[1]
    half = (seq // 2, D)
    assert rows == 2 and lax.axis_size("tensor") == 4 and seq == 4 * length
    high = dp_size // 2
    aligned = shard_rows % 16 == 0

    if aligned:
        pack_a, keep_tok, send_tok, keep_cot, send_cot = call(
            pack_kernel,
            "pack_a",
            (),
            (qkv_master, out_master, tokens, cotangent),
            (sds((high, shard_rows, D), bf16),) + (sds((length, D), bf16),) * 4,
            limit=FULL_LIMIT,
        )
        order = lambda pair: pair
        blocks_out = (sds((high, shard_rows, D), bf16),) * 2
    else:
        packed = jnp.concatenate([*qkv_master, out_master.T], axis=1).astype(bf16)
        pack_a = jnp.broadcast_to(packed, (high,) + packed.shape)
        blocks_out = (sds((D, D), bf16),)
        keep_tok, send_tok, keep_cot, send_cot = call(
            rows_kernel, "rows", (), (tokens, cotangent), (sds((length, D), bf16),) * 4
        )

        def order(pair):
            own, other = pair
            first = jnp.where(row_bit == 0, own, other)
            second = jnp.where(row_bit == 0, other, own)
            both = jnp.moveaxis(jnp.stack([first, second], axis=1), (0, 1), (-4, -3))
            both = both.reshape(both.shape[:-4] + (D, both.shape[-1]))
            lower, upper = both[..., : D // 2, :], both[..., D // 2 :, :]
            return (
                jnp.where(row_bit == 0, lower, upper)[None],
                jnp.where(row_bit == 0, upper, lower)[None],
            )

    high_a = over_high(pack_a)
    got_tok = swap_x(send_tok)
    tok_rows = (keep_tok, got_tok, swap_core(keep_tok), swap_core(got_tok))
    got_cot = swap_x(send_cot)
    cot_rows = (keep_cot, got_cot, swap_core(keep_cot), swap_core(got_cot))
    a_y = swap_y(high_a)
    a_x = swap_x(high_a)
    h1, token = call(
        norm_kernel,
        "first_norm",
        (),
        (*tok_rows, norm_gains),
        (sds((seq, D), bf16), sds((8, 128), f32)),
    )
    (pack_ud,) = call(
        pack_ud_kernel,
        "pack_ud",
        (),
        (up_master, down_master.T),
        (sds((high, 2, shard_rows, units), bf16),),
        gates=(token,),
    )
    high_ud = over_high(pack_ud)

    a_other = (a_x, swap_y(a_x))
    wT0, qkvT0, oT0, lse0 = attend(0, segment_ids, position_bias.T, h1, order((high_a, a_y)))
    (relay_ud,) = call(relay_kernel, "relay_ud", (), (high_ud,), (sds(high_ud.shape, bf16),), gates=(lse0, got_cot))
    ud_x = swap_x(relay_ud)
    ud_y = swap_y(relay_ud)
    wT1, qkvT1, oT1, lse1 = attend(2, segment_ids, position_bias.T, h1, order(a_other))

    keep, send = call(
        project_kernel,
        "project",
        (),
        (oT0, oT1, wT0, wT1),
        (sds(half, f32), sds(half, bf16)),
        (pltpu.VMEM((seq, 2 * width), bf16),),
    )
    x2, h2 = call(
        middle_kernel,
        "second_norm",
        (),
        (keep_tok, got_tok, keep, swap_core(send), norm_gains),
        (sds(half, f32), sds(half, bf16)),
    )
    h2_other = swap_core(h2)
    picked_u, picked_d = call(
        pick_kernel,
        "pick_ud",
        (),
        (ud_x, ud_y),
        (sds((high, shard_rows, units), bf16),) * 2,
        gates=(h2,),
    )
    u_xy = swap_y(picked_u)
    d_xy = swap_x(picked_d)

    def of_y(grad, wanted):
        blocks = grad.reshape((high, 2, shard_rows) + grad.shape[1:])
        return lax.dynamic_index_in_dim(blocks, wanted, 1, keepdims=False)

    def by_y(grads):
        if aligned:
            return tuple(grads)
        return tuple(of_y(grad, wanted) for grad in grads for wanted in (row_bit, 1 - row_bit))

    def plus(name, *terms, gates=()):
        outs = (sds(terms[0].shape, bf16), sds((8, 128), f32))
        return call(add_kernel, name, (), terms, outs, gates=gates)

    def over_high_bits(name, *terms, gates=()):
        if high != 4:
            total, token = plus(name, *terms, gates=gates)
            return (over_high(total),), token
        block = terms[0].shape[1:]
        own, *sent, token = call(
            send_kernel,
            name,
            (),
            terms,
            (sds(block, f32),) + (sds(block, bf16),) * 3 + (sds((8, 128), f32),),
            (pltpu.VMEM(terms[0].shape, f32),),
            gates=gates,
        )
        return (own, *(swap_dp(piece, 2 * bits) for bits, piece in enumerate(sent, 1))), token

    feed_scratch = (
        *([pltpu.VMEM((D, units), bf16)] * 2),
        *([pltpu.VMEM((seq, units), bf16)] * 2),
        pltpu.VMEM((2, D, units), bf16),
    )
    dh_part, pool_part, hot, *grads = call(
        feed_own_kernel,
        "feed_own",
        (),
        (h2, h2_other, *cot_rows, *order((relay_ud, ud_y)), segment_ids, x2),
        (sds((seq, D), f32), sds((SEGS, D), f32), sds((SEGS, seq), bf16), *blocks_out, *blocks_out),
        feed_scratch,
        limit=FEED_LIMIT,
    )
    gu0_own, gu0_oth, gd0_own, gd0_oth = by_y(grads)
    if aligned:
        ud_other = (ud_x, u_xy, d_xy)
    else:
        first, second = order((ud_x, jnp.stack([u_xy, d_xy], axis=1)))
        ud_other = (first, second[:, 0], second[:, 1])
    keep, send, pool_part, *grads = call(
        feed_other_kernel,
        "feed_other",
        (),
        (h2, h2_other, *cot_rows, *ud_other, hot, dh_part, pool_part),
        (sds(half, f32), sds(half, bf16), sds((SEGS, D), f32), *blocks_out, *blocks_out),
        feed_scratch,
        limit=FEED_LIMIT,
    )
    got = swap_core(send)
    gu1_own, gu1_oth, gd1_own, gd1_oth = by_y(grads)
    up_y1 = swap_y(gu1_oth)
    down_x1 = swap_x(gd1_oth)
    dx2, da, gain_grad_second = call(
        middle_back_kernel,
        "second_norm_back",
        (),
        (x2, keep, got, keep_cot, got_cot, norm_gains),
        (sds(half, f32), sds(half, bf16), sds((1, D), f32)),
        work=10,
    )
    da_other = swap_core(da)
    doT0, doT1, goT0, goT1 = call(
        branch_back_kernel,
        "branch_back",
        (),
        (da, da_other, wT0, wT1, oT0, oT1),
        (sds((width, seq), bf16),) * 2 + (sds((width, D), bf16),) * 2,
        (pltpu.VMEM((seq, D), bf16),),
        work=10,
    )
    up_late, down_late = call(
        relay_kernel,
        "relay_grads",
        (),
        (gu0_oth, gd1_own),
        (sds(gu0_oth.shape, bf16),) * 2,
        gates=(doT0,),
    )
    up_y0 = swap_y(up_late)
    down_x0 = swap_x(down_late)
    dqkvT1, *ga1, dbias1 = attend_back(
        2, segment_ids, position_bias.T, qkvT1, doT1, lse1, h1, goT1, blocks_out, ()
    )
    up_add, down_add, token = call(
        add_pairs_kernel,
        "add_ud",
        (),
        (gu1_own, up_y1, gd0_oth, down_x1),
        (sds(gu1_own.shape, bf16),) * 2 + (sds((8, 128), f32),),
        gates=(dbias1,),
    )
    up_x = swap_x(up_add)
    down_y = swap_y(down_add)
    ga1_own, ga1_oth = by_y(ga1)
    a_y1 = swap_y(ga1_oth)
    dqkvT0, *ga0, dbias0 = attend_back(
        0, segment_ids, position_bias.T, qkvT0, doT0, lse0, h1, goT0, blocks_out, (token,)
    )
    ga0_own, ga0_oth = by_y(ga0)
    a_y0 = swap_y(ga0_oth)
    token = dbias0
    up_pieces, token = over_high_bits("total_up", gu0_own, up_y0, up_x, gates=(token,))
    down_pieces, token = over_high_bits("total_down", gd0_own, down_x0, down_y, gates=(token,))
    grad_up, up_squares = call(
        finish_kernel,
        "finish_up",
        (),
        up_pieces,
        (sds((shard_rows, units), f32), sds((8, 128), f32)),
        gates=(token,),
    )
    token = up_squares
    a_add, token = plus("add_a", ga1_own, a_y1, gates=(token,))
    a_x1 = swap_x(a_add)
    keep, send, token = call(
        first_back_kernel,
        "first_back",
        (),
        (dqkvT0, dqkvT1, wT0, wT1),
        (sds(half, f32), sds(half, bf16), sds((8, 128), f32)),
        (pltpu.VMEM((seq, 6 * width), bf16),),
        gates=(token,),
    )
    first_got = swap_core(send)
    grad_downT, down_squares = call(
        finish_kernel,
        "finish_down",
        (),
        down_pieces,
        (sds((shard_rows, units), f32), sds((8, 128), f32)),
        gates=(token,),
    )
    token = down_squares
    a_pieces, token = over_high_bits("total_a", ga0_own, a_y0, a_x1, gates=(token,))
    tg_own, tg_away, gain_grad_first, mean_keep = call(
        token_grad_kernel,
        "first_norm_back",
        (),
        (keep_tok, got_tok, keep, first_got, dx2, norm_gains, pool_part, swap_core(pool_part), hot),
        (
            sds((length, D), f32),
            sds((length + SEGS, D), bf16),
            sds((1, D), f32),
            sds((SEGS, width), f32),
        ),
        gates=(token,),
    )
    tg_got = swap_x(tg_away)
    devices = dp_size * lax.axis_size("tensor")
    def from_all(value):
        return lax.all_to_all(value, ("dp", "tensor"), 0, 0, tiled=True)

    if aligned:
        grad_qkv, grad_out, squares = call(
            finish_a_kernel,
            "finish_a",
            (),
            (*a_pieces, up_squares, down_squares),
            (sds(qkv_master.shape, f32), sds(out_master.shape, f32), sds((8, 128), f32)),
            gates=(gain_grad_first,),
        )
    else:
        grad_a = jnp.sum(a_pieces[0].astype(f32), axis=0)
        grad_qkv = jnp.stack([grad_a[:, i * width : (i + 1) * width] for i in range(3)])
        grad_out = grad_a[:, 3 * width :].T
        squares = jnp.broadcast_to(
            up_squares + down_squares + jnp.sum(grad_a * grad_a), (8, 128)
        )

    (small,) = call(
        small_kernel,
        "small",
        (),
        (gain_grad_first, gain_grad_second, dbias0, dbias1, squares),
        (sds((devices, SMALL_ROWS, 128), f32),),
    )
    small_all = from_all(small)
    tokens_grad, pooled = call(
        place_kernel,
        "tokens_grad",
        (),
        (tg_own, tg_got, mean_keep),
        (sds(tokens.shape, f32), sds((rows, SEGS, width), f32)),
        gates=(small,),
    )
    groups = (
        (qkv_master, grad_qkv, qkv_first, qkv_second),
        (out_master, grad_out, out_first, out_second),
        (up_master, grad_up, up_first, up_second),
        (down_master.T, grad_downT, down_first.T, down_second.T),
        (norm_gains, None, gain_first, gain_second),
        (position_bias.T, None, bias_first.T, bias_second.T),
    )
    operands = [array for group in groups for array in group if array is not None]
    updates = pl.pallas_call(
        adam_kernel,
        out_shape=[sds(group[0].shape, f32) for group in groups for _ in range(2)]
        + [sds(norm_gains.shape, f32), sds(position_bias.shape[::-1], f32), sds((1, 1), f32)],
        in_specs=[VMEM_SPEC] + [pl.BlockSpec(memory_space=pltpu.HBM)] * (len(operands) + 1),
        out_specs=[pl.BlockSpec(memory_space=pltpu.HBM)] * 8 + [VMEM_SPEC] * 6 + [SMEM_SPEC],
        scratch_shapes=[pltpu.VMEM(array.shape, f32) for array in operands]
        + [pltpu.VMEM(group[0].shape, f32) for group in groups[:4] for _ in range(2)]
        + [pltpu.SemaphoreType.DMA((len(operands),)), pltpu.SemaphoreType.DMA((8,))],
        compiler_params=pltpu.CompilerParams(vmem_limit_bytes=60 << 20),
        name="adam",
    )(small_all, *operands, pooled)
    new_qkv, second_qkv, new_out, second_out, new_up, second_up = updates[0:6]
    new_gains, second_gains = updates[8:10]
    new_down, second_down, new_bias, second_bias = (updates[i].T for i in (6, 7, 10, 11))
    grad_gains, grad_biasT = updates[12:14]
    grad_down, grad_bias = grad_downT.T, grad_biasT.T
    gradient_norm = updates[14].reshape(())
    return (
        pooled,
        tokens_grad,
        grad_qkv,
        grad_out,
        grad_up,
        grad_down,
        grad_gains,
        grad_bias,
        gradient_norm,
        new_qkv,
        new_out,
        new_up,
        new_down,
        new_gains,
        new_bias,
        second_qkv,
        second_out,
        second_up,
        second_down,
        second_gains,
        second_bias,
    )


def solution(mesh):
    in_specs = (
        P("dp", "tensor", None),
        P("dp", None),
        P("dp", "tensor", None),
        P(None, "dp", "tensor"),
        P("tensor", "dp"),
        P("dp", "tensor"),
        P("tensor", "dp"),
        P(),
        P(),
        P(None, "dp", "tensor"),
        P(None, "dp", "tensor"),
        P("tensor", "dp"),
        P("tensor", "dp"),
        P("dp", "tensor"),
        P("dp", "tensor"),
        P("tensor", "dp"),
        P("tensor", "dp"),
        P(),
        P(),
        P(),
        P(),
    )
    out_specs = (
        P("dp", None, "tensor"),
        P("dp", "tensor", None),
        P(None, "dp", "tensor"),
        P("tensor", "dp"),
        P("dp", "tensor"),
        P("tensor", "dp"),
        P(),
        P(),
        P(),
        P(None, "dp", "tensor"),
        P("tensor", "dp"),
        P("dp", "tensor"),
        P("tensor", "dp"),
        P(),
        P(),
        P(None, "dp", "tensor"),
        P("tensor", "dp"),
        P("dp", "tensor"),
        P("tensor", "dp"),
        P(),
        P(),
    )
    return jax.shard_map(
        per_device, mesh=mesh, in_specs=in_specs, out_specs=out_specs, check_vma=False
    )
```
